32 devices in a mesh: tm: 8 (over z, y), site: 4 (over x, core).
Axes of the slice: x: 2, y: 2, z: 4, core: 2. Of those that a mesh axis runs over, the one named last changes fastest.
Arguments:
- obs_rows: bfloat16 [16384, 256], P(('tm', 'site')), may hold values from -2 to 2
- obs_values: bfloat16 [16384], P(('tm', 'site')), may hold values from -6 to 6
- obs_hours: int32 [16384], P(('tm', 'site')), may hold values from 0 to 3
- prior_precision: float32 [256, 256], replicated, may hold values from -1 to 3, as said below
- transition: float32 [256, 256], replicated, may hold values from -1 to 1
- site_basis: bfloat16 [131072, 256], P(('tm', 'site')), may hold values from -0.375 to 0.375
Outputs:
- prediction: bfloat16 [32, 131072], P(None, ('tm', 'site'))
The draws below stay inside these ranges and needn't reach their ends.
Inputs may be any that keep to these rules, and one draw needn't show every extreme that they name: `prior_precision`: symmetric and positive definite.
All inputs are finite; a program needn't handle non-finite values. Where the reference program divides by a largest or mean magnitude, that divisor is 1e-20 or more.
Results may differ from the reference program's by a relative error of at most 0.0049.
Values may be sent and summed in bfloat16 or wider, within the bound.
No kernel may reach another device: no remote copies, remote signals or barrier semaphores. Data moves between devices by JAX's collectives and lax.ppermute only.
A program may use at most 64 MiB of HBM per device.

```python
import jax
import jax.numpy as jnp
from jax import lax

S = 256
NS_ITERS = 8
OBS_DEV = 512
HR = 4
HOURS = 32
OBS = 16384
SITES = 131072
N_TM = 8
N_SITE = 4


def draw_obs_rows(key, part):
    scale_key, block_key, entry_key = jax.random.split(jax.random.fold_in(key, 31), 3)
    lowest, highest = (0.03, 0.6)
    column_scale = jnp.exp(jax.random.uniform(scale_key, (S,), jnp.float32, jnp.log(lowest), jnp.log(highest)))
    blocks = HOURS // HR
    block_scale = jnp.exp(jax.random.uniform(block_key, (blocks, 1, S), jnp.float32, jnp.log(0.5), jnp.log(2.0)))
    entries = jnp.clip(jax.random.normal(entry_key, (blocks, OBS // blocks, S), jnp.float32), -4.0, 4.0)
    scaled = entries * (column_scale * OBS_DEV ** (-0.5))[None, None, :] * block_scale
    return scaled.reshape(OBS, S).astype(jnp.bfloat16)


def draw_prior_precision(key, part):
    first_key, second_key = jax.random.split(jax.random.fold_in(key, 11))
    lowest, highest = (0.25, 1.5)
    diagonal = jnp.exp(jax.random.uniform(first_key, (S,), jnp.float32, jnp.log(lowest), jnp.log(highest)))
    factor = jax.random.normal(second_key, (S, S), jnp.float32)
    return jnp.diag(diagonal) + 0.5 * jnp.dot(factor, factor.T, precision=lax.Precision.HIGHEST) / S


def draw_transition(key, part):
    first_key, second_key = jax.random.split(jax.random.fold_in(key, 23))
    slowest, fastest = (0.25 / HOURS, 0.1)
    rates = jnp.exp(jax.random.uniform(first_key, (S,), jnp.float32, jnp.log(slowest), jnp.log(fastest)))
    mixing = jnp.eye(S, dtype=jnp.float32) + jax.random.normal(second_key, (S, S), jnp.float32) * (0.05 * S ** (-0.5))
    for sweep in range(12):
        square = jnp.dot(mixing, mixing.T, precision=lax.Precision.HIGHEST)
        mixing = 1.5 * mixing - 0.5 * jnp.dot(square, mixing, precision=lax.Precision.HIGHEST)
    return jnp.exp(-rates)[:, None] * mixing


def place_ends(drawn, own_key, least, top_value):
    shape = drawn.shape
    spot = [jax.random.randint(jax.random.fold_in(own_key, axis), (), 0, shape[axis]) for axis in range(len(shape))]
    drawn = drawn.at[tuple(spot)].set(least)
    longest = shape.index(max(shape))
    spot[longest] = (spot[longest] + 1) % shape[longest]
    return drawn.at[tuple(spot)].set(top_value)


def level_of(own_key, extent, cuts, low, high):
    def one(dim, shards_of):
        draws = jax.random.uniform(jax.random.fold_in(jax.random.fold_in(own_key, 6), dim), (shards_of,), jnp.float32, low / len(cuts), high / len(cuts))
        return jnp.repeat(jnp.exp(draws), extent[dim] // shards_of).reshape((-1,) + (1,) * (len(extent) - dim - 1))

    factor_of = one(*cuts[0])
    for cut in cuts[1:]:
        factor_of = factor_of * one(*cut)
    return factor_of


def scatter_about(own_key, extent, width, most, shards=(), held_as=jnp.bfloat16):
    values = jax.random.normal(own_key, extent, jnp.float32) * width
    if len(shards) > 0:
        values = level_of(own_key, extent, shards, -0.22, 0.18) * values
    return jnp.clip(values, min=-most, max=most).astype(held_as)


def setup_inputs(seed: int = 0) -> dict:
    key_of = jax.random.split(jax.random.key(seed), 7)
    return {
        "obs_rows": draw_obs_rows(jax.random.fold_in(key_of[6], 71), 0),
        "obs_values": scatter_about(key_of[1], (OBS,), 1.0, 6.0, ((0, 32),)),
        "obs_hours": place_ends(jax.random.randint(key_of[2], (OBS,), 0, HR), jax.random.fold_in(key_of[2], 1), 0, HR - 1).astype(jnp.int32),
        "prior_precision": draw_prior_precision(jax.random.fold_in(key_of[6], 71), 0),
        "transition": draw_transition(jax.random.fold_in(key_of[6], 71), 0),
        "site_basis": scatter_about(key_of[5], (SITES, S), S ** -0.5, 0.375, ((0, 32),)),
    }


def reference(obs_rows, obs_values, obs_hours, prior_precision, transition, site_basis):
    block_rows = N_SITE * OBS_DEV
    features = obs_rows.reshape(N_TM, block_rows, S)
    values = obs_values.reshape(N_TM, block_rows)
    labels = obs_hours.reshape(N_TM, block_rows)
    coupled = jnp.dot(prior_precision, transition, precision=lax.Precision.HIGHEST)

    def block_step(running, inputs):
        feature_block, value_block, label_block = inputs
        hour_slot = lax.broadcasted_iota(jnp.int32, (N_SITE, block_rows), 0)
        member = label_block[None, :] == hour_slot
        wide_rows = feature_block.astype(jnp.float32)
        masked = jnp.where(member[:, :, None], wide_rows[None], jnp.float32(0.0))
        grams = jnp.einsum("hrs,rt->hst", masked, wide_rows, precision=lax.Precision.HIGHEST)
        weighted = jnp.where(member, value_block.astype(jnp.float32)[None], jnp.float32(0.0))
        drives = jnp.einsum("hr,rs->hs", weighted, wide_rows, precision=lax.Precision.HIGHEST)
        state_mean = running
        results = []
        for position in range(N_SITE):
            precision_mat = prior_precision + grams[position]
            bound = jnp.max(jnp.sum(jnp.abs(precision_mat), axis=1))
            source = jnp.dot(coupled, state_mean, precision=lax.Precision.HIGHEST) + drives[position]

            def series_step(counter, state):
                current, summed = state
                summed = summed + current
                current = current - jnp.dot(precision_mat, current, precision=lax.Precision.HIGHEST) / bound
                return current, summed

            finished = lax.fori_loop(0, 2 ** NS_ITERS, series_step, (source, jnp.zeros_like(source)))
            state_mean = finished[1] / bound
            results.append(state_mean)
        return state_mean, jnp.stack(results)

    final_mean, means = lax.scan(block_step, jnp.zeros((S,), jnp.float32), (features, values, labels))
    rounded = means.reshape(HOURS, S).astype(jnp.bfloat16)
    return jnp.dot(rounded, site_basis.T, preferred_element_type=jnp.float32).astype(jnp.bfloat16)
```

```python
import functools

import jax
import jax.numpy as jnp
from jax import lax
from jax.experimental import pallas as pl
from jax.experimental.pallas import tpu as pltpu
from jax.sharding import PartitionSpec as P

NS_ITERS = 8
TAIL = 8
BF16 = jnp.bfloat16
F32 = jnp.float32
VMEM_LIMIT = 40 * 2**20


def whole():
    return pl.BlockSpec(memory_space=pltpu.VMEM)


def call(kernel, outs, args, name, scratch=()):
    return pl.pallas_call(
        kernel,
        out_shape=outs,
        in_specs=[whole()] * len(args),
        out_specs=jax.tree.map(lambda _: whole(), outs),
        scratch_shapes=scratch,
        compiler_params=pltpu.CompilerParams(vmem_limit_bytes=VMEM_LIMIT),
        name=name,
    )(*args)


def dot(a, b):
    return jnp.dot(a, b, preferred_element_type=F32)


def split(x):
    high = x.astype(BF16)
    return high, (x - high.astype(F32)).astype(BF16)


def dot_wide(a, b):
    a_high, a_low = split(a)
    b_high, b_low = split(b)
    return dot(
        jnp.concatenate([a_high, a_low, a_high], axis=1),
        jnp.concatenate([b_high, b_high, b_low], axis=0),
    )


def thirds(row):
    first = row.astype(BF16).astype(F32)
    second = (row - first).astype(BF16).astype(F32)
    third = row - first - second
    zeros = jnp.zeros((13, row.shape[1]), F32)
    return jnp.concatenate([first, second, third, zeros], axis=0).astype(BF16)


def row_times(row, *weights):
    rows = thirds(row)
    total = dot(rows, weights[0])
    for w in weights[1:]:
        total += dot(rows, w)
    return jnp.sum(total, axis=0, keepdims=True)


def own_half(hours):
    return lax.rem(lax.axis_index("site"), 2) * (hours // 2)


def local_grams(hours, rows_ref, values_ref, codes_ref, keep_ref, send_ref):
    half = hours // 2
    states = rows_ref.shape[1]
    start = own_half(hours)
    rows = rows_ref[...]
    turned = rows.T
    codes = codes_ref[...]
    values = values_ref[...].astype(F32)
    slots = []
    for slot in range(hours):
        hour = lax.rem(start + slot, hours)
        slots.append((codes == hour).astype(F32))
    masked = jnp.concatenate([turned * s.astype(BF16) for s in slots], axis=0)
    grams = dot(masked, rows)
    weighted = jnp.concatenate([s * values for s in slots], axis=0)
    pad = jnp.zeros((16 - hours, weighted.shape[1]), F32)
    drives = dot(jnp.concatenate([weighted, pad], axis=0).astype(BF16), rows)
    row_id = lax.broadcasted_iota(jnp.int32, (states, states), 0)
    column_id = lax.broadcasted_iota(jnp.int32, (states, states), 1)
    for out_ref, base in ((keep_ref, 0), (send_ref, half)):
        for pair in range(half // 2):
            first = base + 2 * pair
            a = grams[first * states : (first + 1) * states]
            b = grams[(first + 1) * states : (first + 2) * states]
            diagonal = jnp.sum(jnp.where(row_id == column_id, b, 0.0), axis=0, keepdims=True)
            out_ref[pair, :states, :] = jnp.where(row_id <= column_id, a, b)
            out_ref[pair, states:, :] = jnp.concatenate(
                [diagonal, drives[first : first + 2], jnp.zeros((TAIL - 3, states), F32)], axis=0
            )


def add_and_round(keep_ref, received_ref, sum_ref, send_ref):
    states = keep_ref.shape[2]
    for pair in range(keep_ref.shape[0]):
        total = keep_ref[pair] + received_ref[pair]
        sum_ref[pair] = total
        send_ref[pair, :states, :] = total[:states].astype(BF16)
        tail = total[states:]
        high = tail.astype(BF16).astype(F32)
        send_ref[pair, states:, :] = jnp.concatenate([high, tail - high], axis=0).astype(BF16)


def add_received(sum_ref, received_ref, out_ref):
    states = sum_ref.shape[2]
    for pair in range(sum_ref.shape[0]):
        out_ref[pair] = sum_of(sum_ref, received_ref, pair, states)


def sum_of(sum_ref, received_ref, pair, states):
    received = received_ref[pair].astype(F32)
    tail = received[states : states + TAIL] + received[states + TAIL :]
    return sum_ref[pair] + jnp.concatenate([received[:states], tail], axis=0)


def hour_maps(sum_ref, received_ref, prior_ref, turned_ref, out_ref):
    states = prior_ref.shape[0]
    prior = prior_ref[...]
    turned = turned_ref[...]
    row_id = lax.broadcasted_iota(jnp.int32, (states, states), 0)
    column_id = lax.broadcasted_iota(jnp.int32, (states, states), 1)
    running = []
    for pair in range(sum_ref.shape[0]):
        total = sum_of(sum_ref, received_ref, pair, states)
        square = total[:states]
        flipped = square.T
        upper, lower = row_id <= column_id, row_id > column_id
        gram_a = jnp.where(upper, square, flipped)
        gram_b = jnp.where(lower, square, flipped)
        gram_b = jnp.where(row_id == column_id, total[states : states + 1], gram_b)
        for gram, place in ((gram_a, states + 1), (gram_b, states + 2)):
            precision = prior + gram
            bound = jnp.max(jnp.sum(jnp.abs(precision), axis=0, keepdims=True), axis=1, keepdims=True)
            scale = 1.0 / bound
            offset = jnp.concatenate(
                [total[place : place + 1], jnp.zeros((15, states), F32)], axis=0
            )
            running.append((precision * scale, turned * scale, offset * scale))
    stacked = tuple(jnp.concatenate(parts, axis=0) for parts in running)

    def step(_, state):
        return tuple(2.0 * z - dot_wide(z, z[:states]) for z in state)

    stacked = lax.fori_loop(0, NS_ITERS - 1, step, stacked)
    maps = []
    for z in stacked:
        v = z[states:]
        maps.append(2.0 * v - dot_wide(v, z[:states]))
    joined = maps[0]
    out_ref[0] = joined
    for position in range(1, len(maps)):
        joined = append(joined, maps[position])
        out_ref[position] = joined


def append(earlier, latter):
    states = latter.shape[1]
    product = dot_wide(earlier, latter[:states])
    return jnp.concatenate([product[:states], product[states:] + latter[states:]], axis=0)


def in_order(half, own_ref, received_ref):
    first = own_half(2 * half) == 0
    early = [jnp.where(first, own_ref[i], received_ref[i]) for i in range(half)]
    late = [jnp.where(first, received_ref[i], own_ref[i]) for i in range(half)]
    return early, late


def block_map(own_ref, received_ref, out_ref):
    half, rows, states = own_ref.shape
    early, late = in_order(half, own_ref, received_ref)
    joined = append(early[-1], late[-1])
    out_ref[:states, :] = joined[:states].astype(BF16)
    out_ref[states:, :] = thirds(joined[states : states + 1])


def shift_of(block):
    states = block.shape[1]
    return jnp.sum(block[states:].astype(F32), axis=0, keepdims=True)


def pick(refs, slot):
    value = refs[0][...]
    for i in range(1, len(refs)):
        value = jnp.where(slot == i, refs[i][...], value)
    return value


def apply(block, mean):
    return row_times(mean, block[: block.shape[1]]) + shift_of(block)


def follow(earlier, latter):
    states = latter.shape[1]
    product = dot(earlier[:states], latter[:states]).astype(BF16)
    return jnp.concatenate([product, thirds(apply(latter, shift_of(earlier)))], axis=0)


def group_shift(*refs):
    gathered, out_ref = refs[:-1], refs[-1]
    place = lax.rem(lax.axis_index("tm"), len(gathered))
    mean = shift_of(pick(gathered, place))
    for i in range(1, len(gathered)):
        mean = apply(pick(gathered, place ^ i), mean)
    out_ref[...] = jnp.broadcast_to(mean, out_ref.shape)


def group_map(*refs):
    gathered, out_ref = refs[:-1], refs[-1]
    place = lax.rem(lax.axis_index("tm"), len(gathered))
    joined = pick(gathered, place)
    for i in range(1, len(gathered)):
        joined = follow(joined, pick(gathered, place ^ i))
    out_ref[...] = joined


def pair_map(distance, own_ref, received_ref, out_ref):
    upper = is_upper(distance)
    first = jnp.where(upper, received_ref[...], own_ref[...])
    second = jnp.where(upper, own_ref[...], received_ref[...])
    out_ref[...] = follow(first, second)


def is_upper(distance):
    return lax.rem(lax.axis_index("tm") // distance, 2) == 1


def block_means(distances, *refs):
    out_ref, own_ref, other_ref = refs[-1], refs[0], refs[1]
    levels, gathered = refs[2 : 2 + len(distances)], refs[2 + len(distances) : -1]
    half, rows, states = own_ref.shape
    mean = jnp.zeros((1, states), F32)
    for level in reversed(range(len(distances))):
        if level == len(distances) - 1:
            entered = levels[level][0:1, :]
        else:
            entered = apply(levels[level][...], mean)
        mean = jnp.where(is_upper(distances[level]), entered, mean)
    place = lax.rem(lax.axis_index("tm"), len(gathered))
    for i in range(len(gathered) - 1):
        mean = jnp.where(i < place, apply(pick(gathered, place ^ i), mean), mean)
    early, late = in_order(half, own_ref, other_ref)
    results = []
    for maps in (early, late):
        start = mean
        for each in maps:
            mean = row_times(start, *split(each[:states])) + each[states : states + 1]
            results.append(mean)
    results = jnp.concatenate(results, axis=0).astype(BF16)
    for copy in range(out_ref.shape[0]):
        out_ref[copy] = results


def swaps(size, distance):
    return [(i, i ^ distance) for i in range(size)]


def body(obs_rows, obs_values, obs_hours, prior_precision, transition, site_basis):
    hours = lax.axis_size("site")
    blocks = lax.axis_size("tm")
    count, states = obs_rows.shape
    half = hours // 2
    pairs = half // 2
    sds = jax.ShapeDtypeStruct
    turned = jnp.dot(transition.T, prior_precision.T, precision=lax.Precision.HIGHEST)
    packed = sds((pairs, states + TAIL, states), F32)
    keep, send = call(
        functools.partial(local_grams, hours),
        (packed, packed),
        (obs_rows, obs_values.reshape(1, count), obs_hours.reshape(1, count)),
        "local_grams",
    )
    received = lax.ppermute(send, "site", swaps(hours, 1))
    rounded = sds((pairs, states + 2 * TAIL, states), BF16)
    distance = 2
    while distance < hours:
        total, send = call(add_and_round, (packed, rounded), (keep, received), "add_and_round")
        received = lax.ppermute(send, "site", swaps(hours, distance))
        distance *= 2
        if distance < hours:
            keep = call(add_received, packed, (total, received), "add_received")
            received = jnp.zeros_like(keep)
    maps = call(
        hour_maps,
        sds((half, states + 16, states), F32),
        (total, received, prior_precision, turned),
        "hour_maps",
    )
    other = lax.ppermute(maps, "site", swaps(hours, 1))
    own = call(block_map, sds((states + 16, states), BF16), (maps, other), "block_map")
    radix = min(4, blocks)
    gathered = [own] + [lax.ppermute(own, "tm", swaps(blocks, d)) for d in range(1, radix)]
    distances, levels = [], []
    distance = radix
    if 2 * distance < blocks:
        joined = call(group_map, sds(own.shape, BF16), gathered, "group_map")
    while distance < blocks:
        if 2 * distance == blocks:
            if levels:
                shift = joined[states:].astype(F32).sum(axis=0, keepdims=True)
                shift = jnp.broadcast_to(shift, (8, states))
            else:
                shift = call(group_shift, sds((8, states), F32), gathered, "group_shift")
            received = lax.ppermute(shift, "tm", swaps(blocks, distance))
        else:
            received = lax.ppermute(joined, "tm", swaps(blocks, distance))
            joined = call(
                functools.partial(pair_map, distance),
                sds(own.shape, BF16),
                (joined, received),
                "pair_map",
            )
        distances.append(distance)
        levels.append(received)
        distance *= 2
    means = call(
        functools.partial(block_means, tuple(distances)),
        sds((blocks, hours, states), BF16),
        [maps, other] + levels + gathered,
        "block_means",
    )
    means = lax.all_to_all(means, "tm", 0, 0, tiled=True).reshape(blocks * hours, states)
    return jnp.einsum("hs,ns->hn", means, site_basis, preferred_element_type=F32).astype(BF16)


def solution(mesh):
    in_specs = (
        P(("tm", "site"), None),
        P(("tm", "site")),
        P(("tm", "site")),
        P(),
        P(),
        P(("tm", "site"), None),
    )
    out_specs = P(None, ("tm", "site"))
    return jax.shard_map(body, mesh=mesh, in_specs=in_specs, out_specs=out_specs, check_vma=False)
```

```python
import functools

import jax
import jax.numpy as jnp
from jax import lax
from jax.experimental import pallas as pl
from jax.experimental.pallas import tpu as pltpu
from jax.sharding import PartitionSpec as P

NS_ITERS = 8
TAIL = 8
BF16 = jnp.bfloat16
F32 = jnp.float32
VMEM_LIMIT = 40 * 2**20


def whole():
    return pl.BlockSpec(memory_space=pltpu.VMEM)


def call(kernel, outs, args, name, scratch=(), in_hbm=False):
    if in_hbm:
        args = [pltpu.with_memory_space_constraint(arg, pltpu.HBM) for arg in args]
    return pl.pallas_call(
        kernel,
        out_shape=outs,
        in_specs=[pl.BlockSpec(memory_space=pltpu.HBM) if in_hbm else whole()] * len(args),
        out_specs=jax.tree.map(lambda _: whole(), outs),
        scratch_shapes=scratch,
        compiler_params=pltpu.CompilerParams(vmem_limit_bytes=VMEM_LIMIT),
        name=name,
    )(*args)


def dot(a, b):
    return jnp.dot(a, b, preferred_element_type=F32)


def split(x):
    high = x.astype(BF16)
    return high, (x - high.astype(F32)).astype(BF16)


def dot_wide(a, b):
    a_high, a_low = split(a)
    b_high, b_low = split(b)
    return dot(
        jnp.concatenate([a_high, a_low, a_high], axis=1),
        jnp.concatenate([b_high, b_high, b_low], axis=0),
    )


def thirds(row):
    first = row.astype(BF16).astype(F32)
    second = (row - first).astype(BF16).astype(F32)
    third = row - first - second
    zeros = jnp.zeros((13, row.shape[1]), F32)
    return jnp.concatenate([first, second, third, zeros], axis=0).astype(BF16)


def row_times(row, *weights):
    rows = thirds(row)
    total = dot(rows, weights[0])
    for w in weights[1:]:
        total += dot(rows, w)
    return jnp.sum(total, axis=0, keepdims=True)


def own_half(hours):
    return lax.rem(lax.axis_index("site"), 2) * (hours // 2)


def local_grams(
    hours,
    rows_hbm,
    values_hbm,
    codes_hbm,
    keep_ref,
    send_ref,
    rows_ref,
    values_ref,
    codes_ref,
    sems,
):
    half = hours // 2
    states = rows_hbm.shape[1]
    start = own_half(hours)
    copies = [
        pltpu.make_async_copy(rows_hbm, rows_ref, sems.at[0]),
        pltpu.make_async_copy(values_hbm, values_ref, sems.at[1]),
        pltpu.make_async_copy(codes_hbm, codes_ref, sems.at[2]),
    ]
    for copy in copies:
        copy.start()
    for copy in copies:
        copy.wait()
    rows = rows_ref[...]
    turned = rows.T
    codes = codes_ref[...].reshape(1, rows.shape[0])
    values = values_ref[...].astype(F32).reshape(1, rows.shape[0])
    slots = []
    for slot in range(hours):
        hour = lax.rem(start + slot, hours)
        slots.append((codes == hour).astype(F32))
    masked = jnp.concatenate([turned * s.astype(BF16) for s in slots], axis=0)
    grams = dot(masked, rows)
    weighted = jnp.concatenate([s * values for s in slots], axis=0)
    pad = jnp.zeros((16 - hours, weighted.shape[1]), F32)
    drives = dot(jnp.concatenate([weighted, pad], axis=0).astype(BF16), rows)
    row_id = lax.broadcasted_iota(jnp.int32, (states, states), 0)
    column_id = lax.broadcasted_iota(jnp.int32, (states, states), 1)
    for out_ref, base in ((keep_ref, 0), (send_ref, half)):
        for pair in range(half // 2):
            first = base + 2 * pair
            a = grams[first * states : (first + 1) * states]
            b = grams[(first + 1) * states : (first + 2) * states]
            diagonal = jnp.sum(jnp.where(row_id == column_id, b, 0.0), axis=0, keepdims=True)
            out_ref[pair, :states, :] = jnp.where(row_id <= column_id, a, b)
            out_ref[pair, states:, :] = jnp.concatenate(
                [diagonal, drives[first : first + 2], jnp.zeros((TAIL - 3, states), F32)], axis=0
            )


def coupled_turned(prior_ref, transition_ref, prior_out_ref, turned_ref):
    prior = prior_ref[...]
    prior_out_ref[...] = prior
    turned_ref[...] = dot_wide(transition_ref[...].T, prior)


def add_and_round(keep_ref, received_ref, sum_ref, send_ref):
    states = keep_ref.shape[2]
    for pair in range(keep_ref.shape[0]):
        total = keep_ref[pair] + received_ref[pair]
        sum_ref[pair] = total
        send_ref[pair, :states, :] = total[:states].astype(BF16)
        tail = total[states:]
        high = tail.astype(BF16).astype(F32)
        send_ref[pair, states:, :] = jnp.concatenate([high, tail - high], axis=0).astype(BF16)


def add_received(sum_ref, received_ref, out_ref):
    states = sum_ref.shape[2]
    for pair in range(sum_ref.shape[0]):
        out_ref[pair] = sum_of(sum_ref, received_ref, pair, states)


def sum_of(sum_ref, received_ref, pair, states):
    received = received_ref[pair].astype(F32)
    tail = received[states : states + TAIL] + received[states + TAIL :]
    return sum_ref[pair] + jnp.concatenate([received[:states], tail], axis=0)


def hour_maps(sum_ref, received_ref, prior_ref, turned_ref, out_ref):
    states = prior_ref.shape[0]
    prior = prior_ref[...]
    turned = turned_ref[...]
    row_id = lax.broadcasted_iota(jnp.int32, (states, states), 0)
    column_id = lax.broadcasted_iota(jnp.int32, (states, states), 1)
    running = []
    for pair in range(sum_ref.shape[0]):
        total = sum_of(sum_ref, received_ref, pair, states)
        square = total[:states]
        flipped = square.T
        upper, lower = row_id <= column_id, row_id > column_id
        gram_a = jnp.where(upper, square, flipped)
        gram_b = jnp.where(lower, square, flipped)
        gram_b = jnp.where(row_id == column_id, total[states : states + 1], gram_b)
        for gram, place in ((gram_a, states + 1), (gram_b, states + 2)):
            precision = prior + gram
            bound = jnp.max(jnp.sum(jnp.abs(precision), axis=0, keepdims=True), axis=1, keepdims=True)
            scale = 1.0 / bound
            offset = jnp.concatenate(
                [total[place : place + 1], jnp.zeros((15, states), F32)], axis=0
            )
            running.append((precision * scale, turned * scale, offset * scale))
    stacked = [jnp.concatenate(parts, axis=0) for parts in running]

    for _ in range(NS_ITERS - 2):
        stacked = [2.0 * z - dot_wide(z, z[:states]) for z in stacked]
    maps = []
    for z in stacked:
        power = (jnp.where(row_id == column_id, 1.0, 0.0) - z[:states]).astype(BF16)
        v = z[states:]
        product = dot(jnp.concatenate([power, v.astype(BF16)], axis=0), power)
        v = v + product[states:]
        maps.append(v + dot(v.astype(BF16), product[:states].astype(BF16)))
    joined = maps[0]
    out_ref[0] = joined
    for position in range(1, len(maps)):
        joined = append(joined, maps[position])
        out_ref[position] = joined


def append(earlier, latter):
    states = latter.shape[1]
    product = dot_wide(earlier, latter[:states])
    return jnp.concatenate([product[:states], product[states:] + latter[states:]], axis=0)


def in_order(half, own_ref, received_ref):
    first = own_half(2 * half) == 0
    early = [jnp.where(first, own_ref[i], received_ref[i]) for i in range(half)]
    late = [jnp.where(first, received_ref[i], own_ref[i]) for i in range(half)]
    return early, late


def block_map(own_ref, received_ref, out_ref, part_ref):
    half, rows, states = own_ref.shape
    early, late = in_order(half, own_ref, received_ref)
    joined = append(early[-1], late[-1])
    out_ref[:states, :] = joined[:states].astype(BF16)
    out_ref[states:, :] = thirds(joined[states : states + 1])
    height = part_ref.shape[0]
    first = own_half(2 * half) == 0
    part_ref[...] = jnp.where(first, out_ref[:height, :], out_ref[rows - height :, :])


def group_blocks(own_ref, near_ref, part_ref, other_near_ref, other_part_ref, *out_refs):
    first = lax.rem(lax.axis_index("site"), 2) == 0
    rows, height = own_ref.shape[0], part_ref.shape[0]
    out_refs[0][...] = jnp.where(first, near_ref[...], other_near_ref[...])
    out_refs[1][...] = jnp.where(first, other_near_ref[...], near_ref[...])
    out_refs[2][:height, :] = jnp.where(first, part_ref[...], other_part_ref[...])
    low = jnp.where(first, other_part_ref[...], part_ref[...])
    out_refs[2][height:, :] = low[2 * height - rows :]


def shift_of(block):
    states = block.shape[1]
    return jnp.sum(block[states:].astype(F32), axis=0, keepdims=True)


def pick(refs, slot):
    value = refs[0][...]
    for i in range(1, len(refs)):
        value = jnp.where(slot == i, refs[i][...], value)
    return value


def apply(block, mean):
    return row_times(mean, block[: block.shape[1]]) + shift_of(block)


def follow(earlier, latter):
    states = latter.shape[1]
    product = dot(earlier[:states], latter[:states]).astype(BF16)
    return jnp.concatenate([product, thirds(apply(latter, shift_of(earlier)))], axis=0)


def group_shift(*refs):
    gathered, out_ref = refs[:-1], refs[-1]
    place = lax.rem(lax.axis_index("tm"), len(gathered))
    mean = shift_of(pick(gathered, place))
    for i in range(1, len(gathered)):
        mean = apply(pick(gathered, place ^ i), mean)
    out_ref[...] = jnp.broadcast_to(mean, out_ref.shape)


def group_map(*refs):
    gathered, out_ref = refs[:-1], refs[-1]
    place = lax.rem(lax.axis_index("tm"), len(gathered))
    joined = pick(gathered, place)
    for i in range(1, len(gathered)):
        joined = follow(joined, pick(gathered, place ^ i))
    out_ref[...] = joined


def pair_map(distance, own_ref, received_ref, out_ref):
    upper = is_upper(distance)
    first = jnp.where(upper, received_ref[...], own_ref[...])
    second = jnp.where(upper, own_ref[...], received_ref[...])
    out_ref[...] = follow(first, second)


def is_upper(distance):
    return lax.rem(lax.axis_index("tm") // distance, 2) == 1


def block_means(distances, *refs):
    out_ref, own_ref, other_ref = refs[-1], refs[0], refs[1]
    levels, gathered = refs[2 : 2 + len(distances)], refs[2 + len(distances) : -1]
    half, rows, states = own_ref.shape
    mean = jnp.zeros((1, states), F32)
    for level in reversed(range(len(distances))):
        if level == len(distances) - 1:
            entered = levels[level][0:1, :]
        else:
            entered = apply(levels[level][...], mean)
        mean = jnp.where(is_upper(distances[level]), entered, mean)
    place = lax.rem(lax.axis_index("tm"), len(gathered))
    for i in range(len(gathered) - 1):
        mean = jnp.where(i < place, apply(pick(gathered, place ^ i), mean), mean)
    early, late = in_order(half, own_ref, other_ref)
    results = []
    for maps in (early, late):
        start = mean
        for each in maps:
            mean = row_times(start, *split(each[:states])) + each[states : states + 1]
            results.append(mean)
    results = jnp.concatenate(results, axis=0).astype(BF16)
    for copy in range(out_ref.shape[0]):
        out_ref[copy] = results


def swaps(size, distance):
    return [(i, i ^ distance) for i in range(size)]


def body(obs_rows, obs_values, obs_hours, prior_precision, transition, site_basis):
    hours = lax.axis_size("site")
    blocks = lax.axis_size("tm")
    count, states = obs_rows.shape
    half = hours // 2
    pairs = half // 2
    sds = jax.ShapeDtypeStruct
    prior, turned = call(
        coupled_turned,
        (sds((states, states), F32), sds((states, states), F32)),
        (prior_precision, transition),
        "coupled_turned",
    )
    packed = sds((pairs, states + TAIL, states), F32)
    keep, send = call(
        functools.partial(local_grams, hours),
        (packed, packed),
        (obs_rows, obs_values, obs_hours),
        "local_grams",
        [
            pltpu.VMEM(obs_rows.shape, BF16),
            pltpu.VMEM(obs_values.shape, BF16),
            pltpu.VMEM(obs_hours.shape, jnp.int32),
            pltpu.SemaphoreType.DMA((3,)),
        ],
        in_hbm=True,
    )
    received = lax.ppermute(send, "site", swaps(hours, 1))
    rounded = sds((pairs, states + 2 * TAIL, states), BF16)
    distance = 2
    while distance < hours:
        total, send = call(add_and_round, (packed, rounded), (keep, received), "add_and_round")
        received = lax.ppermute(send, "site", swaps(hours, distance))
        distance *= 2
        if distance < hours:
            keep = call(add_received, packed, (total, received), "add_received")
            received = jnp.zeros_like(keep)
    maps = call(
        hour_maps,
        sds((half, states + 16, states), F32),
        (total, received, prior, turned),
        "hour_maps",
    )
    other = lax.ppermute(maps, "site", swaps(hours, 1))
    rows = states + 16
    height = (rows // 2 + 15) // 16 * 16
    own, part = call(
        block_map,
        (sds((rows, states), BF16), sds((height, states), BF16)),
        (maps, other),
        "block_map",
    )
    radix = 4
    devices = [(t, d) for t in range(blocks) for d in range(hours)]
    near_swap = [(t * hours + d, (t ^ (1 + d % 2)) * hours + d) for t, d in devices]
    far_swap = [(t * hours + d, (t ^ 3) * hours + d) for t, d in devices]
    near = lax.ppermute(own, ("tm", "site"), near_swap)
    far = lax.ppermute(part, ("tm", "site"), far_swap)
    other_near = lax.ppermute(near, "site", swaps(hours, 1))
    other_far = lax.ppermute(far, "site", swaps(hours, 1))
    block = sds(own.shape, BF16)
    gathered = (own,) + call(
        group_blocks, (block,) * 3, (own, near, far, other_near, other_far), "group_blocks"
    )
    distances, levels = [], []
    distance = radix
    if 2 * distance < blocks:
        joined = call(group_map, sds(own.shape, BF16), gathered, "group_map")
    while distance < blocks:
        if 2 * distance == blocks:
            if levels:
                shift = joined[states:].astype(F32).sum(axis=0, keepdims=True)
                shift = jnp.broadcast_to(shift, (8, states))
            else:
                shift = call(group_shift, sds((8, states), F32), gathered, "group_shift")
            received = lax.ppermute(shift, "tm", swaps(blocks, distance))
        else:
            received = lax.ppermute(joined, "tm", swaps(blocks, distance))
            joined = call(
                functools.partial(pair_map, distance),
                sds(own.shape, BF16),
                (joined, received),
                "pair_map",
            )
        distances.append(distance)
        levels.append(received)
        distance *= 2
    means = call(
        functools.partial(block_means, tuple(distances)),
        sds((blocks, hours, states), BF16),
        [maps, other] + levels + list(gathered),
        "block_means",
    )
    means = lax.all_to_all(means, "tm", 0, 0, tiled=True).reshape(blocks * hours, states)
    return jnp.einsum("hs,ns->hn", means, site_basis, preferred_element_type=F32).astype(BF16)


def solution(mesh):
    in_specs = (
        P(("tm", "site"), None),
        P(("tm", "site")),
        P(("tm", "site")),
        P(),
        P(),
        P(("tm", "site"), None),
    )
    out_specs = P(None, ("tm", "site"))
    return jax.shard_map(body, mesh=mesh, in_specs=in_specs, out_specs=out_specs, check_vma=False)
```

```python
import functools

import jax
import jax.numpy as jnp
from jax import lax
from jax.experimental import pallas as pl
from jax.experimental.pallas import tpu as pltpu
from jax.sharding import PartitionSpec as P

NS_ITERS = 8
TAIL = 8
CHUNKS = 4
BF16 = jnp.bfloat16
F32 = jnp.float32
VMEM_LIMIT = 40 * 2**20


def whole():
    return pl.BlockSpec(memory_space=pltpu.VMEM)


def call(kernel, outs, args, name, scratch=(), in_hbm=False):
    if in_hbm:
        args = [pltpu.with_memory_space_constraint(arg, pltpu.HBM) for arg in args]
    return pl.pallas_call(
        kernel,
        out_shape=outs,
        in_specs=[pl.BlockSpec(memory_space=pltpu.HBM) if in_hbm else whole()] * len(args),
        out_specs=jax.tree.map(lambda _: whole(), outs),
        scratch_shapes=scratch,
        compiler_params=pltpu.CompilerParams(vmem_limit_bytes=VMEM_LIMIT),
        name=name,
    )(*args)


def dot(a, b):
    return jnp.dot(a, b, preferred_element_type=F32)


def split(x):
    high = x.astype(BF16)
    return high, (x - high.astype(F32)).astype(BF16)


def dot_wide(a, b):
    a_high, a_low = split(a)
    b_high, b_low = split(b)
    return dot(
        jnp.concatenate([a_high, a_low, a_high], axis=1),
        jnp.concatenate([b_high, b_high, b_low], axis=0),
    )


def thirds(row):
    first = row.astype(BF16).astype(F32)
    second = (row - first).astype(BF16).astype(F32)
    third = row - first - second
    zeros = jnp.zeros((13, row.shape[1]), F32)
    return jnp.concatenate([first, second, third, zeros], axis=0).astype(BF16)


def row_times(row, *weights):
    rows = thirds(row)
    total = dot(rows, weights[0])
    for w in weights[1:]:
        total += dot(rows, w)
    return jnp.sum(total, axis=0, keepdims=True)


def own_half(hours):
    return lax.rem(lax.axis_index("site"), 2) * (hours // 2)


def local_grams(
    hours,
    rows_hbm,
    values_hbm,
    codes_hbm,
    keep_ref,
    send_ref,
    rows_ref,
    values_ref,
    codes_ref,
    sems,
):
    half = hours // 2
    states = rows_hbm.shape[1]
    start = own_half(hours)
    copies = [
        pltpu.make_async_copy(rows_hbm, rows_ref, sems.at[0]),
        pltpu.make_async_copy(values_hbm, values_ref, sems.at[1]),
        pltpu.make_async_copy(codes_hbm, codes_ref, sems.at[2]),
    ]
    for copy in copies:
        copy.start()
    for copy in copies:
        copy.wait()
    rows = rows_ref[...]
    turned = rows.T
    codes = codes_ref[...].reshape(1, rows.shape[0])
    values = values_ref[...].astype(F32).reshape(1, rows.shape[0])
    slots = []
    for slot in range(hours):
        hour = lax.rem(start + slot, hours)
        slots.append((codes == hour).astype(F32))
    masked = jnp.concatenate([turned * s.astype(BF16) for s in slots], axis=0)
    grams = dot(masked, rows)
    weighted = jnp.concatenate([s * values for s in slots], axis=0)
    pad = jnp.zeros((16 - hours, weighted.shape[1]), F32)
    drives = dot(jnp.concatenate([weighted, pad], axis=0).astype(BF16), rows)
    row_id = lax.broadcasted_iota(jnp.int32, (states, states), 0)
    column_id = lax.broadcasted_iota(jnp.int32, (states, states), 1)
    for out_ref, base in ((keep_ref, 0), (send_ref, half)):
        for pair in range(half // 2):
            first = base + 2 * pair
            a = grams[first * states : (first + 1) * states]
            b = grams[(first + 1) * states : (first + 2) * states]
            diagonal = jnp.sum(jnp.where(row_id == column_id, b, 0.0), axis=0, keepdims=True)
            out_ref[pair, :states, :] = jnp.where(row_id <= column_id, a, b)
            out_ref[pair, states:, :] = jnp.concatenate(
                [diagonal, drives[first : first + 2], jnp.zeros((TAIL - 3, states), F32)], axis=0
            )


def prepare(prior_ref, transition_ref, basis_ref, prior_out_ref, turned_ref, basis_out_ref):
    basis_out_ref[...] = basis_ref[...].T
    prior = prior_ref[...]
    prior_out_ref[...] = prior
    turned_ref[...] = dot_wide(transition_ref[...].T, prior)


def add_and_round(keep_ref, received_ref, sum_ref, send_ref):
    states = keep_ref.shape[2]
    for pair in range(keep_ref.shape[0]):
        total = keep_ref[pair] + received_ref[pair]
        sum_ref[pair] = total
        send_ref[pair, :states, :] = total[:states].astype(BF16)
        tail = total[states:]
        high = tail.astype(BF16).astype(F32)
        send_ref[pair, states:, :] = jnp.concatenate([high, tail - high], axis=0).astype(BF16)


def add_received(sum_ref, received_ref, out_ref):
    states = sum_ref.shape[2]
    for pair in range(sum_ref.shape[0]):
        out_ref[pair] = sum_of(sum_ref, received_ref, pair, states)


def sum_of(sum_ref, received_ref, pair, states):
    received = received_ref[pair].astype(F32)
    tail = received[states : states + TAIL] + received[states + TAIL :]
    return sum_ref[pair] + jnp.concatenate([received[:states], tail], axis=0)


def hour_maps(sum_ref, received_ref, prior_ref, turned_ref, out_ref, last_ref, firsts_ref):
    states = prior_ref.shape[0]
    prior = prior_ref[...]
    turned = turned_ref[...]
    row_id = lax.broadcasted_iota(jnp.int32, (states, states), 0)
    column_id = lax.broadcasted_iota(jnp.int32, (states, states), 1)
    running = []
    for pair in range(sum_ref.shape[0]):
        total = sum_of(sum_ref, received_ref, pair, states)
        square = total[:states]
        flipped = square.T
        upper, lower = row_id <= column_id, row_id > column_id
        gram_a = jnp.where(upper, square, flipped)
        gram_b = jnp.where(lower, square, flipped)
        gram_b = jnp.where(row_id == column_id, total[states : states + 1], gram_b)
        for gram, place in ((gram_a, states + 1), (gram_b, states + 2)):
            precision = prior + gram
            bound = jnp.max(jnp.sum(jnp.abs(precision), axis=0, keepdims=True), axis=1, keepdims=True)
            scale = 1.0 / bound
            offset = jnp.concatenate(
                [total[place : place + 1], jnp.zeros((15, states), F32)], axis=0
            )
            running.append((precision * scale, turned * scale, offset * scale))
    stacked = [jnp.concatenate(parts, axis=0) for parts in running]

    for _ in range(NS_ITERS - 2):
        stacked = [2.0 * z - dot_wide(z, z[:states]) for z in stacked]
    maps = []
    for z in stacked:
        power = (jnp.where(row_id == column_id, 1.0, 0.0) - z[:states]).astype(BF16)
        v = z[states:]
        product = dot(jnp.concatenate([power, v.astype(BF16)], axis=0), power)
        v = v + product[states:]
        maps.append(v + dot(v.astype(BF16), product[:states].astype(BF16)))
    for position in range(len(maps)):
        joined = maps[0] if position == 0 else append(joined, maps[position])
        out_ref[position] = joined
        if position < len(maps) - 1:
            firsts_ref[position] = rounded(joined)
    last_ref[...] = rounded(joined)


def rounded(affine):
    states = affine.shape[1]
    return jnp.concatenate([affine[:states].astype(BF16), thirds(affine[states : states + 1])], axis=0)


def append(earlier, latter):
    states = latter.shape[1]
    product = dot_wide(earlier, latter[:states])
    return jnp.concatenate([product[:states], product[states:] + latter[states:]], axis=0)


def in_order(own_ref, received_ref):
    first = lax.rem(lax.axis_index("site"), 2) == 0
    count = len(own_ref) if isinstance(own_ref, list) else own_ref.shape[0]
    early = [jnp.where(first, own_ref[i], received_ref[i]) for i in range(count)]
    late = [jnp.where(first, received_ref[i], own_ref[i]) for i in range(count)]
    return early, late


def block_map(own_ref, received_ref, out_ref, part_ref):
    half, rows, states = own_ref.shape
    early, late = in_order(own_ref, received_ref)
    out_ref[...] = rounded(append(early[-1], late[-1]))
    height = part_ref.shape[0]
    first = own_half(2 * half) == 0
    part_ref[...] = jnp.where(first, out_ref[:height, :], out_ref[rows - height :, :])


def merge(last_ref, near_ref, far_ref, out_ref):
    out_ref[...] = jnp.concatenate([last_ref[...], near_ref[...], far_ref[...]], axis=0)


def group_blocks(merged_ref, other_ref, *out_refs):
    first = lax.rem(lax.axis_index("site"), 2) == 0
    rows = out_refs[0].shape[0]
    height = (merged_ref.shape[0] - rows) // 2
    own, other = merged_ref[:rows, :], other_ref[:rows, :]
    out_refs[0][...] = follow(jnp.where(first, own, other), jnp.where(first, other, own))
    for place in range(2):
        start = rows + place * height
        part, other = merged_ref[start : start + height, :], other_ref[start : start + height, :]
        low = jnp.where(first, other, part)[2 * height - rows :]
        out_refs[1 + place][...] = jnp.concatenate([jnp.where(first, part, other), low], axis=0)


def shift_of(block):
    states = block.shape[1]
    return jnp.sum(block[states:].astype(F32), axis=0, keepdims=True)


def pick(refs, slot):
    value = refs[0][...]
    for i in range(1, len(refs)):
        value = jnp.where(slot == i, refs[i][...], value)
    return value


def apply(block, mean):
    return row_times(mean, block[: block.shape[1]]) + shift_of(block)


def follow(earlier, latter):
    states = latter.shape[1]
    product = dot(earlier[:states], latter[:states]).astype(BF16)
    return jnp.concatenate([product, thirds(apply(latter, shift_of(earlier)))], axis=0)


def group_shift(*refs):
    gathered, out_ref = refs[:-1], refs[-1]
    place = lax.rem(lax.axis_index("tm"), len(gathered))
    mean = shift_of(pick(gathered, place))
    for i in range(1, len(gathered)):
        mean = apply(pick(gathered, place ^ i), mean)
    out_ref[...] = jnp.broadcast_to(mean, out_ref.shape)


def group_map(*refs):
    gathered, out_ref = refs[:-1], refs[-1]
    place = lax.rem(lax.axis_index("tm"), len(gathered))
    joined = pick(gathered, place)
    for i in range(1, len(gathered)):
        joined = follow(joined, pick(gathered, place ^ i))
    out_ref[...] = joined


def pair_map(distance, own_ref, received_ref, out_ref):
    upper = is_upper(distance)
    first = jnp.where(upper, received_ref[...], own_ref[...])
    second = jnp.where(upper, own_ref[...], received_ref[...])
    out_ref[...] = follow(first, second)


def is_upper(distance):
    return lax.rem(lax.axis_index("tm") // distance, 2) == 1


def hold(maps_ref, received_ref, out_ref):
    out_ref[...] = maps_ref[...]


def pair_means(distances, *refs):
    out_ref = refs[-1]
    own_ref, other_ref, last_ref, other_last_ref = refs[:4]
    levels, gathered = refs[4 : 4 + len(distances)], refs[4 + len(distances) : -1]
    half, rows, states = own_ref.shape
    mean = jnp.zeros((1, states), F32)
    for level in reversed(range(len(distances))):
        if level == len(distances) - 1:
            entered = levels[level][0:1, :]
        else:
            entered = apply(levels[level][...], mean)
        mean = jnp.where(is_upper(distances[level]), entered, mean)
    place = lax.rem(lax.axis_index("tm"), len(gathered))
    for i in range(2):
        mean = jnp.where(place >= 2, apply(pick(gathered, place ^ i), mean), mean)
    odd = lax.rem(place, 2) == 1
    between = apply(pick(gathered, place & 1), mean)
    own_start = jnp.where(odd, between, mean)
    own = []
    for maps in in_order(own_ref, other_ref):
        start = own_start if not own else own[-1]
        for each in maps:
            own.append(row_times(start, *split(each[:states])) + each[states : states + 1])
    state = jnp.where(odd, mean, own[-1])
    partner = []
    for maps in in_order([last_ref[:rows, :]], [other_last_ref[:rows, :]]):
        partner += [state] * (half - 1)
        state = apply(maps[0], state)
        partner.append(state)
    own, partner = jnp.concatenate(own, axis=0), jnp.concatenate(partner, axis=0)
    out_ref[: 2 * half, :] = jnp.where(odd, partner, own)
    out_ref[2 * half :, :] = jnp.where(odd, own, partner)


def rest_of_means(means_ref, firsts_ref, other_ref, out_ref):
    count = firsts_ref.shape[0]
    hours = 2 * (count + 1)
    odd = lax.rem(lax.axis_index("tm"), 2) == 1
    out_ref[...] = means_ref[...]
    partner = jnp.where(odd, means_ref[:hours, :], means_ref[hours:, :])
    for side, maps in enumerate(in_order(firsts_ref, other_ref)):
        for i in range(count):
            hour = side * (count + 1) + i
            mean = apply(maps[i], partner[hour : hour + 1])
            out_ref[pl.ds(jnp.where(odd, hour, hours + hour), 1), :] = mean


def own_means(means_ref, out_ref):
    hours = out_ref.shape[1]
    odd = lax.rem(lax.axis_index("tm"), 2) == 1
    means = jnp.where(odd, means_ref[hours:, :], means_ref[:hours, :]).astype(BF16)
    for copy in range(out_ref.shape[0]):
        out_ref[copy] = means


def predict(*refs):
    means_refs, basis_ref, out_hbm, held_ref, sems = refs[:-4], *refs[-4:]
    if len(means_refs) > 1:
        place = lax.axis_index("tm") // 2
        means = [pick(means_refs, place ^ i) for i in range(len(means_refs))]
        means = jnp.concatenate(means, axis=0).astype(BF16)
    else:
        means = means_refs[0][...]
    width = held_ref.shape[2]
    copies = []
    for chunk in range(CHUNKS):
        columns = pl.ds(chunk * width, width)
        held_ref[chunk] = dot(means, basis_ref[:, columns]).astype(BF16)
        copy = pltpu.make_async_copy(held_ref.at[chunk], out_hbm.at[:, columns], sems.at[chunk])
        copy.start()
        copies.append(copy)
    for copy in copies:
        copy.wait()


def swaps(size, distance):
    return [(i, i ^ distance) for i in range(size)]


def body(obs_rows, obs_values, obs_hours, prior_precision, transition, site_basis):
    hours = lax.axis_size("site")
    blocks = lax.axis_size("tm")
    count, states = obs_rows.shape
    half = hours // 2
    pairs = half // 2
    sds = jax.ShapeDtypeStruct
    square = sds((states, states), F32)
    prior, turned, basis = call(
        prepare,
        (square, square, sds(site_basis.shape[::-1], BF16)),
        (prior_precision, transition, site_basis),
        "prepare",
    )
    packed = sds((pairs, states + TAIL, states), F32)
    keep, send = call(
        functools.partial(local_grams, hours),
        (packed, packed),
        (obs_rows, obs_values, obs_hours),
        "local_grams",
        [
            pltpu.VMEM(obs_rows.shape, BF16),
            pltpu.VMEM(obs_values.shape, BF16),
            pltpu.VMEM(obs_hours.shape, jnp.int32),
            pltpu.SemaphoreType.DMA((3,)),
        ],
        in_hbm=True,
    )
    received = lax.ppermute(send, "site", swaps(hours, 1))
    rounded = sds((pairs, states + 2 * TAIL, states), BF16)
    distance = 2
    while distance < hours:
        total, send = call(add_and_round, (packed, rounded), (keep, received), "add_and_round")
        received = lax.ppermute(send, "site", swaps(hours, distance))
        distance *= 2
        if distance < hours:
            keep = call(add_received, packed, (total, received), "add_received")
            received = jnp.zeros_like(keep)
    rows = states + 16
    block, height = sds((rows, states), BF16), (rows // 2 + 15) // 16 * 16
    firsts = sds((half - 1, rows, states), BF16)
    maps, last, first_maps = call(
        hour_maps,
        (sds((half, rows, states), F32), block, firsts),
        (total, received, prior, turned),
        "hour_maps",
    )
    other = lax.ppermute(maps, "site", swaps(hours, 1))
    last = lax.ppermute(last, "tm", swaps(blocks, 1))
    first_maps = lax.ppermute(first_maps, "tm", swaps(blocks, 1))
    own, part = call(
        block_map, (block, sds((height, states), BF16)), (maps, other), "block_map"
    )
    near = lax.ppermute(part, "tm", swaps(blocks, 2))
    far = lax.ppermute(part, "tm", swaps(blocks, 3))
    merged = call(merge, sds((rows + 2 * height, states), BF16), (last, near, far), "merge")
    other_merged = lax.ppermute(merged, "site", swaps(hours, 1))
    radix = 4
    gathered = (own,) + tuple(call(
        group_blocks, (block,) * 3, (merged, other_merged), "group_blocks"
    ))
    distances, levels = [], []
    distance = radix
    if 2 * distance < blocks:
        joined = call(group_map, sds(own.shape, BF16), gathered, "group_map")
    while distance < blocks:
        if 2 * distance == blocks:
            if levels:
                shift = joined[states:].astype(F32).sum(axis=0, keepdims=True)
                shift = jnp.broadcast_to(shift, (8, states))
            else:
                shift = call(group_shift, sds((8, states), F32), gathered, "group_shift")
            received = lax.ppermute(shift, "tm", swaps(blocks, distance))
        else:
            received = lax.ppermute(joined, "tm", swaps(blocks, distance))
            joined = call(
                functools.partial(pair_map, distance),
                sds(own.shape, BF16),
                (joined, received),
                "pair_map",
            )
        distances.append(distance)
        levels.append(received)
        distance *= 2
    means = call(
        functools.partial(pair_means, tuple(distances)),
        sds((2 * hours, states), F32),
        [maps, other, merged, other_merged] + levels + list(gathered),
        "pair_means",
    )
    first_maps = call(hold, firsts, (first_maps, levels[-1]), "hold")
    other_firsts = lax.ppermute(first_maps, "site", swaps(hours, 1))
    means = call(
        rest_of_means,
        sds(means.shape, F32),
        (means, first_maps, other_firsts),
        "rest_of_means",
    )
    if blocks <= 8:
        means = [means] + [lax.ppermute(means, "tm", swaps(blocks, d)) for d in range(2, blocks, 2)]
    else:
        means = call(own_means, sds((blocks, hours, states), BF16), (means,), "own_means")
        means = [lax.all_to_all(means, "tm", 0, 0, tiled=True).reshape(blocks * hours, states)]
    sites = site_basis.shape[0]
    return pl.pallas_call(
        predict,
        out_shape=sds((blocks * hours, sites), BF16),
        in_specs=[whole()] * (len(means) + 1),
        out_specs=pl.BlockSpec(memory_space=pltpu.HBM),
        scratch_shapes=[
            pltpu.VMEM((CHUNKS, blocks * hours, sites // CHUNKS), BF16),
            pltpu.SemaphoreType.DMA((CHUNKS,)),
        ],
        compiler_params=pltpu.CompilerParams(vmem_limit_bytes=VMEM_LIMIT),
        name="predict",
    )(*means, basis)


def solution(mesh):
    in_specs = (
        P(("tm", "site"), None),
        P(("tm", "site")),
        P(("tm", "site")),
        P(),
        P(),
        P(("tm", "site"), None),
    )
    out_specs = P(None, ("tm", "site"))
    return jax.shard_map(body, mesh=mesh, in_specs=in_specs, out_specs=out_specs, check_vma=False)
```

```python
import functools

import jax
import jax.numpy as jnp
from jax import lax
from jax.experimental import pallas as pl
from jax.experimental.pallas import tpu as pltpu
from jax.sharding import PartitionSpec as P

NS_ITERS = 8
TAIL = 8
CHUNKS = 4
BF16 = jnp.bfloat16
F32 = jnp.float32
VMEM_LIMIT = 40 * 2**20


def whole():
    return pl.BlockSpec(memory_space=pltpu.VMEM)


def call(kernel, outs, args, name, scratch=(), in_hbm=False):
    if in_hbm:
        args = [pltpu.with_memory_space_constraint(arg, pltpu.HBM) for arg in args]
    return pl.pallas_call(
        kernel,
        out_shape=outs,
        in_specs=[pl.BlockSpec(memory_space=pltpu.HBM) if in_hbm else whole()] * len(args),
        out_specs=jax.tree.map(lambda _: whole(), outs),
        scratch_shapes=scratch,
        compiler_params=pltpu.CompilerParams(vmem_limit_bytes=VMEM_LIMIT),
        name=name,
    )(*args)


def dot(a, b):
    return jnp.dot(a, b, preferred_element_type=F32)


def split(x):
    high = x.astype(BF16)
    return high, (x - high.astype(F32)).astype(BF16)


def dot_wide(a, b):
    a_high, a_low = split(a)
    b_high, b_low = split(b)
    return dot(
        jnp.concatenate([a_high, a_low, a_high], axis=1),
        jnp.concatenate([b_high, b_high, b_low], axis=0),
    )


def thirds(row):
    first = row.astype(BF16).astype(F32)
    second = (row - first).astype(BF16).astype(F32)
    third = row - first - second
    zeros = jnp.zeros((13, row.shape[1]), F32)
    return jnp.concatenate([first, second, third, zeros], axis=0).astype(BF16)


def row_times(row, *weights):
    rows = thirds(row)
    total = dot(rows, weights[0])
    for w in weights[1:]:
        total += dot(rows, w)
    return jnp.sum(total, axis=0, keepdims=True)


def own_half(hours):
    return lax.rem(lax.axis_index("site"), 2) * (hours // 2)


def local_grams(
    hours,
    rows_hbm,
    values_hbm,
    codes_hbm,
    keep_ref,
    send_ref,
    rows_ref,
    values_ref,
    codes_ref,
    sems,
):
    half = hours // 2
    states = rows_hbm.shape[1]
    start = own_half(hours)
    copies = [
        pltpu.make_async_copy(rows_hbm, rows_ref, sems.at[0]),
        pltpu.make_async_copy(values_hbm, values_ref, sems.at[1]),
        pltpu.make_async_copy(codes_hbm, codes_ref, sems.at[2]),
    ]
    for copy in copies:
        copy.start()
    for copy in copies:
        copy.wait()
    rows = rows_ref[...]
    turned = rows.T
    codes = codes_ref[...].reshape(1, rows.shape[0])
    values = values_ref[...].astype(F32).reshape(1, rows.shape[0])
    slots = []
    for slot in range(hours):
        hour = lax.rem(start + slot, hours)
        slots.append((codes == hour).astype(F32))
    masked = jnp.concatenate([turned * s.astype(BF16) for s in slots], axis=0)
    grams = dot(masked, rows)
    weighted = jnp.concatenate([s * values for s in slots], axis=0)
    pad = jnp.zeros((16 - hours, weighted.shape[1]), F32)
    drives = dot(jnp.concatenate([weighted, pad], axis=0).astype(BF16), rows)
    row_id = lax.broadcasted_iota(jnp.int32, (states, states), 0)
    column_id = lax.broadcasted_iota(jnp.int32, (states, states), 1)
    for out_ref, base in ((keep_ref, 0), (send_ref, half)):
        for pair in range(half // 2):
            first = base + 2 * pair
            a = grams[first * states : (first + 1) * states]
            b = grams[(first + 1) * states : (first + 2) * states]
            diagonal = jnp.sum(jnp.where(row_id == column_id, b, 0.0), axis=0, keepdims=True)
            out_ref[pair, :states, :] = jnp.where(row_id <= column_id, a, b)
            out_ref[pair, states:, :] = jnp.concatenate(
                [diagonal, drives[first : first + 2], jnp.zeros((TAIL - 3, states), F32)], axis=0
            )


def prepare(
    prior_hbm,
    transition_hbm,
    basis_hbm,
    prior_out_ref,
    turned_ref,
    basis_out_ref,
    transition_ref,
    basis_ref,
    sems,
):
    copies = [
        pltpu.make_async_copy(prior_hbm, prior_out_ref, sems.at[0]),
        pltpu.make_async_copy(transition_hbm, transition_ref, sems.at[1]),
        pltpu.make_async_copy(basis_hbm, basis_ref, sems.at[2]),
    ]
    for copy in copies:
        copy.start()
    copies[0].wait()
    copies[1].wait()
    prior = prior_out_ref[...]
    turned_ref[...] = dot_wide(transition_ref[...].T, prior)
    copies[2].wait()
    basis_out_ref[...] = basis_ref[...].T


def add_and_round(keep_ref, received_ref, sum_ref, send_ref):
    states = keep_ref.shape[2]
    for pair in range(keep_ref.shape[0]):
        total = keep_ref[pair] + received_ref[pair]
        sum_ref[pair] = total
        send_ref[pair, :states, :] = total[:states].astype(BF16)
        tail = total[states:]
        high = tail.astype(BF16).astype(F32)
        send_ref[pair, states:, :] = jnp.concatenate([high, tail - high], axis=0).astype(BF16)


def add_received(sum_ref, received_ref, out_ref):
    states = sum_ref.shape[2]
    for pair in range(sum_ref.shape[0]):
        out_ref[pair] = sum_of(sum_ref, received_ref, pair, states)


def sum_of(sum_ref, received_ref, pair, states):
    received = received_ref[pair].astype(F32)
    tail = received[states : states + TAIL] + received[states + TAIL :]
    return sum_ref[pair] + jnp.concatenate([received[:states], tail], axis=0)


def hour_maps(
    sum_ref,
    received_ref,
    prior_ref,
    turned_ref,
    last_ref,
    firsts_ref,
    rounded_last_ref,
    rounded_firsts_ref,
):
    states = prior_ref.shape[0]
    prior = prior_ref[...]
    turned = turned_ref[...]
    row_id = lax.broadcasted_iota(jnp.int32, (states, states), 0)
    column_id = lax.broadcasted_iota(jnp.int32, (states, states), 1)
    running = []
    for pair in range(sum_ref.shape[0]):
        total = sum_of(sum_ref, received_ref, pair, states)
        square = total[:states]
        flipped = square.T
        upper, lower = row_id <= column_id, row_id > column_id
        gram_a = jnp.where(upper, square, flipped)
        gram_b = jnp.where(lower, square, flipped)
        gram_b = jnp.where(row_id == column_id, total[states : states + 1], gram_b)
        for gram, place in ((gram_a, states + 1), (gram_b, states + 2)):
            precision = prior + gram
            bound = jnp.max(jnp.sum(jnp.abs(precision), axis=0, keepdims=True), axis=1, keepdims=True)
            scale = 1.0 / bound
            offset = jnp.concatenate(
                [total[place : place + 1], jnp.zeros((15, states), F32)], axis=0
            )
            running.append((precision * scale, turned * scale, offset * scale))
    stacked = [jnp.concatenate(parts, axis=0) for parts in running]

    for _ in range(NS_ITERS - 2):
        stacked = [2.0 * z - dot_wide(z, z[:states]) for z in stacked]
    maps = []
    for z in stacked:
        power = (jnp.where(row_id == column_id, 1.0, 0.0) - z[:states]).astype(BF16)
        v = z[states:]
        product = dot(jnp.concatenate([power, v.astype(BF16)], axis=0), power)
        v = v + product[states:]
        maps.append(v + dot(v.astype(BF16), product[:states].astype(BF16)))
    for position in range(len(maps)):
        joined = maps[0] if position == 0 else append(joined, maps[position])
        if position < len(maps) - 1:
            firsts_ref[position] = joined
            rounded_firsts_ref[position] = rounded(joined)
    last_ref[...] = joined
    rounded_last_ref[...] = rounded(joined)


def rounded(affine):
    states = affine.shape[1]
    return jnp.concatenate([affine[:states].astype(BF16), thirds(affine[states : states + 1])], axis=0)


def append(earlier, latter):
    states = latter.shape[1]
    product = dot_wide(earlier, latter[:states])
    return jnp.concatenate([product[:states], product[states:] + latter[states:]], axis=0)


def in_order(own_ref, received_ref):
    first = lax.rem(lax.axis_index("site"), 2) == 0
    count = len(own_ref) if isinstance(own_ref, list) else own_ref.shape[0]
    early = [jnp.where(first, own_ref[i], received_ref[i]) for i in range(count)]
    late = [jnp.where(first, received_ref[i], own_ref[i]) for i in range(count)]
    return early, late


def block_map(own_ref, received_ref, out_ref):
    (early,), (late,) = in_order([own_ref[...]], [received_ref[...]])
    out_ref[...] = rounded(append(early, late))


def merge(last_ref, far_ref, out_ref):
    out_ref[0] = last_ref[...]
    out_ref[1] = far_ref[...]


def group_blocks(own_ref, merged_ref, other_ref, *out_refs):
    shift_ref, out_refs = out_refs[-1], out_refs[:-1]
    (early,), (late,) = in_order([merged_ref[0]], [other_ref[0]])
    out_refs[0][...] = follow(early, late)
    (near,), (far,) = in_order([merged_ref[1]], [other_ref[1]])
    out_refs[1][...] = near
    out_refs[2][...] = far
    group_shift(own_ref, *out_refs, shift_ref)


def shift_of(block):
    states = block.shape[1]
    return jnp.sum(block[states:].astype(F32), axis=0, keepdims=True)


def choose(values, slot):
    value = values[0]
    for i in range(1, len(values)):
        value = jnp.where(slot == i, values[i], value)
    return value


def pick(refs, slot):
    return choose([ref[...] for ref in refs], slot)


def apply(block, mean):
    return row_times(mean, block[: block.shape[1]]) + shift_of(block)


def follow(earlier, latter):
    states = latter.shape[1]
    product = dot(earlier[:states], latter[:states]).astype(BF16)
    return jnp.concatenate([product, thirds(apply(latter, shift_of(earlier)))], axis=0)


def group_shift(*refs):
    gathered, out_ref = refs[:-1], refs[-1]
    place = lax.rem(lax.axis_index("tm"), len(gathered))
    mean = shift_of(pick(gathered, place))
    for i in range(1, len(gathered)):
        mean = apply(pick(gathered, place ^ i), mean)
    out_ref[...] = jnp.broadcast_to(mean, out_ref.shape)


def group_map(*refs):
    gathered, out_ref = refs[:-1], refs[-1]
    place = lax.rem(lax.axis_index("tm"), len(gathered))
    joined = pick(gathered, place)
    for i in range(1, len(gathered)):
        joined = follow(joined, pick(gathered, place ^ i))
    out_ref[...] = joined


def pair_map(distance, own_ref, received_ref, out_ref):
    upper = is_upper(distance)
    first = jnp.where(upper, received_ref[...], own_ref[...])
    second = jnp.where(upper, own_ref[...], received_ref[...])
    out_ref[...] = follow(first, second)


def is_upper(distance):
    return lax.rem(lax.axis_index("tm") // distance, 2) == 1


def hold(maps_ref, received_ref, out_ref):
    out_ref[...] = maps_ref[...]


def pair_means(distances, *refs):
    out_ref = refs[-1]
    own_last_ref, own_other_ref, own_firsts_ref, other_firsts_ref, merged_ref, other_merged_ref = refs[:6]
    levels, gathered = refs[6 : 6 + len(distances)], refs[6 + len(distances) : -1]
    rows, states = own_last_ref.shape
    half = own_firsts_ref.shape[0] + 1
    mean = jnp.zeros((1, states), F32)
    for level in reversed(range(len(distances))):
        if level == len(distances) - 1:
            entered = levels[level][0:1, :]
        else:
            entered = apply(levels[level][...], mean)
        mean = jnp.where(is_upper(distances[level]), entered, mean)
    place = lax.rem(lax.axis_index("tm"), len(gathered))
    for i in range(2):
        mean = jnp.where(place >= 2, apply(pick(gathered, place ^ i), mean), mean)
    odd = lax.rem(place, 2) == 1
    between = apply(pick(gathered, place & 1), mean)
    own_start = jnp.where(odd, between, mean)
    own = []
    sides = [
        [firsts[i] for i in range(half - 1)] + [last[...]]
        for firsts, last in ((own_firsts_ref, own_last_ref), (other_firsts_ref, own_other_ref))
    ]
    for maps in in_order(*sides):
        start = own_start if not own else own[-1]
        for each in maps:
            own.append(row_times(start, *split(each[:states])) + each[states : states + 1])
    state = jnp.where(odd, mean, own[-1])
    partner = []
    for maps in in_order([merged_ref[0]], [other_merged_ref[0]]):
        partner += [state] * (half - 1)
        state = apply(maps[0], state)
        partner.append(state)
    own, partner = jnp.concatenate(own, axis=0), jnp.concatenate(partner, axis=0)
    out_ref[: 2 * half, :] = jnp.where(odd, partner, own)
    out_ref[2 * half :, :] = jnp.where(odd, own, partner)


def rest_of_means(means_ref, firsts_ref, other_ref, out_ref):
    count = firsts_ref.shape[0]
    hours = 2 * (count + 1)
    odd = lax.rem(lax.axis_index("tm"), 2) == 1
    out_ref[...] = means_ref[...]
    partner = jnp.where(odd, means_ref[:hours, :], means_ref[hours:, :])
    for side, maps in enumerate(in_order(firsts_ref, other_ref)):
        for i in range(count):
            hour = side * (count + 1) + i
            mean = apply(maps[i], partner[hour : hour + 1])
            out_ref[pl.ds(jnp.where(odd, hour, hours + hour), 1), :] = mean


def own_means(means_ref, out_ref):
    hours = out_ref.shape[1]
    odd = lax.rem(lax.axis_index("tm"), 2) == 1
    means = jnp.where(odd, means_ref[hours:, :], means_ref[:hours, :]).astype(BF16)
    for copy in range(out_ref.shape[0]):
        out_ref[copy] = means


def predict(*refs):
    means_refs, basis_ref, out_hbm, held_ref, sems = refs[:-4], *refs[-4:]
    if len(means_refs) > 1:
        place = lax.axis_index("tm") // 2
        own, near, far, other_far = [ref[...] for ref in means_refs]
        (third,), (fourth,) = in_order([far], [other_far])
        by_distance = [own, near, third, fourth]
        means = jnp.concatenate([choose(by_distance, place ^ i) for i in range(4)], axis=0)
        means = means.astype(BF16)
    else:
        means = means_refs[0][...]
    width = held_ref.shape[2]
    copies = []
    for chunk in range(CHUNKS):
        columns = pl.ds(chunk * width, width)
        held_ref[chunk] = dot(means, basis_ref[:, columns]).astype(BF16)
        copy = pltpu.make_async_copy(held_ref.at[chunk], out_hbm.at[:, columns], sems.at[chunk])
        copy.start()
        copies.append(copy)
    for copy in copies:
        copy.wait()


def core_swaps(blocks, hours, first, second):
    distances = [first, second] * (hours // 2)
    return [
        (t * hours + d, (t ^ distances[d]) * hours + d) for t in range(blocks) for d in range(hours)
    ]


def swaps(size, distance):
    return [(i, i ^ distance) for i in range(size)]


def body(obs_rows, obs_values, obs_hours, prior_precision, transition, site_basis):
    hours = lax.axis_size("site")
    blocks = lax.axis_size("tm")
    count, states = obs_rows.shape
    half = hours // 2
    pairs = half // 2
    sds = jax.ShapeDtypeStruct
    square = sds((states, states), F32)
    prior, turned, basis = call(
        prepare,
        (square, square, sds(site_basis.shape[::-1], BF16)),
        (prior_precision, transition, site_basis),
        "prepare",
        [
            pltpu.VMEM(transition.shape, F32),
            pltpu.VMEM(site_basis.shape, BF16),
            pltpu.SemaphoreType.DMA((3,)),
        ],
        in_hbm=True,
    )
    packed = sds((pairs, states + TAIL, states), F32)
    keep, send = call(
        functools.partial(local_grams, hours),
        (packed, packed),
        (obs_rows, obs_values, obs_hours),
        "local_grams",
        [
            pltpu.VMEM(obs_rows.shape, BF16),
            pltpu.VMEM(obs_values.shape, BF16),
            pltpu.VMEM(obs_hours.shape, jnp.int32),
            pltpu.SemaphoreType.DMA((3,)),
        ],
        in_hbm=True,
    )
    received = lax.ppermute(send, "site", swaps(hours, 1))
    rounded = sds((pairs, states + 2 * TAIL, states), BF16)
    distance = 2
    while distance < hours:
        total, send = call(add_and_round, (packed, rounded), (keep, received), "add_and_round")
        received = lax.ppermute(send, "site", swaps(hours, distance))
        distance *= 2
        if distance < hours:
            keep = call(add_received, packed, (total, received), "add_received")
            received = jnp.zeros_like(keep)
    rows = states + 16
    block = sds((rows, states), BF16)
    firsts = sds((half - 1, rows, states), BF16)
    own_last, own_firsts, last, first_maps = call(
        hour_maps,
        (sds((rows, states), F32), sds((half - 1, rows, states), F32), block, firsts),
        (total, received, prior, turned),
        "hour_maps",
    )
    other_last = lax.ppermute(own_last, "site", swaps(hours, 1))
    last = lax.ppermute(last, "tm", swaps(blocks, 1))
    first_maps = lax.ppermute(first_maps, "tm", swaps(blocks, 1))
    own = call(block_map, block, (own_last, other_last), "block_map")
    far = lax.ppermute(own, ("tm", "site"), core_swaps(blocks, hours, 2, 3))
    merged = call(merge, sds((2, rows, states), BF16), (last, far), "merge")
    other_merged = lax.ppermute(merged, "site", swaps(hours, 1))
    radix = 4
    *gathered, shift = call(
        group_blocks,
        (block,) * 3 + (sds((8, states), F32),),
        (own, merged, other_merged),
        "group_blocks",
    )
    gathered = (own, *gathered)
    distances, levels = [], []
    distance = radix
    if 2 * distance < blocks:
        joined = call(group_map, sds(own.shape, BF16), gathered, "group_map")
    while distance < blocks:
        if 2 * distance == blocks:
            if levels:
                shift = joined[states:].astype(F32).sum(axis=0, keepdims=True)
                shift = jnp.broadcast_to(shift, (8, states))
            received = lax.ppermute(shift, "tm", swaps(blocks, distance))
        else:
            received = lax.ppermute(joined, "tm", swaps(blocks, distance))
            joined = call(
                functools.partial(pair_map, distance),
                sds(own.shape, BF16),
                (joined, received),
                "pair_map",
            )
        distances.append(distance)
        levels.append(received)
        distance *= 2
    other_firsts = lax.ppermute(own_firsts, "site", swaps(hours, 1))
    means = call(
        functools.partial(pair_means, tuple(distances)),
        sds((2 * hours, states), F32),
        [own_last, other_last, own_firsts, other_firsts, merged, other_merged]
        + levels
        + list(gathered),
        "pair_means",
    )
    first_maps = call(hold, firsts, (first_maps, levels[-1]), "hold")
    other_firsts = lax.ppermute(first_maps, "site", swaps(hours, 1))
    means = call(
        rest_of_means,
        sds(means.shape, F32),
        (means, first_maps, other_firsts),
        "rest_of_means",
    )
    if blocks == 2 * radix:
        far = lax.ppermute(means, ("tm", "site"), core_swaps(blocks, hours, 4, 6))
        near = lax.ppermute(means, "tm", swaps(blocks, 2))
        other_far = lax.ppermute(far, "site", swaps(hours, 1))
        means = [means, near, far, other_far]
    else:
        means = call(own_means, sds((blocks, hours, states), BF16), (means,), "own_means")
        means = [lax.all_to_all(means, "tm", 0, 0, tiled=True).reshape(blocks * hours, states)]
    sites = site_basis.shape[0]
    return pl.pallas_call(
        predict,
        out_shape=sds((blocks * hours, sites), BF16),
        in_specs=[whole()] * (len(means) + 1),
        out_specs=pl.BlockSpec(memory_space=pltpu.HBM),
        scratch_shapes=[
            pltpu.VMEM((CHUNKS, blocks * hours, sites // CHUNKS), BF16),
            pltpu.SemaphoreType.DMA((CHUNKS,)),
        ],
        compiler_params=pltpu.CompilerParams(vmem_limit_bytes=VMEM_LIMIT),
        name="predict",
    )(*means, basis)


def solution(mesh):
    in_specs = (
        P(("tm", "site"), None),
        P(("tm", "site")),
        P(("tm", "site")),
        P(),
        P(),
        P(("tm", "site"), None),
    )
    out_specs = P(None, ("tm", "site"))
    return jax.shard_map(body, mesh=mesh, in_specs=in_specs, out_specs=out_specs, check_vma=False)
```

```python
import functools

import jax
import jax.numpy as jnp
from jax import lax
from jax.experimental import pallas as pl
from jax.experimental.pallas import tpu as pltpu
from jax.sharding import PartitionSpec as P

NS_ITERS = 8
TAIL = 8
CHUNKS = 4
BF16 = jnp.bfloat16
F32 = jnp.float32
VMEM_LIMIT = 40 * 2**20


def whole():
    return pl.BlockSpec(memory_space=pltpu.VMEM)


def call(kernel, outs, args, name, scratch=(), in_hbm=False):
    if in_hbm:
        args = [pltpu.with_memory_space_constraint(arg, pltpu.HBM) for arg in args]
    return pl.pallas_call(
        kernel,
        out_shape=outs,
        in_specs=[pl.BlockSpec(memory_space=pltpu.HBM) if in_hbm else whole()] * len(args),
        out_specs=jax.tree.map(lambda _: whole(), outs),
        scratch_shapes=scratch,
        compiler_params=pltpu.CompilerParams(vmem_limit_bytes=VMEM_LIMIT),
        name=name,
    )(*args)


def dot(a, b):
    return jnp.dot(a, b, preferred_element_type=F32)


def split(x):
    high = x.astype(BF16)
    return high, (x - high.astype(F32)).astype(BF16)


def dot_wide(a, b):
    a_high, a_low = split(a)
    b_high, b_low = split(b)
    return dot(
        jnp.concatenate([a_high, a_low, a_high], axis=1),
        jnp.concatenate([b_high, b_high, b_low], axis=0),
    )


def thirds(row):
    first = row.astype(BF16).astype(F32)
    second = (row - first).astype(BF16).astype(F32)
    third = row - first - second
    zeros = jnp.zeros((13, row.shape[1]), F32)
    return jnp.concatenate([first, second, third, zeros], axis=0).astype(BF16)


def row_times(row, *weights):
    rows = thirds(row)
    total = dot(rows, weights[0])
    for w in weights[1:]:
        total += dot(rows, w)
    return jnp.sum(total, axis=0, keepdims=True)


def own_half(hours):
    return lax.rem(lax.axis_index("site"), 2) * (hours // 2)


def local_grams(
    hours,
    rows_hbm,
    values_hbm,
    codes_hbm,
    keep_ref,
    send_ref,
    rows_ref,
    values_ref,
    codes_ref,
    sems,
):
    half = hours // 2
    states = rows_hbm.shape[1]
    start = own_half(hours)
    copies = [
        pltpu.make_async_copy(rows_hbm, rows_ref, sems.at[0]),
        pltpu.make_async_copy(values_hbm, values_ref, sems.at[1]),
        pltpu.make_async_copy(codes_hbm, codes_ref, sems.at[2]),
    ]
    for copy in copies:
        copy.start()
    for copy in copies:
        copy.wait()
    rows = rows_ref[...]
    turned = rows.T
    codes = codes_ref[...].reshape(1, rows.shape[0])
    values = values_ref[...].astype(F32).reshape(1, rows.shape[0])
    slots = []
    for slot in range(hours):
        hour = lax.rem(start + slot, hours)
        slots.append((codes == hour).astype(F32))
    masked = jnp.concatenate([turned * s.astype(BF16) for s in slots], axis=0)
    grams = dot(masked, rows)
    weighted = jnp.concatenate([s * values for s in slots], axis=0)
    pad = jnp.zeros((16 - hours, weighted.shape[1]), F32)
    drives = dot(jnp.concatenate([weighted, pad], axis=0).astype(BF16), rows)
    row_id = lax.broadcasted_iota(jnp.int32, (states, states), 0)
    column_id = lax.broadcasted_iota(jnp.int32, (states, states), 1)
    for base in (0, half):
        for pair in range(half // 2):
            first = base + 2 * pair
            a = grams[first * states : (first + 1) * states]
            b = grams[(first + 1) * states : (first + 2) * states]
            diagonals = [
                jnp.sum(jnp.where(row_id == column_id, gram, 0.0), axis=0, keepdims=True)
                for gram in (a, b)
            ]
            square = jnp.where(row_id <= column_id, a, b)
            tail = jnp.concatenate(
                diagonals + [drives[first : first + 2], jnp.zeros((TAIL - 4, states), F32)], axis=0
            )
            if base == 0:
                keep_ref[pair, :states, :] = square
                keep_ref[pair, states:, :] = tail
            else:
                store_rounded(send_ref, pair, square, tail)


def prepare(
    prior_hbm,
    transition_hbm,
    basis_hbm,
    prior_out_ref,
    turned_ref,
    basis_out_ref,
    transition_ref,
    basis_ref,
    sems,
):
    copies = [
        pltpu.make_async_copy(prior_hbm, prior_out_ref, sems.at[0]),
        pltpu.make_async_copy(transition_hbm, transition_ref, sems.at[1]),
        pltpu.make_async_copy(basis_hbm, basis_ref, sems.at[2]),
    ]
    for copy in copies:
        copy.start()
    copies[0].wait()
    copies[1].wait()
    prior = prior_out_ref[...]
    turned_ref[...] = dot_wide(transition_ref[...].T, prior)
    copies[2].wait()
    basis_out_ref[...] = basis_ref[...].T


def add_and_round(keep_ref, received_ref, sum_ref, send_ref):
    states = keep_ref.shape[2]
    for pair in range(keep_ref.shape[0]):
        total = sum_of(keep_ref, received_ref, pair, states)
        sum_ref[pair] = total
        store_rounded(send_ref, pair, total[:states], total[states:])


def store_rounded(out_ref, pair, square, tail):
    states = square.shape[1]
    out_ref[pair, :states, :] = square.astype(BF16)
    high = tail.astype(BF16).astype(F32)
    out_ref[pair, states:, :] = jnp.concatenate([high, tail - high], axis=0).astype(BF16)


def add_received(sum_ref, received_ref, out_ref):
    states = sum_ref.shape[2]
    for pair in range(sum_ref.shape[0]):
        out_ref[pair] = sum_of(sum_ref, received_ref, pair, states)


def sum_of(sum_ref, received_ref, pair, states):
    received = received_ref[pair].astype(F32)
    tail = received[states : states + TAIL] + received[states + TAIL :]
    return sum_ref[pair] + jnp.concatenate([received[:states], tail], axis=0)


def hour_maps(
    sum_ref,
    received_ref,
    prior_ref,
    turned_ref,
    last_ref,
    firsts_ref,
    rounded_last_ref,
    rounded_firsts_ref,
):
    states = prior_ref.shape[0]
    prior = prior_ref[...]
    turned = turned_ref[...]
    row_id = lax.broadcasted_iota(jnp.int32, (states, states), 0)
    column_id = lax.broadcasted_iota(jnp.int32, (states, states), 1)
    running = []
    for pair in range(sum_ref.shape[0]):
        total = sum_of(sum_ref, received_ref, pair, states)
        square = total[:states]
        flipped = square.T
        upper, lower = row_id <= column_id, row_id > column_id
        grams = (jnp.where(upper, square, flipped), jnp.where(lower, square, flipped))
        for place, gram in enumerate(grams):
            diagonal, drive = [total[states + i : states + i + 1] for i in (place, place + 2)]
            gram = jnp.where(row_id == column_id, diagonal, gram)
            precision = prior + gram
            bound = jnp.max(jnp.sum(jnp.abs(precision), axis=0, keepdims=True), axis=1, keepdims=True)
            scale = 1.0 / bound
            offset = jnp.concatenate([drive, jnp.zeros((15, states), F32)], axis=0)
            running.append((precision * scale, turned * scale, offset * scale))
    stacked = [jnp.concatenate(parts, axis=0) for parts in running]

    for _ in range(NS_ITERS - 2):
        stacked = [2.0 * z - dot_wide(z, z[:states]) for z in stacked]
    maps = []
    for z in stacked:
        power = (jnp.where(row_id == column_id, 1.0, 0.0) - z[:states]).astype(BF16)
        v = z[states:]
        product = dot(jnp.concatenate([power, v.astype(BF16)], axis=0), power)
        v = v + product[states:]
        maps.append(v + dot(v.astype(BF16), product[:states].astype(BF16)))
    for position in range(len(maps)):
        joined = maps[0] if position == 0 else append(joined, maps[position])
        if position < len(maps) - 1:
            firsts_ref[position] = joined
            rounded_firsts_ref[position] = rounded(joined)
    last_ref[...] = joined
    rounded_last_ref[...] = rounded(joined)


def rounded(affine):
    states = affine.shape[1]
    return jnp.concatenate([affine[:states].astype(BF16), thirds(affine[states : states + 1])], axis=0)


def append(earlier, latter):
    states = latter.shape[1]
    product = dot_wide(earlier, latter[:states])
    return jnp.concatenate([product[:states], product[states:] + latter[states:]], axis=0)


def in_order(own_ref, received_ref):
    first = lax.rem(lax.axis_index("site"), 2) == 0
    count = len(own_ref) if isinstance(own_ref, list) else own_ref.shape[0]
    early = [jnp.where(first, own_ref[i], received_ref[i]) for i in range(count)]
    late = [jnp.where(first, received_ref[i], own_ref[i]) for i in range(count)]
    return early, late


def block_map(own_ref, received_ref, out_ref):
    (early,), (late,) = in_order([own_ref[...]], [received_ref[...]])
    out_ref[...] = rounded(append(early, late))


def group_blocks(own_ref, last_ref, far_ref, other_last_ref, other_far_ref, *out_refs):
    shift_ref, out_refs = out_refs[-1], out_refs[:-1]
    (early,), (late,) = in_order([last_ref[...]], [other_last_ref[...]])
    out_refs[0][...] = follow(early, late)
    (near,), (far,) = in_order([far_ref[...]], [other_far_ref[...]])
    out_refs[1][...] = near
    out_refs[2][...] = far
    group_shift(own_ref, *out_refs, shift_ref)


def shift_of(block):
    states = block.shape[1]
    return jnp.sum(block[states:].astype(F32), axis=0, keepdims=True)


def choose(values, slot):
    value = values[0]
    for i in range(1, len(values)):
        value = jnp.where(slot == i, values[i], value)
    return value


def pick(refs, slot):
    return choose([ref[...] for ref in refs], slot)


def apply(block, mean):
    return row_times(mean, block[: block.shape[1]]) + shift_of(block)


def follow(earlier, latter):
    states = latter.shape[1]
    product = dot(earlier[:states], latter[:states]).astype(BF16)
    return jnp.concatenate([product, thirds(apply(latter, shift_of(earlier)))], axis=0)


def group_shift(*refs):
    gathered, out_ref = refs[:-1], refs[-1]
    place = lax.rem(lax.axis_index("tm"), len(gathered))
    mean = shift_of(pick(gathered, place))
    for i in range(1, len(gathered)):
        mean = apply(pick(gathered, place ^ i), mean)
    out_ref[...] = jnp.broadcast_to(mean, out_ref.shape)


def group_map(*refs):
    gathered, out_ref = refs[:-1], refs[-1]
    place = lax.rem(lax.axis_index("tm"), len(gathered))
    joined = pick(gathered, place)
    for i in range(1, len(gathered)):
        joined = follow(joined, pick(gathered, place ^ i))
    out_ref[...] = joined


def pair_map(distance, own_ref, received_ref, out_ref):
    upper = is_upper(distance)
    first = jnp.where(upper, received_ref[...], own_ref[...])
    second = jnp.where(upper, own_ref[...], received_ref[...])
    out_ref[...] = follow(first, second)


def is_upper(distance):
    return lax.rem(lax.axis_index("tm") // distance, 2) == 1


def hold(maps_ref, received_ref, out_ref):
    out_ref[...] = maps_ref[...]


def pair_means(distances, *refs):
    out_ref = refs[-1]
    own_last_ref, own_other_ref, own_firsts_ref, other_firsts_ref, last_ref, other_last_ref = refs[:6]
    levels, gathered = refs[6 : 6 + len(distances)], refs[6 + len(distances) : -1]
    rows, states = own_last_ref.shape
    half = own_firsts_ref.shape[0] + 1
    mean = jnp.zeros((1, states), F32)
    for level in reversed(range(len(distances))):
        if level == len(distances) - 1:
            entered = levels[level][0:1, :]
        else:
            entered = apply(levels[level][...], mean)
        mean = jnp.where(is_upper(distances[level]), entered, mean)
    place = lax.rem(lax.axis_index("tm"), len(gathered))
    for i in range(2):
        mean = jnp.where(place >= 2, apply(pick(gathered, place ^ i), mean), mean)
    odd = lax.rem(place, 2) == 1
    between = apply(pick(gathered, place & 1), mean)
    own_start = jnp.where(odd, between, mean)
    own = []
    sides = [
        [firsts[i] for i in range(half - 1)] + [last[...]]
        for firsts, last in ((own_firsts_ref, own_last_ref), (other_firsts_ref, own_other_ref))
    ]
    for maps in in_order(*sides):
        start = own_start if not own else own[-1]
        for each in maps:
            own.append(row_times(start, *split(each[:states])) + each[states : states + 1])
    state = jnp.where(odd, mean, own[-1])
    partner = []
    for maps in in_order([last_ref[...]], [other_last_ref[...]]):
        partner += [state] * (half - 1)
        state = apply(maps[0], state)
        partner.append(state)
    own, partner = jnp.concatenate(own, axis=0), jnp.concatenate(partner, axis=0)
    out_ref[: 2 * half, :] = jnp.where(odd, partner, own)
    out_ref[2 * half :, :] = jnp.where(odd, own, partner)


def rest_of_means(means_ref, firsts_ref, other_ref, out_ref):
    count = firsts_ref.shape[0]
    hours = 2 * (count + 1)
    odd = lax.rem(lax.axis_index("tm"), 2) == 1
    out_ref[...] = means_ref[...]
    partner = jnp.where(odd, means_ref[:hours, :], means_ref[hours:, :])
    for side, maps in enumerate(in_order(firsts_ref, other_ref)):
        for i in range(count):
            hour = side * (count + 1) + i
            mean = apply(maps[i], partner[hour : hour + 1])
            out_ref[pl.ds(jnp.where(odd, hour, hours + hour), 1), :] = mean


def own_means(means_ref, out_ref):
    hours = out_ref.shape[1]
    odd = lax.rem(lax.axis_index("tm"), 2) == 1
    means = jnp.where(odd, means_ref[hours:, :], means_ref[:hours, :]).astype(BF16)
    for copy in range(out_ref.shape[0]):
        out_ref[copy] = means


def predict(*refs):
    means_refs, basis_ref, out_hbm, held_ref, sems = refs[:-4], *refs[-4:]
    if len(means_refs) > 1:
        place = lax.axis_index("tm") // 2
        own, near, far, other_far = [ref[...] for ref in means_refs]
        (third,), (fourth,) = in_order([far], [other_far])
        by_distance = [own, near, third, fourth]
        means = jnp.concatenate([choose(by_distance, place ^ i) for i in range(4)], axis=0)
        means = means.astype(BF16)
    else:
        means = means_refs[0][...]
    width = held_ref.shape[2]
    copies = []
    for chunk in range(CHUNKS):
        columns = pl.ds(chunk * width, width)
        held_ref[chunk] = dot(means, basis_ref[:, columns]).astype(BF16)
        copy = pltpu.make_async_copy(held_ref.at[chunk], out_hbm.at[:, columns], sems.at[chunk])
        copy.start()
        copies.append(copy)
    for copy in copies:
        copy.wait()


def core_swaps(blocks, hours, first, second):
    distances = [first, second] * (hours // 2)
    return [
        (t * hours + d, (t ^ distances[d]) * hours + d) for t in range(blocks) for d in range(hours)
    ]


def swaps(size, distance):
    return [(i, i ^ distance) for i in range(size)]


def body(obs_rows, obs_values, obs_hours, prior_precision, transition, site_basis):
    hours = lax.axis_size("site")
    blocks = lax.axis_size("tm")
    count, states = obs_rows.shape
    half = hours // 2
    pairs = half // 2
    sds = jax.ShapeDtypeStruct
    square = sds((states, states), F32)
    prior, turned, basis = call(
        prepare,
        (square, square, sds(site_basis.shape[::-1], BF16)),
        (prior_precision, transition, site_basis),
        "prepare",
        [
            pltpu.VMEM(transition.shape, F32),
            pltpu.VMEM(site_basis.shape, BF16),
            pltpu.SemaphoreType.DMA((3,)),
        ],
        in_hbm=True,
    )
    packed = sds((pairs, states + TAIL, states), F32)
    rounded = sds((pairs, states + 2 * TAIL, states), BF16)
    keep, send = call(
        functools.partial(local_grams, hours),
        (packed, rounded),
        (obs_rows, obs_values, obs_hours),
        "local_grams",
        [
            pltpu.VMEM(obs_rows.shape, BF16),
            pltpu.VMEM(obs_values.shape, BF16),
            pltpu.VMEM(obs_hours.shape, jnp.int32),
            pltpu.SemaphoreType.DMA((3,)),
        ],
        in_hbm=True,
    )
    received = lax.ppermute(send, "site", swaps(hours, 1))
    distance = 2
    while distance < hours:
        total, send = call(add_and_round, (packed, rounded), (keep, received), "add_and_round")
        received = lax.ppermute(send, "site", swaps(hours, distance))
        distance *= 2
        if distance < hours:
            keep = call(add_received, packed, (total, received), "add_received")
            received = jnp.zeros_like(received)
    rows = states + 16
    block = sds((rows, states), BF16)
    firsts = sds((half - 1, rows, states), BF16)
    own_last, own_firsts, last, first_maps = call(
        hour_maps,
        (sds((rows, states), F32), sds((half - 1, rows, states), F32), block, firsts),
        (total, received, prior, turned),
        "hour_maps",
    )
    other_last = lax.ppermute(own_last, "site", swaps(hours, 1))
    last = lax.ppermute(last, "tm", swaps(blocks, 1))
    first_maps = lax.ppermute(first_maps, "tm", swaps(blocks, 1))
    own = call(block_map, block, (own_last, other_last), "block_map")
    far = lax.ppermute(own, ("tm", "site"), core_swaps(blocks, hours, 2, 3))
    others_last = lax.ppermute(last, "site", swaps(hours, 1))
    others_far = lax.ppermute(far, "site", swaps(hours, 1))
    radix = 4
    *gathered, shift = call(
        group_blocks,
        (block,) * 3 + (sds((8, states), F32),),
        (own, last, far, others_last, others_far),
        "group_blocks",
    )
    gathered = (own, *gathered)
    distances, levels = [], []
    distance = radix
    if 2 * distance < blocks:
        joined = call(group_map, sds(own.shape, BF16), gathered, "group_map")
    while distance < blocks:
        if 2 * distance == blocks:
            if levels:
                shift = joined[states:].astype(F32).sum(axis=0, keepdims=True)
                shift = jnp.broadcast_to(shift, (8, states))
            received = lax.ppermute(shift, "tm", swaps(blocks, distance))
        else:
            received = lax.ppermute(joined, "tm", swaps(blocks, distance))
            joined = call(
                functools.partial(pair_map, distance),
                sds(own.shape, BF16),
                (joined, received),
                "pair_map",
            )
        distances.append(distance)
        levels.append(received)
        distance *= 2
    other_firsts = lax.ppermute(own_firsts, "site", swaps(hours, 1))
    means = call(
        functools.partial(pair_means, tuple(distances)),
        sds((2 * hours, states), F32),
        [own_last, other_last, own_firsts, other_firsts, last, others_last]
        + levels
        + list(gathered),
        "pair_means",
    )
    first_maps = call(hold, firsts, (first_maps, levels[-1]), "hold")
    other_firsts = lax.ppermute(first_maps, "site", swaps(hours, 1))
    means = call(
        rest_of_means,
        sds(means.shape, F32),
        (means, first_maps, other_firsts),
        "rest_of_means",
    )
    if blocks == 2 * radix:
        far = lax.ppermute(means, ("tm", "site"), core_swaps(blocks, hours, 4, 6))
        near = lax.ppermute(means, "tm", swaps(blocks, 2))
        other_far = lax.ppermute(far, "site", swaps(hours, 1))
        means = [means, near, far, other_far]
    else:
        means = call(own_means, sds((blocks, hours, states), BF16), (means,), "own_means")
        means = [lax.all_to_all(means, "tm", 0, 0, tiled=True).reshape(blocks * hours, states)]
    sites = site_basis.shape[0]
    return pl.pallas_call(
        predict,
        out_shape=sds((blocks * hours, sites), BF16),
        in_specs=[whole()] * (len(means) + 1),
        out_specs=pl.BlockSpec(memory_space=pltpu.HBM),
        scratch_shapes=[
            pltpu.VMEM((CHUNKS, blocks * hours, sites // CHUNKS), BF16),
            pltpu.SemaphoreType.DMA((CHUNKS,)),
        ],
        compiler_params=pltpu.CompilerParams(vmem_limit_bytes=VMEM_LIMIT),
        name="predict",
    )(*means, basis)


def solution(mesh):
    in_specs = (
        P(("tm", "site"), None),
        P(("tm", "site")),
        P(("tm", "site")),
        P(),
        P(),
        P(("tm", "site"), None),
    )
    out_specs = P(None, ("tm", "site"))
    return jax.shard_map(body, mesh=mesh, in_specs=in_specs, out_specs=out_specs, check_vma=False)
```

```python
import functools

import jax
import jax.numpy as jnp
from jax import lax
from jax.experimental import pallas as pl
from jax.experimental.pallas import tpu as pltpu
from jax.sharding import PartitionSpec as P

NS_ITERS = 8
TAIL = 8
CHUNKS = 4
BF16 = jnp.bfloat16
F32 = jnp.float32
VMEM_LIMIT = 40 * 2**20


def whole():
    return pl.BlockSpec(memory_space=pltpu.VMEM)


def call(kernel, outs, args, name, scratch=(), in_hbm=False):
    if in_hbm:
        args = [pltpu.with_memory_space_constraint(arg, pltpu.HBM) for arg in args]
    return pl.pallas_call(
        kernel,
        out_shape=outs,
        in_specs=[pl.BlockSpec(memory_space=pltpu.HBM) if in_hbm else whole()] * len(args),
        out_specs=jax.tree.map(lambda _: whole(), outs),
        scratch_shapes=scratch,
        compiler_params=pltpu.CompilerParams(vmem_limit_bytes=VMEM_LIMIT),
        name=name,
    )(*args)


def dot(a, b):
    return jnp.dot(a, b, preferred_element_type=F32)


def split(x):
    high = x.astype(BF16)
    return high, (x - high.astype(F32)).astype(BF16)


def dot_wide(a, b):
    a_high, a_low = split(a)
    b_high, b_low = split(b)
    return dot(
        jnp.concatenate([a_high, a_low, a_high], axis=1),
        jnp.concatenate([b_high, b_high, b_low], axis=0),
    )


def thirds(row):
    first = row.astype(BF16).astype(F32)
    second = (row - first).astype(BF16).astype(F32)
    third = row - first - second
    zeros = jnp.zeros((13, row.shape[1]), F32)
    return jnp.concatenate([first, second, third, zeros], axis=0).astype(BF16)


def row_times(row, *weights):
    rows = thirds(row)
    total = dot(rows, weights[0])
    for w in weights[1:]:
        total += dot(rows, w)
    return jnp.sum(total, axis=0, keepdims=True)


def own_half(hours):
    return lax.rem(lax.axis_index("site"), 2) * (hours // 2)


def local_grams(
    hours,
    rows_hbm,
    values_hbm,
    codes_hbm,
    keep_ref,
    send_ref,
    rows_ref,
    values_ref,
    codes_ref,
    sems,
):
    half = hours // 2
    states = rows_hbm.shape[1]
    start = own_half(hours)
    copies = [
        pltpu.make_async_copy(rows_hbm, rows_ref, sems.at[0]),
        pltpu.make_async_copy(values_hbm, values_ref, sems.at[1]),
        pltpu.make_async_copy(codes_hbm, codes_ref, sems.at[2]),
    ]
    for copy in copies:
        copy.start()
    for copy in copies:
        copy.wait()
    rows = rows_ref[...]
    turned = rows.T
    codes = codes_ref[...].reshape(1, rows.shape[0])
    values = values_ref[...].astype(F32).reshape(1, rows.shape[0])
    slots = []
    for slot in range(hours):
        hour = lax.rem(start + slot, hours)
        slots.append((codes == hour).astype(F32))
    masked = jnp.concatenate([turned * s.astype(BF16) for s in slots], axis=0)
    grams = dot(masked, rows)
    weighted = jnp.concatenate([s * values for s in slots], axis=0)
    pad = jnp.zeros((16 - hours, weighted.shape[1]), F32)
    drives = dot(jnp.concatenate([weighted, pad], axis=0).astype(BF16), rows)
    row_id = lax.broadcasted_iota(jnp.int32, (states, states), 0)
    column_id = lax.broadcasted_iota(jnp.int32, (states, states), 1)
    for base in (0, half):
        for pair in range(half // 2):
            first = base + 2 * pair
            a = grams[first * states : (first + 1) * states]
            b = grams[(first + 1) * states : (first + 2) * states]
            diagonals = [
                jnp.sum(jnp.where(row_id == column_id, gram, 0.0), axis=0, keepdims=True)
                for gram in (a, b)
            ]
            square = jnp.where(row_id <= column_id, a, b)
            tail = jnp.concatenate(
                diagonals + [drives[first : first + 2], jnp.zeros((TAIL - 4, states), F32)], axis=0
            )
            if base == 0:
                keep_ref[pair, :states, :] = square
                keep_ref[pair, states:, :] = tail
            else:
                store_rounded(send_ref, pair, square, tail)


def prepare(
    prior_hbm,
    transition_hbm,
    basis_hbm,
    prior_out_ref,
    turned_ref,
    basis_out_ref,
    transition_ref,
    basis_ref,
    sems,
):
    copies = [
        pltpu.make_async_copy(prior_hbm, prior_out_ref, sems.at[0]),
        pltpu.make_async_copy(transition_hbm, transition_ref, sems.at[1]),
        pltpu.make_async_copy(basis_hbm, basis_ref, sems.at[2]),
    ]
    for copy in copies:
        copy.start()
    copies[0].wait()
    copies[1].wait()
    prior = prior_out_ref[...]
    turned_ref[...] = dot_wide(transition_ref[...].T, prior)
    copies[2].wait()
    basis_out_ref[...] = basis_ref[...].T


def add_and_round(keep_ref, received_ref, sum_ref, send_ref):
    states = keep_ref.shape[2]
    for pair in range(keep_ref.shape[0]):
        total = sum_of(keep_ref, received_ref, pair, states)
        sum_ref[pair] = total
        store_rounded(send_ref, pair, total[:states], total[states:])


def store_rounded(out_ref, pair, square, tail):
    states = square.shape[1]
    out_ref[pair, :states, :] = square.astype(BF16)
    high = tail.astype(BF16).astype(F32)
    out_ref[pair, states:, :] = jnp.concatenate([high, tail - high], axis=0).astype(BF16)


def add_received(sum_ref, received_ref, out_ref):
    states = sum_ref.shape[2]
    for pair in range(sum_ref.shape[0]):
        out_ref[pair] = sum_of(sum_ref, received_ref, pair, states)


def sum_of(sum_ref, received_ref, pair, states):
    received = received_ref[pair].astype(F32)
    tail = received[states : states + TAIL] + received[states + TAIL :]
    return sum_ref[pair] + jnp.concatenate([received[:states], tail], axis=0)


def times_own(z):
    states = z.shape[1]
    high, low = split(z)
    d_high, d_low = high[:states], low[:states]
    mixed = dot(d_high, d_low)
    square = dot(d_high, d_high) + (mixed + mixed.T)
    rest = dot(
        jnp.concatenate([high[states:], low[states:], high[states:]], axis=1),
        jnp.concatenate([d_high, d_high, d_low], axis=0),
    )
    return jnp.concatenate([square, rest], axis=0)


def hour_maps(
    sum_ref,
    received_ref,
    prior_ref,
    turned_ref,
    last_ref,
    firsts_ref,
    rounded_last_ref,
    rounded_firsts_ref,
):
    states = prior_ref.shape[0]
    prior = prior_ref[...]
    turned = turned_ref[...]
    row_id = lax.broadcasted_iota(jnp.int32, (states, states), 0)
    column_id = lax.broadcasted_iota(jnp.int32, (states, states), 1)
    running = []
    for pair in range(sum_ref.shape[0]):
        total = sum_of(sum_ref, received_ref, pair, states)
        square = total[:states]
        flipped = square.T
        upper, lower = row_id <= column_id, row_id > column_id
        grams = (jnp.where(upper, square, flipped), jnp.where(lower, square, flipped))
        for place, gram in enumerate(grams):
            diagonal, drive = [total[states + i : states + i + 1] for i in (place, place + 2)]
            gram = jnp.where(row_id == column_id, diagonal, gram)
            precision = prior + gram
            bound = jnp.max(jnp.sum(jnp.abs(precision), axis=0, keepdims=True), axis=1, keepdims=True)
            scale = 1.0 / bound
            offset = jnp.concatenate([drive, jnp.zeros((15, states), F32)], axis=0)
            running.append((precision * scale, turned * scale, offset * scale))
    stacked = [jnp.concatenate(parts, axis=0) for parts in running]

    for _ in range(NS_ITERS - 2):
        stacked = [2.0 * z - times_own(z) for z in stacked]
    maps = []
    for z in stacked:
        power = (jnp.where(row_id == column_id, 1.0, 0.0) - z[:states]).astype(BF16)
        v = z[states:]
        product = dot(jnp.concatenate([power, v.astype(BF16)], axis=0), power)
        v = v + product[states:]
        maps.append(v + dot(v.astype(BF16), product[:states].astype(BF16)))
    for position in range(len(maps)):
        joined = maps[0] if position == 0 else append(joined, maps[position])
        if position < len(maps) - 1:
            firsts_ref[position] = joined
            rounded_firsts_ref[position] = rounded(joined)
    last_ref[...] = joined
    rounded_last_ref[...] = rounded(joined)


def rounded(affine):
    states = affine.shape[1]
    return jnp.concatenate([affine[:states].astype(BF16), thirds(affine[states : states + 1])], axis=0)


def append(earlier, latter):
    states = latter.shape[1]
    product = dot_wide(earlier, latter[:states])
    return jnp.concatenate([product[:states], product[states:] + latter[states:]], axis=0)


def in_order(own_ref, received_ref):
    first = lax.rem(lax.axis_index("site"), 2) == 0
    count = len(own_ref) if isinstance(own_ref, list) else own_ref.shape[0]
    early = [jnp.where(first, own_ref[i], received_ref[i]) for i in range(count)]
    late = [jnp.where(first, received_ref[i], own_ref[i]) for i in range(count)]
    return early, late


def block_map(own_ref, received_ref, out_ref):
    (early,), (late,) = in_order([own_ref[...]], [received_ref[...]])
    out_ref[...] = rounded(append(early, late))


def group_blocks(own_ref, last_ref, far_ref, other_last_ref, other_far_ref, *out_refs):
    shift_ref, out_refs = out_refs[-1], out_refs[:-1]
    (early,), (late,) = in_order([last_ref[...]], [other_last_ref[...]])
    out_refs[0][...] = follow(early, late)
    (near,), (far,) = in_order([far_ref[...]], [other_far_ref[...]])
    out_refs[1][...] = near
    out_refs[2][...] = far
    group_shift(own_ref, *out_refs, shift_ref)


def shift_of(block):
    states = block.shape[1]
    return jnp.sum(block[states:].astype(F32), axis=0, keepdims=True)


def choose(values, slot):
    value = values[0]
    for i in range(1, len(values)):
        value = jnp.where(slot == i, values[i], value)
    return value


def pick(refs, slot):
    return choose([ref[...] for ref in refs], slot)


def apply(block, mean):
    return row_times(mean, block[: block.shape[1]]) + shift_of(block)


def follow(earlier, latter):
    states = latter.shape[1]
    product = dot(earlier[:states], latter[:states]).astype(BF16)
    return jnp.concatenate([product, thirds(apply(latter, shift_of(earlier)))], axis=0)


def group_shift(*refs):
    gathered, out_ref = refs[:-1], refs[-1]
    place = lax.rem(lax.axis_index("tm"), len(gathered))
    mean = shift_of(pick(gathered, place))
    for i in range(1, len(gathered)):
        mean = apply(pick(gathered, place ^ i), mean)
    out_ref[...] = jnp.broadcast_to(mean, out_ref.shape)


def group_map(*refs):
    gathered, out_ref = refs[:-1], refs[-1]
    place = lax.rem(lax.axis_index("tm"), len(gathered))
    joined = pick(gathered, place)
    for i in range(1, len(gathered)):
        joined = follow(joined, pick(gathered, place ^ i))
    out_ref[...] = joined


def pair_map(distance, own_ref, received_ref, out_ref):
    upper = is_upper(distance)
    first = jnp.where(upper, received_ref[...], own_ref[...])
    second = jnp.where(upper, own_ref[...], received_ref[...])
    out_ref[...] = follow(first, second)


def is_upper(distance):
    return lax.rem(lax.axis_index("tm") // distance, 2) == 1


def hold(maps_ref, received_ref, out_ref):
    out_ref[...] = maps_ref[...]


def pair_means(distances, *refs):
    out_ref = refs[-1]
    own_last_ref, own_other_ref, own_firsts_ref, other_firsts_ref, last_ref, other_last_ref = refs[:6]
    levels, gathered = refs[6 : 6 + len(distances)], refs[6 + len(distances) : -1]
    rows, states = own_last_ref.shape
    half = own_firsts_ref.shape[0] + 1
    mean = jnp.zeros((1, states), F32)
    for level in reversed(range(len(distances))):
        if level == len(distances) - 1:
            entered = levels[level][0:1, :]
        else:
            entered = apply(levels[level][...], mean)
        mean = jnp.where(is_upper(distances[level]), entered, mean)
    place = lax.rem(lax.axis_index("tm"), len(gathered))
    for i in range(2):
        mean = jnp.where(place >= 2, apply(pick(gathered, place ^ i), mean), mean)
    odd = lax.rem(place, 2) == 1
    between = apply(pick(gathered, place & 1), mean)
    own_start = jnp.where(odd, between, mean)
    own = []
    sides = [
        [firsts[i] for i in range(half - 1)] + [last[...]]
        for firsts, last in ((own_firsts_ref, own_last_ref), (other_firsts_ref, own_other_ref))
    ]
    for maps in in_order(*sides):
        start = own_start if not own else own[-1]
        for each in maps:
            own.append(row_times(start, *split(each[:states])) + each[states : states + 1])
    state = jnp.where(odd, mean, own[-1])
    partner = []
    for maps in in_order([last_ref[...]], [other_last_ref[...]]):
        partner += [state] * (half - 1)
        state = apply(maps[0], state)
        partner.append(state)
    own, partner = jnp.concatenate(own, axis=0), jnp.concatenate(partner, axis=0)
    out_ref[: 2 * half, :] = jnp.where(odd, partner, own)
    out_ref[2 * half :, :] = jnp.where(odd, own, partner)


def rest_of_means(means_ref, firsts_ref, other_ref, out_ref):
    count = firsts_ref.shape[0]
    hours = 2 * (count + 1)
    odd = lax.rem(lax.axis_index("tm"), 2) == 1
    out_ref[...] = means_ref[...]
    partner = jnp.where(odd, means_ref[:hours, :], means_ref[hours:, :])
    for side, maps in enumerate(in_order(firsts_ref, other_ref)):
        for i in range(count):
            hour = side * (count + 1) + i
            mean = apply(maps[i], partner[hour : hour + 1])
            out_ref[pl.ds(jnp.where(odd, hour, hours + hour), 1), :] = mean


def own_means(means_ref, out_ref):
    hours = out_ref.shape[1]
    odd = lax.rem(lax.axis_index("tm"), 2) == 1
    means = jnp.where(odd, means_ref[hours:, :], means_ref[:hours, :]).astype(BF16)
    for copy in range(out_ref.shape[0]):
        out_ref[copy] = means


def predict(*refs):
    means_refs, basis_ref, out_hbm, held_ref, sems = refs[:-4], *refs[-4:]
    if len(means_refs) > 1:
        place = lax.axis_index("tm") // 2
        own, near, far, other_far = [ref[...] for ref in means_refs]
        (third,), (fourth,) = in_order([far], [other_far])
        by_distance = [own, near, third, fourth]
        means = jnp.concatenate([choose(by_distance, place ^ i) for i in range(4)], axis=0)
        means = means.astype(BF16)
    else:
        means = means_refs[0][...]
    width = held_ref.shape[2]
    copies = []
    for chunk in range(CHUNKS):
        columns = pl.ds(chunk * width, width)
        held_ref[chunk] = dot(means, basis_ref[:, columns]).astype(BF16)
        copy = pltpu.make_async_copy(held_ref.at[chunk], out_hbm.at[:, columns], sems.at[chunk])
        copy.start()
        copies.append(copy)
    for copy in copies:
        copy.wait()


def core_swaps(blocks, hours, first, second):
    distances = [first, second] * (hours // 2)
    return [
        (t * hours + d, (t ^ distances[d]) * hours + d) for t in range(blocks) for d in range(hours)
    ]


def swaps(size, distance):
    return [(i, i ^ distance) for i in range(size)]


def body(obs_rows, obs_values, obs_hours, prior_precision, transition, site_basis):
    hours = lax.axis_size("site")
    blocks = lax.axis_size("tm")
    count, states = obs_rows.shape
    half = hours // 2
    pairs = half // 2
    sds = jax.ShapeDtypeStruct
    square = sds((states, states), F32)
    prior, turned, basis = call(
        prepare,
        (square, square, sds(site_basis.shape[::-1], BF16)),
        (prior_precision, transition, site_basis),
        "prepare",
        [
            pltpu.VMEM(transition.shape, F32),
            pltpu.VMEM(site_basis.shape, BF16),
            pltpu.SemaphoreType.DMA((3,)),
        ],
        in_hbm=True,
    )
    packed = sds((pairs, states + TAIL, states), F32)
    rounded = sds((pairs, states + 2 * TAIL, states), BF16)
    keep, send = call(
        functools.partial(local_grams, hours),
        (packed, rounded),
        (obs_rows, obs_values, obs_hours),
        "local_grams",
        [
            pltpu.VMEM(obs_rows.shape, BF16),
            pltpu.VMEM(obs_values.shape, BF16),
            pltpu.VMEM(obs_hours.shape, jnp.int32),
            pltpu.SemaphoreType.DMA((3,)),
        ],
        in_hbm=True,
    )
    received = lax.ppermute(send, "site", swaps(hours, 1))
    distance = 2
    while distance < hours:
        total, send = call(add_and_round, (packed, rounded), (keep, received), "add_and_round")
        received = lax.ppermute(send, "site", swaps(hours, distance))
        distance *= 2
        if distance < hours:
            keep = call(add_received, packed, (total, received), "add_received")
            received = jnp.zeros_like(received)
    rows = states + 16
    block = sds((rows, states), BF16)
    firsts = sds((half - 1, rows, states), BF16)
    own_last, own_firsts, last, first_maps = call(
        hour_maps,
        (sds((rows, states), F32), sds((half - 1, rows, states), F32), block, firsts),
        (total, received, prior, turned),
        "hour_maps",
    )
    other_last = lax.ppermute(own_last, "site", swaps(hours, 1))
    last = lax.ppermute(last, "tm", swaps(blocks, 1))
    first_maps = lax.ppermute(first_maps, "tm", swaps(blocks, 1))
    own = call(block_map, block, (own_last, other_last), "block_map")
    far = lax.ppermute(own, ("tm", "site"), core_swaps(blocks, hours, 2, 3))
    others_last = lax.ppermute(last, "site", swaps(hours, 1))
    others_far = lax.ppermute(far, "site", swaps(hours, 1))
    radix = 4
    *gathered, shift = call(
        group_blocks,
        (block,) * 3 + (sds((8, states), F32),),
        (own, last, far, others_last, others_far),
        "group_blocks",
    )
    gathered = (own, *gathered)
    distances, levels = [], []
    distance = radix
    if 2 * distance < blocks:
        joined = call(group_map, sds(own.shape, BF16), gathered, "group_map")
    while distance < blocks:
        if 2 * distance == blocks:
            if levels:
                shift = joined[states:].astype(F32).sum(axis=0, keepdims=True)
                shift = jnp.broadcast_to(shift, (8, states))
            received = lax.ppermute(shift, "tm", swaps(blocks, distance))
        else:
            received = lax.ppermute(joined, "tm", swaps(blocks, distance))
            joined = call(
                functools.partial(pair_map, distance),
                sds(own.shape, BF16),
                (joined, received),
                "pair_map",
            )
        distances.append(distance)
        levels.append(received)
        distance *= 2
    other_firsts = lax.ppermute(own_firsts, "site", swaps(hours, 1))
    means = call(
        functools.partial(pair_means, tuple(distances)),
        sds((2 * hours, states), F32),
        [own_last, other_last, own_firsts, other_firsts, last, others_last]
        + levels
        + list(gathered),
        "pair_means",
    )
    first_maps = call(hold, firsts, (first_maps, levels[-1]), "hold")
    other_firsts = lax.ppermute(first_maps, "site", swaps(hours, 1))
    means = call(
        rest_of_means,
        sds(means.shape, F32),
        (means, first_maps, other_firsts),
        "rest_of_means",
    )
    if blocks == 2 * radix:
        far = lax.ppermute(means, ("tm", "site"), core_swaps(blocks, hours, 4, 6))
        near = lax.ppermute(means, "tm", swaps(blocks, 2))
        other_far = lax.ppermute(far, "site", swaps(hours, 1))
        means = [means, near, far, other_far]
    else:
        means = call(own_means, sds((blocks, hours, states), BF16), (means,), "own_means")
        means = [lax.all_to_all(means, "tm", 0, 0, tiled=True).reshape(blocks * hours, states)]
    sites = site_basis.shape[0]
    return pl.pallas_call(
        predict,
        out_shape=sds((blocks * hours, sites), BF16),
        in_specs=[whole()] * (len(means) + 1),
        out_specs=pl.BlockSpec(memory_space=pltpu.HBM),
        scratch_shapes=[
            pltpu.VMEM((CHUNKS, blocks * hours, sites // CHUNKS), BF16),
            pltpu.SemaphoreType.DMA((CHUNKS,)),
        ],
        compiler_params=pltpu.CompilerParams(vmem_limit_bytes=VMEM_LIMIT),
        name="predict",
    )(*means, basis)


def solution(mesh):
    in_specs = (
        P(("tm", "site"), None),
        P(("tm", "site")),
        P(("tm", "site")),
        P(),
        P(),
        P(("tm", "site"), None),
    )
    out_specs = P(None, ("tm", "site"))
    return jax.shard_map(body, mesh=mesh, in_specs=in_specs, out_specs=out_specs, check_vma=False)
```

```python
import functools

import jax
import jax.numpy as jnp
from jax import lax
from jax.experimental import pallas as pl
from jax.experimental.pallas import tpu as pltpu
from jax.sharding import PartitionSpec as P

NS_ITERS = 8
TAIL = 8
CHUNKS = 4
BF16 = jnp.bfloat16
F32 = jnp.float32
VMEM_LIMIT = 40 * 2**20
COSTS = {
    "pair_block": pl.CostEstimate(flops=3000000000, bytes_accessed=0, transcendentals=0),
}


def whole():
    return pl.BlockSpec(memory_space=pltpu.VMEM)


def call(kernel, outs, args, name, scratch=(), in_hbm=False):
    if in_hbm:
        args = [pltpu.with_memory_space_constraint(arg, pltpu.HBM) for arg in args]
    return pl.pallas_call(
        kernel,
        out_shape=outs,
        in_specs=[pl.BlockSpec(memory_space=pltpu.HBM) if in_hbm else whole()] * len(args),
        out_specs=jax.tree.map(lambda _: whole(), outs),
        scratch_shapes=scratch,
        compiler_params=pltpu.CompilerParams(vmem_limit_bytes=VMEM_LIMIT),
        cost_estimate=COSTS.get(name),
        name=name,
    )(*args)


def dot(a, b):
    return jnp.dot(a, b, preferred_element_type=F32)


def split(x):
    high = x.astype(BF16)
    return high, (x - high.astype(F32)).astype(BF16)


def dot_wide(a, b):
    a_high, a_low = split(a)
    b_high, b_low = split(b)
    return dot(
        jnp.concatenate([a_high, a_low, a_high], axis=1),
        jnp.concatenate([b_high, b_high, b_low], axis=0),
    )


def thirds(row):
    first = row.astype(BF16).astype(F32)
    second = (row - first).astype(BF16).astype(F32)
    third = row - first - second
    zeros = jnp.zeros((13, row.shape[1]), F32)
    return jnp.concatenate([first, second, third, zeros], axis=0).astype(BF16)


def row_times(row, *weights):
    rows = thirds(row)
    total = dot(rows, weights[0])
    for w in weights[1:]:
        total += dot(rows, w)
    return jnp.sum(total, axis=0, keepdims=True)


def own_half(hours):
    return lax.rem(lax.axis_index("site"), 2) * (hours // 2)


def local_grams(
    hours,
    rows_hbm,
    values_hbm,
    codes_hbm,
    keep_ref,
    send_ref,
    rows_ref,
    values_ref,
    codes_ref,
    sems,
):
    half = hours // 2
    states = rows_hbm.shape[1]
    start = own_half(hours)
    copies = [
        pltpu.make_async_copy(rows_hbm, rows_ref, sems.at[0]),
        pltpu.make_async_copy(values_hbm, values_ref, sems.at[1]),
        pltpu.make_async_copy(codes_hbm, codes_ref, sems.at[2]),
    ]
    for copy in copies:
        copy.start()
    for copy in copies:
        copy.wait()
    rows = rows_ref[...]
    turned = rows.T
    codes = codes_ref[...].reshape(1, rows.shape[0])
    values = values_ref[...].astype(F32).reshape(1, rows.shape[0])
    slots = []
    for slot in range(hours):
        hour = lax.rem(start + slot, hours)
        slots.append((codes == hour).astype(F32))
    masked = jnp.concatenate([turned * s.astype(BF16) for s in slots], axis=0)
    grams = dot(masked, rows)
    weighted = jnp.concatenate([s * values for s in slots], axis=0)
    pad = jnp.zeros((16 - hours, weighted.shape[1]), F32)
    drives = dot(jnp.concatenate([weighted, pad], axis=0).astype(BF16), rows)
    row_id = lax.broadcasted_iota(jnp.int32, (states, states), 0)
    column_id = lax.broadcasted_iota(jnp.int32, (states, states), 1)
    for base in (0, half):
        for pair in range(half // 2):
            first = base + 2 * pair
            a = grams[first * states : (first + 1) * states]
            b = grams[(first + 1) * states : (first + 2) * states]
            diagonals = [
                jnp.sum(jnp.where(row_id == column_id, gram, 0.0), axis=0, keepdims=True)
                for gram in (a, b)
            ]
            square = jnp.where(row_id <= column_id, a, b)
            tail = jnp.concatenate(
                diagonals + [drives[first : first + 2], jnp.zeros((TAIL - 4, states), F32)], axis=0
            )
            if base == 0:
                keep_ref[pair, :states, :] = square
                keep_ref[pair, states:, :] = tail
            else:
                store_rounded(send_ref, pair, square, tail)


def prepare(
    prior_hbm,
    transition_hbm,
    basis_hbm,
    prior_out_ref,
    turned_ref,
    basis_out_ref,
    transition_ref,
    basis_ref,
    sems,
):
    copies = [
        pltpu.make_async_copy(prior_hbm, prior_out_ref, sems.at[0]),
        pltpu.make_async_copy(transition_hbm, transition_ref, sems.at[1]),
        pltpu.make_async_copy(basis_hbm, basis_ref, sems.at[2]),
    ]
    for copy in copies:
        copy.start()
    copies[0].wait()
    copies[1].wait()
    prior = prior_out_ref[...]
    turned_ref[...] = dot_wide(transition_ref[...].T, prior)
    copies[2].wait()
    basis_out_ref[...] = basis_ref[...].T


def add_and_round(keep_ref, received_ref, sum_ref, send_ref):
    states = keep_ref.shape[2]
    for pair in range(keep_ref.shape[0]):
        total = sum_of(keep_ref, received_ref, pair, states)
        sum_ref[pair] = total
        store_rounded(send_ref, pair, total[:states], total[states:])


def store_rounded(out_ref, pair, square, tail):
    states = square.shape[1]
    out_ref[pair, :states, :] = square.astype(BF16)
    high = tail.astype(BF16).astype(F32)
    out_ref[pair, states:, :] = jnp.concatenate([high, tail - high], axis=0).astype(BF16)


def add_received(sum_ref, received_ref, out_ref):
    states = sum_ref.shape[2]
    for pair in range(sum_ref.shape[0]):
        out_ref[pair] = sum_of(sum_ref, received_ref, pair, states)


def sum_of(sum_ref, received_ref, pair, states):
    received = received_ref[pair].astype(F32)
    tail = received[states : states + TAIL] + received[states + TAIL :]
    return sum_ref[pair] + jnp.concatenate([received[:states], tail], axis=0)


def times_own(z):
    states = z.shape[1]
    high, low = split(z)
    d_high, d_low = high[:states], low[:states]
    mixed = dot(d_high, d_low)
    square = dot(d_high, d_high) + (mixed + mixed.T)
    rest = dot(
        jnp.concatenate([high[states:], low[states:], high[states:]], axis=1),
        jnp.concatenate([d_high, d_high, d_low], axis=0),
    )
    return jnp.concatenate([square, rest], axis=0)


def hour_maps(
    sum_ref,
    received_ref,
    prior_ref,
    turned_ref,
    last_ref,
    firsts_ref,
    rounded_last_ref,
    rounded_firsts_ref,
):
    states = prior_ref.shape[0]
    prior = prior_ref[...]
    turned = turned_ref[...]
    row_id = lax.broadcasted_iota(jnp.int32, (states, states), 0)
    column_id = lax.broadcasted_iota(jnp.int32, (states, states), 1)
    running = []
    for pair in range(sum_ref.shape[0]):
        total = sum_of(sum_ref, received_ref, pair, states)
        square = total[:states]
        flipped = square.T
        upper, lower = row_id <= column_id, row_id > column_id
        grams = (jnp.where(upper, square, flipped), jnp.where(lower, square, flipped))
        for place, gram in enumerate(grams):
            diagonal, drive = [total[states + i : states + i + 1] for i in (place, place + 2)]
            gram = jnp.where(row_id == column_id, diagonal, gram)
            precision = prior + gram
            bound = jnp.max(jnp.sum(jnp.abs(precision), axis=0, keepdims=True), axis=1, keepdims=True)
            scale = 1.0 / bound
            offset = jnp.concatenate([drive, jnp.zeros((15, states), F32)], axis=0)
            running.append((precision * scale, turned * scale, offset * scale))
    stacked = [jnp.concatenate(parts, axis=0) for parts in running]

    for _ in range(NS_ITERS - 2):
        stacked = [2.0 * z - times_own(z) for z in stacked]
    maps = []
    for z in stacked:
        power = (jnp.where(row_id == column_id, 1.0, 0.0) - z[:states]).astype(BF16)
        v = z[states:]
        product = dot(jnp.concatenate([power, v.astype(BF16)], axis=0), power)
        v = v + product[states:]
        maps.append(v + dot(v.astype(BF16), product[:states].astype(BF16)))
    for position in range(len(maps)):
        joined = maps[0] if position == 0 else append(joined, maps[position])
        if position < len(maps) - 1:
            firsts_ref[position] = joined
            rounded_firsts_ref[position] = rounded(joined)
    last_ref[...] = joined
    rounded_last_ref[...] = rounded(joined)


def rounded(affine):
    states = affine.shape[1]
    return jnp.concatenate([affine[:states].astype(BF16), thirds(affine[states : states + 1])], axis=0)


def append(earlier, latter):
    states = latter.shape[1]
    product = dot_wide(earlier, latter[:states])
    return jnp.concatenate([product[:states], product[states:] + latter[states:]], axis=0)


def in_order(own_ref, received_ref):
    first = lax.rem(lax.axis_index("site"), 2) == 0
    count = len(own_ref) if isinstance(own_ref, list) else own_ref.shape[0]
    early = [jnp.where(first, own_ref[i], received_ref[i]) for i in range(count)]
    late = [jnp.where(first, received_ref[i], own_ref[i]) for i in range(count)]
    return early, late


def block_map(own_ref, received_ref, out_ref):
    (early,), (late,) = in_order([own_ref[...]], [received_ref[...]])
    out_ref[...] = rounded(append(early, late))


def pair_block(own_ref, last_ref, other_last_ref, next_ref, pair_ref):
    (early,), (late,) = in_order([last_ref[...]], [other_last_ref[...]])
    own, following = own_ref[...], follow(early, late)
    next_ref[...] = following
    odd = lax.rem(lax.axis_index("tm"), 2) == 1
    first, second = jnp.where(odd, following, own), jnp.where(odd, own, following)
    states = own.shape[1]
    pair_ref[:states, :] = dot(first[:states], second[:states])
    pair_ref[states:, :] = jnp.broadcast_to(apply(second, shift_of(first)), (8, states))


def group_blocks(own_ref, next_ref, pair_ref, far_ref, other_far_ref, out_ref, shift_ref):
    (near,), (far,) = in_order([far_ref[...]], [other_far_ref[...]])
    out_ref[0] = own_ref[...]
    out_ref[1] = next_ref[...]
    out_ref[2] = near
    out_ref[3] = far
    states = near.shape[1]
    place = lax.rem(lax.axis_index("tm"), out_ref.shape[0])
    odd, upper = lax.rem(place, 2) == 1, place >= 2
    first, second = jnp.where(odd, far, near), jnp.where(odd, near, far)
    pair = pair_ref[:states, :]
    pair_shift = pair_ref[states : states + 1, :]
    high, low = split(pair)
    mean = jnp.where(upper, shift_of(first), pair_shift)
    mean = apply(jnp.where(upper, second, first), mean)
    high = jnp.where(upper, high, second[:states])
    low = jnp.where(upper, low, jnp.zeros_like(low))
    mean = row_times(mean, high, low) + jnp.where(upper, pair_shift, shift_of(second))
    shift_ref[...] = jnp.broadcast_to(mean, shift_ref.shape)


def shift_of(block):
    states = block.shape[1]
    return jnp.sum(block[states:].astype(F32), axis=0, keepdims=True)


def choose(values, slot):
    value = values[0]
    for i in range(1, len(values)):
        value = jnp.where(slot == i, values[i], value)
    return value


def apply(block, mean):
    return row_times(mean, block[: block.shape[1]]) + shift_of(block)


def follow(earlier, latter):
    states = latter.shape[1]
    product = dot(earlier[:states], latter[:states]).astype(BF16)
    return jnp.concatenate([product, thirds(apply(latter, shift_of(earlier)))], axis=0)


def group_map(gathered_ref, out_ref):
    place = lax.rem(lax.axis_index("tm"), gathered_ref.shape[0])
    joined = gathered_ref[place]
    for i in range(1, gathered_ref.shape[0]):
        joined = follow(joined, gathered_ref[place ^ i])
    out_ref[...] = joined


def pair_map(distance, own_ref, received_ref, out_ref):
    upper = is_upper(distance)
    first = jnp.where(upper, received_ref[...], own_ref[...])
    second = jnp.where(upper, own_ref[...], received_ref[...])
    out_ref[...] = follow(first, second)


def is_upper(distance):
    return lax.rem(lax.axis_index("tm") // distance, 2) == 1


def hold(maps_ref, received_ref, out_ref):
    out_ref[...] = maps_ref[...]


def pair_means(distances, *refs):
    out_ref = refs[-1]
    own_last_ref, own_other_ref, own_firsts_ref, other_firsts_ref, last_ref, other_last_ref = refs[:6]
    levels, gathered_ref = refs[6:-2], refs[-2]
    rows, states = own_last_ref.shape
    half = own_firsts_ref.shape[0] + 1
    mean = jnp.zeros((1, states), F32)
    for level in reversed(range(len(distances))):
        if level == len(distances) - 1:
            entered = levels[level][0:1, :]
        else:
            entered = apply(levels[level][...], mean)
        mean = jnp.where(is_upper(distances[level]), entered, mean)
    place = lax.rem(lax.axis_index("tm"), gathered_ref.shape[0])
    for i in range(2):
        mean = jnp.where(place >= 2, apply(gathered_ref[place ^ i], mean), mean)
    odd = lax.rem(place, 2) == 1
    between = apply(gathered_ref[place & 1], mean)
    own_start = jnp.where(odd, between, mean)
    own = []
    sides = [
        [firsts[i] for i in range(half - 1)] + [last[...]]
        for firsts, last in ((own_firsts_ref, own_last_ref), (other_firsts_ref, own_other_ref))
    ]
    for maps in in_order(*sides):
        start = own_start if not own else own[-1]
        for each in maps:
            own.append(row_times(start, *split(each[:states])) + each[states : states + 1])
    state = jnp.where(odd, mean, own[-1])
    partner = []
    for maps in in_order([last_ref[...]], [other_last_ref[...]]):
        partner += [state] * (half - 1)
        state = apply(maps[0], state)
        partner.append(state)
    own, partner = jnp.concatenate(own, axis=0), jnp.concatenate(partner, axis=0)
    out_ref[: 2 * half, :] = jnp.where(odd, partner, own)
    out_ref[2 * half :, :] = jnp.where(odd, own, partner)


def rest_of_means(means_ref, firsts_ref, other_ref, out_ref):
    count = firsts_ref.shape[0]
    hours = 2 * (count + 1)
    odd = lax.rem(lax.axis_index("tm"), 2) == 1
    out_ref[...] = means_ref[...]
    partner = jnp.where(odd, means_ref[:hours, :], means_ref[hours:, :])
    for side, maps in enumerate(in_order(firsts_ref, other_ref)):
        for i in range(count):
            hour = side * (count + 1) + i
            mean = apply(maps[i], partner[hour : hour + 1])
            out_ref[pl.ds(jnp.where(odd, hour, hours + hour), 1), :] = mean


def own_means(means_ref, out_ref):
    hours = out_ref.shape[1]
    odd = lax.rem(lax.axis_index("tm"), 2) == 1
    means = jnp.where(odd, means_ref[hours:, :], means_ref[:hours, :]).astype(BF16)
    for copy in range(out_ref.shape[0]):
        out_ref[copy] = means


def predict(*refs):
    means_refs, basis_ref, out_hbm, held_ref, sems = refs[:-4], *refs[-4:]
    if len(means_refs) > 1:
        place = lax.axis_index("tm") // 2
        own, near, far, other_far = [ref[...] for ref in means_refs]
        (third,), (fourth,) = in_order([far], [other_far])
        by_distance = [own, near, third, fourth]
        means = jnp.concatenate([choose(by_distance, place ^ i) for i in range(4)], axis=0)
        means = means.astype(BF16)
    else:
        means = means_refs[0][...]
    width = held_ref.shape[2]
    copies = []
    for chunk in range(CHUNKS):
        columns = pl.ds(chunk * width, width)
        held_ref[chunk] = dot(means, basis_ref[:, columns]).astype(BF16)
        copy = pltpu.make_async_copy(held_ref.at[chunk], out_hbm.at[:, columns], sems.at[chunk])
        copy.start()
        copies.append(copy)
    for copy in copies:
        copy.wait()


def core_swaps(blocks, hours, first, second):
    distances = [first, second] * (hours // 2)
    return [
        (t * hours + d, (t ^ distances[d]) * hours + d) for t in range(blocks) for d in range(hours)
    ]


def swaps(size, distance):
    return [(i, i ^ distance) for i in range(size)]


def body(obs_rows, obs_values, obs_hours, prior_precision, transition, site_basis):
    hours = lax.axis_size("site")
    blocks = lax.axis_size("tm")
    count, states = obs_rows.shape
    half = hours // 2
    pairs = half // 2
    sds = jax.ShapeDtypeStruct
    square = sds((states, states), F32)
    prior, turned, basis = call(
        prepare,
        (square, square, sds(site_basis.shape[::-1], BF16)),
        (prior_precision, transition, site_basis),
        "prepare",
        [
            pltpu.VMEM(transition.shape, F32),
            pltpu.VMEM(site_basis.shape, BF16),
            pltpu.SemaphoreType.DMA((3,)),
        ],
        in_hbm=True,
    )
    packed = sds((pairs, states + TAIL, states), F32)
    rounded = sds((pairs, states + 2 * TAIL, states), BF16)
    keep, send = call(
        functools.partial(local_grams, hours),
        (packed, rounded),
        (obs_rows, obs_values, obs_hours),
        "local_grams",
        [
            pltpu.VMEM(obs_rows.shape, BF16),
            pltpu.VMEM(obs_values.shape, BF16),
            pltpu.VMEM(obs_hours.shape, jnp.int32),
            pltpu.SemaphoreType.DMA((3,)),
        ],
        in_hbm=True,
    )
    received = lax.ppermute(send, "site", swaps(hours, 1))
    distance = 2
    while distance < hours:
        total, send = call(add_and_round, (packed, rounded), (keep, received), "add_and_round")
        received = lax.ppermute(send, "site", swaps(hours, distance))
        distance *= 2
        if distance < hours:
            keep = call(add_received, packed, (total, received), "add_received")
            received = jnp.zeros_like(received)
    rows = states + 16
    block = sds((rows, states), BF16)
    firsts = sds((half - 1, rows, states), BF16)
    own_last, own_firsts, last, first_maps = call(
        hour_maps,
        (sds((rows, states), F32), sds((half - 1, rows, states), F32), block, firsts),
        (total, received, prior, turned),
        "hour_maps",
    )
    other_last = lax.ppermute(own_last, "site", swaps(hours, 1))
    last = lax.ppermute(last, "tm", swaps(blocks, 1))
    first_maps = lax.ppermute(first_maps, "tm", swaps(blocks, 1))
    own = call(block_map, block, (own_last, other_last), "block_map")
    far = lax.ppermute(own, ("tm", "site"), core_swaps(blocks, hours, 2, 3))
    others_last = lax.ppermute(last, "site", swaps(hours, 1))
    others_far = lax.ppermute(far, "site", swaps(hours, 1))
    radix = 4
    following, pair = call(
        pair_block,
        (block, sds((states + 8, states), F32)),
        (own, last, others_last),
        "pair_block",
    )
    gathered, shift = call(
        group_blocks,
        (sds((radix, rows, states), BF16), sds((8, states), F32)),
        (own, following, pair, far, others_far),
        "group_blocks",
    )
    distances, levels = [], []
    distance = radix
    if 2 * distance < blocks:
        joined = call(group_map, sds(own.shape, BF16), (gathered,), "group_map")
    while distance < blocks:
        if 2 * distance == blocks:
            if levels:
                shift = joined[states:].astype(F32).sum(axis=0, keepdims=True)
                shift = jnp.broadcast_to(shift, (8, states))
            received = lax.ppermute(shift, "tm", swaps(blocks, distance))
        else:
            received = lax.ppermute(joined, "tm", swaps(blocks, distance))
            joined = call(
                functools.partial(pair_map, distance),
                sds(own.shape, BF16),
                (joined, received),
                "pair_map",
            )
        distances.append(distance)
        levels.append(received)
        distance *= 2
    other_firsts = lax.ppermute(own_firsts, "site", swaps(hours, 1))
    means = call(
        functools.partial(pair_means, tuple(distances)),
        sds((2 * hours, states), F32),
        [own_last, other_last, own_firsts, other_firsts, last, others_last]
        + levels
        + [gathered],
        "pair_means",
    )
    first_maps = call(hold, firsts, (first_maps, levels[-1]), "hold")
    other_firsts = lax.ppermute(first_maps, "site", swaps(hours, 1))
    means = call(
        rest_of_means,
        sds(means.shape, F32),
        (means, first_maps, other_firsts),
        "rest_of_means",
    )
    if blocks == 2 * radix:
        far = lax.ppermute(means, ("tm", "site"), core_swaps(blocks, hours, 4, 6))
        near = lax.ppermute(means, "tm", swaps(blocks, 2))
        other_far = lax.ppermute(far, "site", swaps(hours, 1))
        means = [means, near, far, other_far]
    else:
        means = call(own_means, sds((blocks, hours, states), BF16), (means,), "own_means")
        means = [lax.all_to_all(means, "tm", 0, 0, tiled=True).reshape(blocks * hours, states)]
    sites = site_basis.shape[0]
    return pl.pallas_call(
        predict,
        out_shape=sds((blocks * hours, sites), BF16),
        in_specs=[whole()] * (len(means) + 1),
        out_specs=pl.BlockSpec(memory_space=pltpu.HBM),
        scratch_shapes=[
            pltpu.VMEM((CHUNKS, blocks * hours, sites // CHUNKS), BF16),
            pltpu.SemaphoreType.DMA((CHUNKS,)),
        ],
        compiler_params=pltpu.CompilerParams(vmem_limit_bytes=VMEM_LIMIT),
        name="predict",
    )(*means, basis)


def solution(mesh):
    in_specs = (
        P(("tm", "site"), None),
        P(("tm", "site")),
        P(("tm", "site")),
        P(),
        P(),
        P(("tm", "site"), None),
    )
    out_specs = P(None, ("tm", "site"))
    return jax.shard_map(body, mesh=mesh, in_specs=in_specs, out_specs=out_specs, check_vma=False)
```

```python
import functools

import jax
import jax.numpy as jnp
from jax import lax
from jax.experimental import pallas as pl
from jax.experimental.pallas import tpu as pltpu
from jax.sharding import PartitionSpec as P

NS_ITERS = 8
TAIL = 8
CHUNKS = 4
BF16 = jnp.bfloat16
F32 = jnp.float32
VMEM_LIMIT = 40 * 2**20
COSTS = {
    "pair_block": pl.CostEstimate(flops=3000000000, bytes_accessed=0, transcendentals=0),
}


def whole():
    return pl.BlockSpec(memory_space=pltpu.VMEM)


def call(kernel, outs, args, name, scratch=(), in_hbm=False):
    if in_hbm:
        args = [pltpu.with_memory_space_constraint(arg, pltpu.HBM) for arg in args]
    return pl.pallas_call(
        kernel,
        out_shape=outs,
        in_specs=[pl.BlockSpec(memory_space=pltpu.HBM) if in_hbm else whole()] * len(args),
        out_specs=jax.tree.map(lambda _: whole(), outs),
        scratch_shapes=scratch,
        compiler_params=pltpu.CompilerParams(vmem_limit_bytes=VMEM_LIMIT),
        cost_estimate=COSTS.get(name),
        name=name,
    )(*args)


def dot(a, b):
    return jnp.dot(a, b, preferred_element_type=F32)


def split(x):
    high = x.astype(BF16)
    return high, (x - high.astype(F32)).astype(BF16)


def dot_wide(a, b):
    a_high, a_low = split(a)
    b_high, b_low = split(b)
    return dot(
        jnp.concatenate([a_high, a_low, a_high], axis=1),
        jnp.concatenate([b_high, b_high, b_low], axis=0),
    )


def thirds(row):
    first = row.astype(BF16).astype(F32)
    second = (row - first).astype(BF16).astype(F32)
    third = row - first - second
    zeros = jnp.zeros((13, row.shape[1]), F32)
    return jnp.concatenate([first, second, third, zeros], axis=0).astype(BF16)


def row_times(row, *weights):
    rows = thirds(row)
    total = dot(rows, weights[0])
    for w in weights[1:]:
        total += dot(rows, w)
    return jnp.sum(total, axis=0, keepdims=True)


def own_half(hours):
    return lax.rem(lax.axis_index("site"), 2) * (hours // 2)


def local_grams(
    hours,
    rows_hbm,
    values_hbm,
    codes_hbm,
    keep_ref,
    send_ref,
    rows_ref,
    values_ref,
    codes_ref,
    sems,
):
    half = hours // 2
    states = rows_hbm.shape[1]
    start = own_half(hours)
    copies = [
        pltpu.make_async_copy(rows_hbm, rows_ref, sems.at[0]),
        pltpu.make_async_copy(values_hbm, values_ref, sems.at[1]),
        pltpu.make_async_copy(codes_hbm, codes_ref, sems.at[2]),
    ]
    for copy in copies:
        copy.start()
    for copy in copies:
        copy.wait()
    rows = rows_ref[...]
    turned = rows.T
    codes = codes_ref[...].reshape(1, rows.shape[0])
    values = values_ref[...].astype(F32).reshape(1, rows.shape[0])
    slots = []
    for slot in range(hours):
        hour = lax.rem(start + slot, hours)
        slots.append((codes == hour).astype(F32))
    masked = jnp.concatenate([turned * s.astype(BF16) for s in slots], axis=0)
    grams = dot(masked, rows)
    weighted = jnp.concatenate([s * values for s in slots], axis=0)
    pad = jnp.zeros((16 - hours, weighted.shape[1]), F32)
    drives = dot(jnp.concatenate([weighted, pad], axis=0).astype(BF16), rows)
    row_id = lax.broadcasted_iota(jnp.int32, (states, states), 0)
    column_id = lax.broadcasted_iota(jnp.int32, (states, states), 1)
    for base in (0, half):
        for pair in range(half // 2):
            first = base + 2 * pair
            a = grams[first * states : (first + 1) * states]
            b = grams[(first + 1) * states : (first + 2) * states]
            diagonals = [
                jnp.sum(jnp.where(row_id == column_id, gram, 0.0), axis=0, keepdims=True)
                for gram in (a, b)
            ]
            square = jnp.where(row_id <= column_id, a, b)
            tail = jnp.concatenate(
                diagonals + [drives[first : first + 2], jnp.zeros((TAIL - 4, states), F32)], axis=0
            )
            if base == 0:
                keep_ref[pair, :states, :] = square
                keep_ref[pair, states:, :] = tail
            else:
                store_rounded(send_ref, pair, square, tail)


def prepare(
    prior_hbm,
    transition_hbm,
    basis_hbm,
    prior_out_ref,
    turned_ref,
    basis_out_ref,
    transition_ref,
    basis_ref,
    sems,
):
    copies = [
        pltpu.make_async_copy(prior_hbm, prior_out_ref, sems.at[0]),
        pltpu.make_async_copy(transition_hbm, transition_ref, sems.at[1]),
        pltpu.make_async_copy(basis_hbm, basis_ref, sems.at[2]),
    ]
    for copy in copies:
        copy.start()
    copies[0].wait()
    copies[1].wait()
    prior = prior_out_ref[...]
    turned_ref[...] = dot_wide(transition_ref[...].T, prior)
    copies[2].wait()
    basis_out_ref[...] = basis_ref[...].T


def add_and_round(keep_ref, received_ref, sum_ref, send_ref):
    states = keep_ref.shape[2]
    for pair in range(keep_ref.shape[0]):
        total = sum_of(keep_ref, received_ref, pair, states)
        sum_ref[pair] = total
        store_rounded(send_ref, pair, total[:states], total[states:])


def store_rounded(out_ref, pair, square, tail):
    states = square.shape[1]
    out_ref[pair, :states, :] = square.astype(BF16)
    high = tail.astype(BF16).astype(F32)
    out_ref[pair, states:, :] = jnp.concatenate([high, tail - high], axis=0).astype(BF16)


def add_received(sum_ref, received_ref, out_ref):
    states = sum_ref.shape[2]
    for pair in range(sum_ref.shape[0]):
        out_ref[pair] = sum_of(sum_ref, received_ref, pair, states)


def sum_of(sum_ref, received_ref, pair, states):
    received = received_ref[pair].astype(F32)
    tail = received[states : states + TAIL] + received[states + TAIL :]
    return sum_ref[pair] + jnp.concatenate([received[:states], tail], axis=0)


def times_own(z, coarse):
    states = z.shape[1]
    high, low = split(z)
    d_high, d_low = high[:states], low[:states]
    mixed = dot(d_high, d_low)
    square = dot(d_high, d_high) + (mixed + mixed.T)
    left, right = [high[states:], high[states:]], [d_high, d_low]
    if not coarse:
        left, right = left + [low[states:]], right + [d_high]
    rest = dot(jnp.concatenate(left, axis=1), jnp.concatenate(right, axis=0))
    return jnp.concatenate([square, rest], axis=0)


def hour_maps(
    sum_ref,
    received_ref,
    prior_ref,
    turned_ref,
    last_ref,
    firsts_ref,
    rounded_last_ref,
    rounded_firsts_ref,
):
    states = prior_ref.shape[0]
    prior = prior_ref[...]
    turned = turned_ref[...]
    row_id = lax.broadcasted_iota(jnp.int32, (states, states), 0)
    column_id = lax.broadcasted_iota(jnp.int32, (states, states), 1)
    running = []
    for pair in range(sum_ref.shape[0]):
        total = sum_of(sum_ref, received_ref, pair, states)
        square = total[:states]
        flipped = square.T
        upper, lower = row_id <= column_id, row_id > column_id
        grams = (jnp.where(upper, square, flipped), jnp.where(lower, square, flipped))
        for place, gram in enumerate(grams):
            diagonal, drive = [total[states + i : states + i + 1] for i in (place, place + 2)]
            gram = jnp.where(row_id == column_id, diagonal, gram)
            precision = prior + gram
            bound = jnp.max(jnp.sum(jnp.abs(precision), axis=0, keepdims=True), axis=1, keepdims=True)
            scale = 1.0 / bound
            offset = jnp.concatenate([drive, jnp.zeros((15, states), F32)], axis=0)
            running.append((precision * scale, turned * scale, offset * scale))
    stacked = [jnp.concatenate(parts, axis=0) for parts in running]

    for step in range(NS_ITERS - 2):
        stacked = [2.0 * z - times_own(z, step < 2) for z in stacked]
    maps = []
    for z in stacked:
        power = (jnp.where(row_id == column_id, 1.0, 0.0) - z[:states]).astype(BF16)
        v = z[states:]
        product = dot(jnp.concatenate([power, v.astype(BF16)], axis=0), power)
        v = v + product[states:]
        maps.append(v + dot(v.astype(BF16), product[:states].astype(BF16)))
    for position in range(len(maps)):
        joined = maps[0] if position == 0 else append(joined, maps[position])
        if position < len(maps) - 1:
            firsts_ref[position] = joined
            rounded_firsts_ref[position] = rounded(joined)
    last_ref[...] = joined
    rounded_last_ref[...] = rounded(joined)


def rounded(affine):
    states = affine.shape[1]
    return jnp.concatenate([affine[:states].astype(BF16), thirds(affine[states : states + 1])], axis=0)


def append(earlier, latter):
    states = latter.shape[1]
    product = dot_wide(earlier, latter[:states])
    return jnp.concatenate([product[:states], product[states:] + latter[states:]], axis=0)


def in_order(own_ref, received_ref):
    first = lax.rem(lax.axis_index("site"), 2) == 0
    count = len(own_ref) if isinstance(own_ref, list) else own_ref.shape[0]
    early = [jnp.where(first, own_ref[i], received_ref[i]) for i in range(count)]
    late = [jnp.where(first, received_ref[i], own_ref[i]) for i in range(count)]
    return early, late


def block_map(own_ref, received_ref, out_ref):
    (early,), (late,) = in_order([own_ref[...]], [received_ref[...]])
    out_ref[...] = rounded(append(early, late))


def pair_block(own_ref, last_ref, other_last_ref, next_ref, pair_ref):
    (early,), (late,) = in_order([last_ref[...]], [other_last_ref[...]])
    own, following = own_ref[...], follow(early, late)
    next_ref[...] = following
    odd = lax.rem(lax.axis_index("tm"), 2) == 1
    first, second = jnp.where(odd, following, own), jnp.where(odd, own, following)
    states = own.shape[1]
    pair_ref[:states, :] = dot(first[:states], second[:states])
    pair_ref[states:, :] = jnp.broadcast_to(apply(second, shift_of(first)), (8, states))


def group_blocks(own_ref, next_ref, pair_ref, far_ref, other_far_ref, out_ref, shift_ref):
    (near,), (far,) = in_order([far_ref[...]], [other_far_ref[...]])
    out_ref[0] = own_ref[...]
    out_ref[1] = next_ref[...]
    out_ref[2] = near
    out_ref[3] = far
    states = near.shape[1]
    place = lax.rem(lax.axis_index("tm"), out_ref.shape[0])
    odd, upper = lax.rem(place, 2) == 1, place >= 2
    first, second = jnp.where(odd, far, near), jnp.where(odd, near, far)
    pair = pair_ref[:states, :]
    pair_shift = pair_ref[states : states + 1, :]
    high, low = split(pair)
    mean = jnp.where(upper, shift_of(first), pair_shift)
    mean = apply(jnp.where(upper, second, first), mean)
    high = jnp.where(upper, high, second[:states])
    low = jnp.where(upper, low, jnp.zeros_like(low))
    mean = row_times(mean, high, low) + jnp.where(upper, pair_shift, shift_of(second))
    shift_ref[...] = jnp.broadcast_to(mean, shift_ref.shape)


def shift_of(block):
    states = block.shape[1]
    return jnp.sum(block[states:].astype(F32), axis=0, keepdims=True)


def choose(values, slot):
    value = values[0]
    for i in range(1, len(values)):
        value = jnp.where(slot == i, values[i], value)
    return value


def apply(block, mean):
    return row_times(mean, block[: block.shape[1]]) + shift_of(block)


def follow(earlier, latter):
    states = latter.shape[1]
    product = dot(earlier[:states], latter[:states]).astype(BF16)
    return jnp.concatenate([product, thirds(apply(latter, shift_of(earlier)))], axis=0)


def group_map(gathered_ref, out_ref):
    place = lax.rem(lax.axis_index("tm"), gathered_ref.shape[0])
    joined = gathered_ref[place]
    for i in range(1, gathered_ref.shape[0]):
        joined = follow(joined, gathered_ref[place ^ i])
    out_ref[...] = joined


def pair_map(distance, own_ref, received_ref, out_ref):
    upper = is_upper(distance)
    first = jnp.where(upper, received_ref[...], own_ref[...])
    second = jnp.where(upper, own_ref[...], received_ref[...])
    out_ref[...] = follow(first, second)


def is_upper(distance):
    return lax.rem(lax.axis_index("tm") // distance, 2) == 1


def hold(maps_ref, received_ref, out_ref):
    out_ref[...] = maps_ref[...]


def pair_means(distances, *refs):
    out_ref = refs[-1]
    own_last_ref, own_other_ref, own_firsts_ref, other_firsts_ref, last_ref, other_last_ref = refs[:6]
    levels, gathered_ref = refs[6:-2], refs[-2]
    rows, states = own_last_ref.shape
    half = own_firsts_ref.shape[0] + 1
    mean = jnp.zeros((1, states), F32)
    for level in reversed(range(len(distances))):
        if level == len(distances) - 1:
            entered = levels[level][0:1, :]
        else:
            entered = apply(levels[level][...], mean)
        mean = jnp.where(is_upper(distances[level]), entered, mean)
    place = lax.rem(lax.axis_index("tm"), gathered_ref.shape[0])
    for i in range(2):
        mean = jnp.where(place >= 2, apply(gathered_ref[place ^ i], mean), mean)
    odd = lax.rem(place, 2) == 1
    between = apply(gathered_ref[place & 1], mean)
    own_start = jnp.where(odd, between, mean)
    own = []
    sides = [
        [firsts[i] for i in range(half - 1)] + [last[...]]
        for firsts, last in ((own_firsts_ref, own_last_ref), (other_firsts_ref, own_other_ref))
    ]
    for maps in in_order(*sides):
        start = own_start if not own else own[-1]
        for each in maps:
            own.append(row_times(start, *split(each[:states])) + each[states : states + 1])
    state = jnp.where(odd, mean, own[-1])
    partner = []
    for maps in in_order([last_ref[...]], [other_last_ref[...]]):
        partner += [state] * (half - 1)
        state = apply(maps[0], state)
        partner.append(state)
    own, partner = jnp.concatenate(own, axis=0), jnp.concatenate(partner, axis=0)
    out_ref[: 2 * half, :] = jnp.where(odd, partner, own)
    out_ref[2 * half :, :] = jnp.where(odd, own, partner)


def rest_of_means(means_ref, firsts_ref, other_ref, out_ref):
    count = firsts_ref.shape[0]
    hours = 2 * (count + 1)
    odd = lax.rem(lax.axis_index("tm"), 2) == 1
    out_ref[...] = means_ref[...]
    partner = jnp.where(odd, means_ref[:hours, :], means_ref[hours:, :])
    for side, maps in enumerate(in_order(firsts_ref, other_ref)):
        for i in range(count):
            hour = side * (count + 1) + i
            mean = apply(maps[i], partner[hour : hour + 1])
            out_ref[pl.ds(jnp.where(odd, hour, hours + hour), 1), :] = mean


def own_means(means_ref, out_ref):
    hours = out_ref.shape[1]
    odd = lax.rem(lax.axis_index("tm"), 2) == 1
    means = jnp.where(odd, means_ref[hours:, :], means_ref[:hours, :]).astype(BF16)
    for copy in range(out_ref.shape[0]):
        out_ref[copy] = means


def predict(*refs):
    means_refs, basis_ref, out_hbm, held_ref, sems = refs[:-4], *refs[-4:]
    if len(means_refs) > 1:
        place = lax.axis_index("tm") // 2
        own, near, far, other_far = [ref[...] for ref in means_refs]
        (third,), (fourth,) = in_order([far], [other_far])
        by_distance = [own, near, third, fourth]
        means = jnp.concatenate([choose(by_distance, place ^ i) for i in range(4)], axis=0)
        means = means.astype(BF16)
    else:
        means = means_refs[0][...]
    width = held_ref.shape[2]
    copies = []
    for chunk in range(CHUNKS):
        columns = pl.ds(chunk * width, width)
        held_ref[chunk] = dot(means, basis_ref[:, columns]).astype(BF16)
        copy = pltpu.make_async_copy(held_ref.at[chunk], out_hbm.at[:, columns], sems.at[chunk])
        copy.start()
        copies.append(copy)
    for copy in copies:
        copy.wait()


def core_swaps(blocks, hours, first, second):
    distances = [first, second] * (hours // 2)
    return [
        (t * hours + d, (t ^ distances[d]) * hours + d) for t in range(blocks) for d in range(hours)
    ]


def swaps(size, distance):
    return [(i, i ^ distance) for i in range(size)]


def body(obs_rows, obs_values, obs_hours, prior_precision, transition, site_basis):
    hours = lax.axis_size("site")
    blocks = lax.axis_size("tm")
    count, states = obs_rows.shape
    half = hours // 2
    pairs = half // 2
    sds = jax.ShapeDtypeStruct
    square = sds((states, states), F32)
    prior, turned, basis = call(
        prepare,
        (square, square, sds(site_basis.shape[::-1], BF16)),
        (prior_precision, transition, site_basis),
        "prepare",
        [
            pltpu.VMEM(transition.shape, F32),
            pltpu.VMEM(site_basis.shape, BF16),
            pltpu.SemaphoreType.DMA((3,)),
        ],
        in_hbm=True,
    )
    packed = sds((pairs, states + TAIL, states), F32)
    rounded = sds((pairs, states + 2 * TAIL, states), BF16)
    keep, send = call(
        functools.partial(local_grams, hours),
        (packed, rounded),
        (obs_rows, obs_values, obs_hours),
        "local_grams",
        [
            pltpu.VMEM(obs_rows.shape, BF16),
            pltpu.VMEM(obs_values.shape, BF16),
            pltpu.VMEM(obs_hours.shape, jnp.int32),
            pltpu.SemaphoreType.DMA((3,)),
        ],
        in_hbm=True,
    )
    received = lax.ppermute(send, "site", swaps(hours, 1))
    distance = 2
    while distance < hours:
        total, send = call(add_and_round, (packed, rounded), (keep, received), "add_and_round")
        received = lax.ppermute(send, "site", swaps(hours, distance))
        distance *= 2
        if distance < hours:
            keep = call(add_received, packed, (total, received), "add_received")
            received = jnp.zeros_like(received)
    rows = states + 16
    block = sds((rows, states), BF16)
    firsts = sds((half - 1, rows, states), BF16)
    own_last, own_firsts, last, first_maps = call(
        hour_maps,
        (sds((rows, states), F32), sds((half - 1, rows, states), F32), block, firsts),
        (total, received, prior, turned),
        "hour_maps",
    )
    other_last = lax.ppermute(own_last, "site", swaps(hours, 1))
    last = lax.ppermute(last, "tm", swaps(blocks, 1))
    first_maps = lax.ppermute(first_maps, "tm", swaps(blocks, 1))
    own = call(block_map, block, (own_last, other_last), "block_map")
    far = lax.ppermute(own, ("tm", "site"), core_swaps(blocks, hours, 2, 3))
    others_last = lax.ppermute(last, "site", swaps(hours, 1))
    others_far = lax.ppermute(far, "site", swaps(hours, 1))
    radix = 4
    following, pair = call(
        pair_block,
        (block, sds((states + 8, states), F32)),
        (own, last, others_last),
        "pair_block",
    )
    gathered, shift = call(
        group_blocks,
        (sds((radix, rows, states), BF16), sds((8, states), F32)),
        (own, following, pair, far, others_far),
        "group_blocks",
    )
    distances, levels = [], []
    distance = radix
    if 2 * distance < blocks:
        joined = call(group_map, sds(own.shape, BF16), (gathered,), "group_map")
    while distance < blocks:
        if 2 * distance == blocks:
            if levels:
                shift = joined[states:].astype(F32).sum(axis=0, keepdims=True)
                shift = jnp.broadcast_to(shift, (8, states))
            received = lax.ppermute(shift, "tm", swaps(blocks, distance))
        else:
            received = lax.ppermute(joined, "tm", swaps(blocks, distance))
            joined = call(
                functools.partial(pair_map, distance),
                sds(own.shape, BF16),
                (joined, received),
                "pair_map",
            )
        distances.append(distance)
        levels.append(received)
        distance *= 2
    other_firsts = lax.ppermute(own_firsts, "site", swaps(hours, 1))
    means = call(
        functools.partial(pair_means, tuple(distances)),
        sds((2 * hours, states), F32),
        [own_last, other_last, own_firsts, other_firsts, last, others_last]
        + levels
        + [gathered],
        "pair_means",
    )
    first_maps = call(hold, firsts, (first_maps, levels[-1]), "hold")
    other_firsts = lax.ppermute(first_maps, "site", swaps(hours, 1))
    means = call(
        rest_of_means,
        sds(means.shape, F32),
        (means, first_maps, other_firsts),
        "rest_of_means",
    )
    if blocks == 2 * radix:
        far = lax.ppermute(means, ("tm", "site"), core_swaps(blocks, hours, 4, 6))
        near = lax.ppermute(means, "tm", swaps(blocks, 2))
        other_far = lax.ppermute(far, "site", swaps(hours, 1))
        means = [means, near, far, other_far]
    else:
        means = call(own_means, sds((blocks, hours, states), BF16), (means,), "own_means")
        means = [lax.all_to_all(means, "tm", 0, 0, tiled=True).reshape(blocks * hours, states)]
    sites = site_basis.shape[0]
    return pl.pallas_call(
        predict,
        out_shape=sds((blocks * hours, sites), BF16),
        in_specs=[whole()] * (len(means) + 1),
        out_specs=pl.BlockSpec(memory_space=pltpu.HBM),
        scratch_shapes=[
            pltpu.VMEM((CHUNKS, blocks * hours, sites // CHUNKS), BF16),
            pltpu.SemaphoreType.DMA((CHUNKS,)),
        ],
        compiler_params=pltpu.CompilerParams(vmem_limit_bytes=VMEM_LIMIT),
        name="predict",
    )(*means, basis)


def solution(mesh):
    in_specs = (
        P(("tm", "site"), None),
        P(("tm", "site")),
        P(("tm", "site")),
        P(),
        P(),
        P(("tm", "site"), None),
    )
    out_specs = P(None, ("tm", "site"))
    return jax.shard_map(body, mesh=mesh, in_specs=in_specs, out_specs=out_specs, check_vma=False)
```

```python
import functools

import jax
import jax.numpy as jnp
from jax import lax
from jax.experimental import pallas as pl
from jax.experimental.pallas import tpu as pltpu
from jax.sharding import PartitionSpec as P

NS_ITERS = 8
TAIL = 8
CHUNKS = 4
BF16 = jnp.bfloat16
F32 = jnp.float32
VMEM_LIMIT = 40 * 2**20
COSTS = {
    "pair_block": pl.CostEstimate(flops=3000000000, bytes_accessed=0, transcendentals=0),
}


def whole():
    return pl.BlockSpec(memory_space=pltpu.VMEM)


def call(kernel, outs, args, name, scratch=(), in_hbm=False):
    if in_hbm:
        args = [pltpu.with_memory_space_constraint(arg, pltpu.HBM) for arg in args]
    return pl.pallas_call(
        kernel,
        out_shape=outs,
        in_specs=[pl.BlockSpec(memory_space=pltpu.HBM) if in_hbm else whole()] * len(args),
        out_specs=jax.tree.map(lambda _: whole(), outs),
        scratch_shapes=scratch,
        compiler_params=pltpu.CompilerParams(vmem_limit_bytes=VMEM_LIMIT),
        cost_estimate=COSTS.get(name),
        name=name,
    )(*args)


def dot(a, b):
    return jnp.dot(a, b, preferred_element_type=F32)


def split(x):
    high = x.astype(BF16)
    return high, (x - high.astype(F32)).astype(BF16)


def dot_wide(a, b):
    a_high, a_low = split(a)
    b_high, b_low = split(b)
    return dot(
        jnp.concatenate([a_high, a_low, a_high], axis=1),
        jnp.concatenate([b_high, b_high, b_low], axis=0),
    )


def thirds(row):
    first = row.astype(BF16).astype(F32)
    second = (row - first).astype(BF16).astype(F32)
    third = row - first - second
    zeros = jnp.zeros((13, row.shape[1]), F32)
    return jnp.concatenate([first, second, third, zeros], axis=0).astype(BF16)


def row_times(row, *weights):
    rows = thirds(row)
    total = dot(rows, weights[0])
    for w in weights[1:]:
        total += dot(rows, w)
    return jnp.sum(total, axis=0, keepdims=True)


def own_half(hours):
    return lax.rem(lax.axis_index("site"), 2) * (hours // 2)


def local_grams(
    hours,
    rows_hbm,
    values_hbm,
    codes_hbm,
    keep_ref,
    send_ref,
    rows_ref,
    values_ref,
    codes_ref,
    sems,
):
    half = hours // 2
    states = rows_hbm.shape[1]
    start = own_half(hours)
    copies = [
        pltpu.make_async_copy(rows_hbm, rows_ref, sems.at[0]),
        pltpu.make_async_copy(values_hbm, values_ref, sems.at[1]),
        pltpu.make_async_copy(codes_hbm, codes_ref, sems.at[2]),
    ]
    for copy in copies:
        copy.start()
    for copy in copies:
        copy.wait()
    rows = rows_ref[...]
    turned = rows.T
    codes = codes_ref[...].reshape(1, rows.shape[0])
    values = values_ref[...].astype(F32).reshape(1, rows.shape[0])
    slots = []
    for slot in range(hours):
        hour = lax.rem(start + slot, hours)
        slots.append((codes == hour).astype(F32))
    masked = jnp.concatenate([turned * s.astype(BF16) for s in slots], axis=0)
    grams = dot(masked, rows)
    weighted = jnp.concatenate([s * values for s in slots], axis=0)
    pad = jnp.zeros((16 - hours, weighted.shape[1]), F32)
    drives = dot(jnp.concatenate([weighted, pad], axis=0).astype(BF16), rows)
    row_id = lax.broadcasted_iota(jnp.int32, (states, states), 0)
    column_id = lax.broadcasted_iota(jnp.int32, (states, states), 1)
    for base in (0, half):
        for pair in range(half // 2):
            first = base + 2 * pair
            a = grams[first * states : (first + 1) * states]
            b = grams[(first + 1) * states : (first + 2) * states]
            diagonals = [
                jnp.sum(jnp.where(row_id == column_id, gram, 0.0), axis=0, keepdims=True)
                for gram in (a, b)
            ]
            square = jnp.where(row_id <= column_id, a, b)
            tail = jnp.concatenate(
                diagonals + [drives[first : first + 2], jnp.zeros((TAIL - 4, states), F32)], axis=0
            )
            if base == 0:
                keep_ref[pair, :states, :] = square
                keep_ref[pair, states:, :] = tail
            else:
                store_rounded(send_ref, pair, square, tail)


def prepare(
    prior_hbm,
    transition_hbm,
    basis_hbm,
    prior_out_ref,
    turned_ref,
    basis_out_ref,
    transition_ref,
    basis_ref,
    sems,
):
    copies = [
        pltpu.make_async_copy(prior_hbm, prior_out_ref, sems.at[0]),
        pltpu.make_async_copy(transition_hbm, transition_ref, sems.at[1]),
        pltpu.make_async_copy(basis_hbm, basis_ref, sems.at[2]),
    ]
    for copy in copies:
        copy.start()
    copies[0].wait()
    copies[1].wait()
    prior = prior_out_ref[...]
    turned_ref[...] = dot_wide(transition_ref[...].T, prior)
    copies[2].wait()
    basis_out_ref[...] = basis_ref[...].T


def add_and_round(keep_ref, received_ref, sum_ref, send_ref):
    states = keep_ref.shape[2]
    for pair in range(keep_ref.shape[0]):
        total = sum_of(keep_ref, received_ref, pair, states)
        sum_ref[pair] = total
        store_rounded(send_ref, pair, total[:states], total[states:])


def store_rounded(out_ref, pair, square, tail):
    states = square.shape[1]
    out_ref[pair, :states, :] = square.astype(BF16)
    high = tail.astype(BF16).astype(F32)
    out_ref[pair, states:, :] = jnp.concatenate([high, tail - high], axis=0).astype(BF16)


def add_received(sum_ref, received_ref, out_ref):
    states = sum_ref.shape[2]
    for pair in range(sum_ref.shape[0]):
        out_ref[pair] = sum_of(sum_ref, received_ref, pair, states)


def sum_of(sum_ref, received_ref, pair, states):
    received = received_ref[pair].astype(F32)
    tail = received[states : states + TAIL] + received[states + TAIL :]
    return sum_ref[pair] + jnp.concatenate([received[:states], tail], axis=0)


def times_own(z, coarse):
    states = z.shape[1]
    high, low = split(z)
    d_high, d_low = high[:states], low[:states]
    mixed = dot(d_high, d_low)
    square = dot(d_high, d_high) + (mixed + mixed.T)
    left, right = [high[states:], high[states:]], [d_high, d_low]
    if not coarse:
        left, right = left + [low[states:]], right + [d_high]
    rest = dot(jnp.concatenate(left, axis=1), jnp.concatenate(right, axis=0))
    return jnp.concatenate([square, rest], axis=0)


def hour_maps(
    sum_ref,
    received_ref,
    prior_ref,
    turned_ref,
    last_ref,
    firsts_ref,
    rounded_last_ref,
    rounded_firsts_ref,
):
    states = prior_ref.shape[0]
    prior = prior_ref[...]
    turned = turned_ref[...]
    row_id = lax.broadcasted_iota(jnp.int32, (states, states), 0)
    column_id = lax.broadcasted_iota(jnp.int32, (states, states), 1)
    running = []
    for pair in range(sum_ref.shape[0]):
        total = sum_of(sum_ref, received_ref, pair, states)
        square = total[:states]
        flipped = square.T
        upper, lower = row_id <= column_id, row_id > column_id
        grams = (jnp.where(upper, square, flipped), jnp.where(lower, square, flipped))
        for place, gram in enumerate(grams):
            diagonal, drive = [total[states + i : states + i + 1] for i in (place, place + 2)]
            gram = jnp.where(row_id == column_id, diagonal, gram)
            precision = prior + gram
            bound = jnp.max(jnp.sum(jnp.abs(precision), axis=0, keepdims=True), axis=1, keepdims=True)
            scale = 1.0 / bound
            offset = jnp.concatenate([drive, jnp.zeros((15, states), F32)], axis=0)
            running.append((precision * scale, turned * scale, offset * scale))
    stacked = [jnp.concatenate(parts, axis=0) for parts in running]

    for step in range(NS_ITERS - 2):
        stacked = [2.0 * z - times_own(z, step < 2) for z in stacked]
    maps = []
    for z in stacked:
        power = (jnp.where(row_id == column_id, 1.0, 0.0) - z[:states]).astype(BF16)
        v = z[states:]
        product = dot(jnp.concatenate([power, v.astype(BF16)], axis=0), power)
        v = v + product[states:]
        maps.append(v + dot(v.astype(BF16), product[:states].astype(BF16)))
    for position in range(len(maps)):
        joined = maps[0] if position == 0 else append(joined, maps[position])
        if position < len(maps) - 1:
            firsts_ref[position] = joined
            rounded_firsts_ref[position] = rounded(joined)
    last_ref[...] = joined
    rounded_last_ref[...] = rounded(joined)


def rounded(affine):
    states = affine.shape[1]
    return jnp.concatenate([affine[:states].astype(BF16), thirds(affine[states : states + 1])], axis=0)


def append(earlier, latter):
    states = latter.shape[1]
    product = dot_wide(earlier, latter[:states])
    return jnp.concatenate([product[:states], product[states:] + latter[states:]], axis=0)


def in_order(own_ref, received_ref):
    first = lax.rem(lax.axis_index("site"), 2) == 0
    count = len(own_ref) if isinstance(own_ref, list) else own_ref.shape[0]
    early = [jnp.where(first, own_ref[i], received_ref[i]) for i in range(count)]
    late = [jnp.where(first, received_ref[i], own_ref[i]) for i in range(count)]
    return early, late


def widened(block):
    states = block.shape[1]
    pad = jnp.zeros((15, states), F32)
    return jnp.concatenate([block[:states].astype(F32), shift_of(block), pad], axis=0)


def block_map(own_ref, received_ref, out_ref):
    (early,), (late,) = in_order([own_ref[...]], [widened(received_ref[...])])
    out_ref[...] = rounded(append(early, late))


def pair_block(own_ref, last_ref, other_last_ref, next_ref, pair_ref):
    (early,), (late,) = in_order([last_ref[...]], [other_last_ref[...]])
    own, following = own_ref[...], follow(early, late)
    next_ref[...] = following
    odd = lax.rem(lax.axis_index("tm"), 2) == 1
    first, second = jnp.where(odd, following, own), jnp.where(odd, own, following)
    states = own.shape[1]
    pair_ref[:states, :] = dot(first[:states], second[:states])
    pair_ref[states:, :] = jnp.broadcast_to(apply(second, shift_of(first)), (8, states))


def group_blocks(own_ref, next_ref, pair_ref, far_ref, other_far_ref, out_ref, shift_ref):
    (near,), (far,) = in_order([far_ref[...]], [other_far_ref[...]])
    out_ref[0] = own_ref[...]
    out_ref[1] = next_ref[...]
    out_ref[2] = near
    out_ref[3] = far
    states = near.shape[1]
    place = lax.rem(lax.axis_index("tm"), out_ref.shape[0])
    odd, upper = lax.rem(place, 2) == 1, place >= 2
    first, second = jnp.where(odd, far, near), jnp.where(odd, near, far)
    pair = pair_ref[:states, :]
    pair_shift = pair_ref[states : states + 1, :]
    high, low = split(pair)
    mean = jnp.where(upper, shift_of(first), pair_shift)
    mean = apply(jnp.where(upper, second, first), mean)
    high = jnp.where(upper, high, second[:states])
    low = jnp.where(upper, low, jnp.zeros_like(low))
    mean = row_times(mean, high, low) + jnp.where(upper, pair_shift, shift_of(second))
    shift_ref[...] = jnp.broadcast_to(mean, shift_ref.shape)


def shift_of(block):
    states = block.shape[1]
    return jnp.sum(block[states:].astype(F32), axis=0, keepdims=True)


def choose(values, slot):
    value = values[0]
    for i in range(1, len(values)):
        value = jnp.where(slot == i, values[i], value)
    return value


def apply(block, mean):
    return row_times(mean, block[: block.shape[1]]) + shift_of(block)


def follow(earlier, latter):
    states = latter.shape[1]
    product = dot(earlier[:states], latter[:states]).astype(BF16)
    return jnp.concatenate([product, thirds(apply(latter, shift_of(earlier)))], axis=0)


def group_map(gathered_ref, out_ref):
    place = lax.rem(lax.axis_index("tm"), gathered_ref.shape[0])
    joined = gathered_ref[place]
    for i in range(1, gathered_ref.shape[0]):
        joined = follow(joined, gathered_ref[place ^ i])
    out_ref[...] = joined


def pair_map(distance, own_ref, received_ref, out_ref):
    upper = is_upper(distance)
    first = jnp.where(upper, received_ref[...], own_ref[...])
    second = jnp.where(upper, own_ref[...], received_ref[...])
    out_ref[...] = follow(first, second)


def is_upper(distance):
    return lax.rem(lax.axis_index("tm") // distance, 2) == 1


def hold(maps_ref, received_ref, out_ref):
    out_ref[...] = maps_ref[...]


def pair_means(distances, *refs):
    out_ref = refs[-1]
    own_last_ref, own_other_ref, own_firsts_ref, other_firsts_ref, last_ref, other_last_ref = refs[:6]
    levels, gathered_ref = refs[6:-2], refs[-2]
    rows, states = own_last_ref.shape
    half = own_firsts_ref.shape[0] + 1
    mean = jnp.zeros((1, states), F32)
    for level in reversed(range(len(distances))):
        if level == len(distances) - 1:
            entered = levels[level][0:1, :]
        else:
            entered = apply(levels[level][...], mean)
        mean = jnp.where(is_upper(distances[level]), entered, mean)
    place = lax.rem(lax.axis_index("tm"), gathered_ref.shape[0])
    for i in range(2):
        mean = jnp.where(place >= 2, apply(gathered_ref[place ^ i], mean), mean)
    odd = lax.rem(place, 2) == 1
    between = apply(gathered_ref[place & 1], mean)
    own_start = jnp.where(odd, between, mean)
    own = []
    sides = [
        [own_firsts_ref[i] for i in range(half - 1)] + [own_last_ref[...]],
        [widened(other_firsts_ref[i]) for i in range(half - 1)] + [widened(own_other_ref[...])],
    ]
    for maps in in_order(*sides):
        start = own_start if not own else own[-1]
        for each in maps:
            own.append(row_times(start, *split(each[:states])) + each[states : states + 1])
    state = jnp.where(odd, mean, own[-1])
    partner = []
    for maps in in_order([last_ref[...]], [other_last_ref[...]]):
        partner += [state] * (half - 1)
        state = apply(maps[0], state)
        partner.append(state)
    own, partner = jnp.concatenate(own, axis=0), jnp.concatenate(partner, axis=0)
    out_ref[: 2 * half, :] = jnp.where(odd, partner, own)
    out_ref[2 * half :, :] = jnp.where(odd, own, partner)


def rest_of_means(means_ref, firsts_ref, other_ref, out_ref):
    count = firsts_ref.shape[0]
    hours = 2 * (count + 1)
    odd = lax.rem(lax.axis_index("tm"), 2) == 1
    out_ref[...] = means_ref[...]
    partner = jnp.where(odd, means_ref[:hours, :], means_ref[hours:, :])
    for side, maps in enumerate(in_order(firsts_ref, other_ref)):
        for i in range(count):
            hour = side * (count + 1) + i
            mean = apply(maps[i], partner[hour : hour + 1])
            out_ref[pl.ds(jnp.where(odd, hour, hours + hour), 1), :] = mean


def own_means(means_ref, out_ref):
    hours = out_ref.shape[1]
    odd = lax.rem(lax.axis_index("tm"), 2) == 1
    means = jnp.where(odd, means_ref[hours:, :], means_ref[:hours, :]).astype(BF16)
    for copy in range(out_ref.shape[0]):
        out_ref[copy] = means


def predict(*refs):
    means_refs, basis_ref, out_hbm, held_ref, sems = refs[:-4], *refs[-4:]
    if len(means_refs) > 1:
        place = lax.axis_index("tm") // 2
        own, near, far, other_far = [ref[...] for ref in means_refs]
        (third,), (fourth,) = in_order([far], [other_far])
        by_distance = [own, near, third, fourth]
        means = jnp.concatenate([choose(by_distance, place ^ i) for i in range(4)], axis=0)
        means = means.astype(BF16)
    else:
        means = means_refs[0][...]
    width = held_ref.shape[2]
    copies = []
    for chunk in range(CHUNKS):
        columns = pl.ds(chunk * width, width)
        held_ref[chunk] = dot(means, basis_ref[:, columns]).astype(BF16)
        copy = pltpu.make_async_copy(held_ref.at[chunk], out_hbm.at[:, columns], sems.at[chunk])
        copy.start()
        copies.append(copy)
    for copy in copies:
        copy.wait()


def core_swaps(blocks, hours, first, second):
    distances = [first, second] * (hours // 2)
    return [
        (t * hours + d, (t ^ distances[d]) * hours + d) for t in range(blocks) for d in range(hours)
    ]


def swaps(size, distance):
    return [(i, i ^ distance) for i in range(size)]


def body(obs_rows, obs_values, obs_hours, prior_precision, transition, site_basis):
    hours = lax.axis_size("site")
    blocks = lax.axis_size("tm")
    count, states = obs_rows.shape
    half = hours // 2
    pairs = half // 2
    sds = jax.ShapeDtypeStruct
    square = sds((states, states), F32)
    prior, turned, basis = call(
        prepare,
        (square, square, sds(site_basis.shape[::-1], BF16)),
        (prior_precision, transition, site_basis),
        "prepare",
        [
            pltpu.VMEM(transition.shape, F32),
            pltpu.VMEM(site_basis.shape, BF16),
            pltpu.SemaphoreType.DMA((3,)),
        ],
        in_hbm=True,
    )
    packed = sds((pairs, states + TAIL, states), F32)
    rounded = sds((pairs, states + 2 * TAIL, states), BF16)
    keep, send = call(
        functools.partial(local_grams, hours),
        (packed, rounded),
        (obs_rows, obs_values, obs_hours),
        "local_grams",
        [
            pltpu.VMEM(obs_rows.shape, BF16),
            pltpu.VMEM(obs_values.shape, BF16),
            pltpu.VMEM(obs_hours.shape, jnp.int32),
            pltpu.SemaphoreType.DMA((3,)),
        ],
        in_hbm=True,
    )
    received = lax.ppermute(send, "site", swaps(hours, 1))
    distance = 2
    while distance < hours:
        total, send = call(add_and_round, (packed, rounded), (keep, received), "add_and_round")
        received = lax.ppermute(send, "site", swaps(hours, distance))
        distance *= 2
        if distance < hours:
            keep = call(add_received, packed, (total, received), "add_received")
            received = jnp.zeros_like(received)
    rows = states + 16
    block = sds((rows, states), BF16)
    firsts = sds((half - 1, rows, states), BF16)
    own_last, own_firsts, last, own_rounded = call(
        hour_maps,
        (sds((rows, states), F32), sds((half - 1, rows, states), F32), block, firsts),
        (total, received, prior, turned),
        "hour_maps",
    )
    other_last = lax.ppermute(last, "site", swaps(hours, 1))
    last = lax.ppermute(last, "tm", swaps(blocks, 1))
    first_maps = lax.ppermute(own_rounded, "tm", swaps(blocks, 1))
    own = call(block_map, block, (own_last, other_last), "block_map")
    far = lax.ppermute(own, ("tm", "site"), core_swaps(blocks, hours, 2, 3))
    others_last = lax.ppermute(last, "site", swaps(hours, 1))
    others_far = lax.ppermute(far, "site", swaps(hours, 1))
    radix = 4
    following, pair = call(
        pair_block,
        (block, sds((states + 8, states), F32)),
        (own, last, others_last),
        "pair_block",
    )
    gathered, shift = call(
        group_blocks,
        (sds((radix, rows, states), BF16), sds((8, states), F32)),
        (own, following, pair, far, others_far),
        "group_blocks",
    )
    distances, levels = [], []
    distance = radix
    if 2 * distance < blocks:
        joined = call(group_map, sds(own.shape, BF16), (gathered,), "group_map")
    while distance < blocks:
        if 2 * distance == blocks:
            if levels:
                shift = joined[states:].astype(F32).sum(axis=0, keepdims=True)
                shift = jnp.broadcast_to(shift, (8, states))
            received = lax.ppermute(shift, "tm", swaps(blocks, distance))
        else:
            received = lax.ppermute(joined, "tm", swaps(blocks, distance))
            joined = call(
                functools.partial(pair_map, distance),
                sds(own.shape, BF16),
                (joined, received),
                "pair_map",
            )
        distances.append(distance)
        levels.append(received)
        distance *= 2
    other_firsts = lax.ppermute(own_rounded, "site", swaps(hours, 1))
    means = call(
        functools.partial(pair_means, tuple(distances)),
        sds((2 * hours, states), F32),
        [own_last, other_last, own_firsts, other_firsts, last, others_last]
        + levels
        + [gathered],
        "pair_means",
    )
    first_maps = call(hold, firsts, (first_maps, levels[-1]), "hold")
    other_firsts = lax.ppermute(first_maps, "site", swaps(hours, 1))
    means = call(
        rest_of_means,
        sds(means.shape, F32),
        (means, first_maps, other_firsts),
        "rest_of_means",
    )
    if blocks == 2 * radix:
        far = lax.ppermute(means, ("tm", "site"), core_swaps(blocks, hours, 4, 6))
        near = lax.ppermute(means, "tm", swaps(blocks, 2))
        other_far = lax.ppermute(far, "site", swaps(hours, 1))
        means = [means, near, far, other_far]
    else:
        means = call(own_means, sds((blocks, hours, states), BF16), (means,), "own_means")
        means = [lax.all_to_all(means, "tm", 0, 0, tiled=True).reshape(blocks * hours, states)]
    sites = site_basis.shape[0]
    return pl.pallas_call(
        predict,
        out_shape=sds((blocks * hours, sites), BF16),
        in_specs=[whole()] * (len(means) + 1),
        out_specs=pl.BlockSpec(memory_space=pltpu.HBM),
        scratch_shapes=[
            pltpu.VMEM((CHUNKS, blocks * hours, sites // CHUNKS), BF16),
            pltpu.SemaphoreType.DMA((CHUNKS,)),
        ],
        compiler_params=pltpu.CompilerParams(vmem_limit_bytes=VMEM_LIMIT),
        name="predict",
    )(*means, basis)


def solution(mesh):
    in_specs = (
        P(("tm", "site"), None),
        P(("tm", "site")),
        P(("tm", "site")),
        P(),
        P(),
        P(("tm", "site"), None),
    )
    out_specs = P(None, ("tm", "site"))
    return jax.shard_map(body, mesh=mesh, in_specs=in_specs, out_specs=out_specs, check_vma=False)
```

```python
import functools

import jax
import jax.numpy as jnp
from jax import lax
from jax.experimental import pallas as pl
from jax.experimental.pallas import tpu as pltpu
from jax.sharding import PartitionSpec as P

NS_ITERS = 8
TAIL = 8
CHUNKS = 4
BF16 = jnp.bfloat16
F32 = jnp.float32
VMEM_LIMIT = 40 * 2**20
COSTS = {
    "pair_block": pl.CostEstimate(flops=3000000000, bytes_accessed=0, transcendentals=0),
}


def whole():
    return pl.BlockSpec(memory_space=pltpu.VMEM)


def call(kernel, outs, args, name, scratch=(), in_hbm=False):
    if in_hbm:
        args = [pltpu.with_memory_space_constraint(arg, pltpu.HBM) for arg in args]
    return pl.pallas_call(
        kernel,
        out_shape=outs,
        in_specs=[pl.BlockSpec(memory_space=pltpu.HBM) if in_hbm else whole()] * len(args),
        out_specs=jax.tree.map(lambda _: whole(), outs),
        scratch_shapes=scratch,
        compiler_params=pltpu.CompilerParams(vmem_limit_bytes=VMEM_LIMIT),
        cost_estimate=COSTS.get(name),
        name=name,
    )(*args)


def dot(a, b):
    return jnp.dot(a, b, preferred_element_type=F32)


def split(x):
    high = x.astype(BF16)
    return high, (x - high.astype(F32)).astype(BF16)


def dot_wide(a, b):
    a_high, a_low = split(a)
    b_high, b_low = split(b)
    return dot(
        jnp.concatenate([a_high, a_low, a_high], axis=1),
        jnp.concatenate([b_high, b_high, b_low], axis=0),
    )


def thirds(row):
    first = row.astype(BF16).astype(F32)
    second = (row - first).astype(BF16).astype(F32)
    third = row - first - second
    zeros = jnp.zeros((13, row.shape[1]), F32)
    return jnp.concatenate([first, second, third, zeros], axis=0).astype(BF16)


def row_times(row, *weights):
    rows = thirds(row)
    total = dot(rows, weights[0])
    for w in weights[1:]:
        total += dot(rows, w)
    return jnp.sum(total, axis=0, keepdims=True)


def own_half(hours):
    return lax.rem(lax.axis_index("site"), 2) * (hours // 2)


def local_grams(
    hours,
    rows_hbm,
    values_hbm,
    codes_hbm,
    keep_ref,
    send_ref,
    rows_ref,
    values_ref,
    codes_ref,
    sems,
):
    half = hours // 2
    states = rows_hbm.shape[1]
    start = own_half(hours)
    copies = [
        pltpu.make_async_copy(rows_hbm, rows_ref, sems.at[0]),
        pltpu.make_async_copy(values_hbm, values_ref, sems.at[1]),
        pltpu.make_async_copy(codes_hbm, codes_ref, sems.at[2]),
    ]
    for copy in copies:
        copy.start()
    for copy in copies:
        copy.wait()
    rows = rows_ref[...]
    turned = rows.T
    codes = codes_ref[...].reshape(1, rows.shape[0])
    values = values_ref[...].astype(F32).reshape(1, rows.shape[0])
    slots = []
    for slot in range(hours):
        hour = lax.rem(start + slot, hours)
        slots.append((codes == hour).astype(F32))
    masked = jnp.concatenate([turned * s.astype(BF16) for s in slots], axis=0)
    grams = dot(masked, rows)
    weighted = jnp.concatenate([s * values for s in slots], axis=0)
    pad = jnp.zeros((16 - hours, weighted.shape[1]), F32)
    drives = dot(jnp.concatenate([weighted, pad], axis=0).astype(BF16), rows)
    row_id = lax.broadcasted_iota(jnp.int32, (states, states), 0)
    column_id = lax.broadcasted_iota(jnp.int32, (states, states), 1)
    for base in (0, half):
        for pair in range(half // 2):
            first = base + 2 * pair
            a = grams[first * states : (first + 1) * states]
            b = grams[(first + 1) * states : (first + 2) * states]
            diagonals = [
                jnp.sum(jnp.where(row_id == column_id, gram, 0.0), axis=0, keepdims=True)
                for gram in (a, b)
            ]
            square = jnp.where(row_id <= column_id, a, b)
            tail = jnp.concatenate(
                diagonals + [drives[first : first + 2], jnp.zeros((TAIL - 4, states), F32)], axis=0
            )
            if base == 0:
                keep_ref[pair, :states, :] = square
                keep_ref[pair, states:, :] = tail
            else:
                store_rounded(send_ref, pair, square, tail)


def prepare(
    prior_hbm,
    transition_hbm,
    basis_hbm,
    prior_out_ref,
    turned_ref,
    basis_out_ref,
    transition_ref,
    basis_ref,
    sems,
):
    copies = [
        pltpu.make_async_copy(prior_hbm, prior_out_ref, sems.at[0]),
        pltpu.make_async_copy(transition_hbm, transition_ref, sems.at[1]),
        pltpu.make_async_copy(basis_hbm, basis_ref, sems.at[2]),
    ]
    for copy in copies:
        copy.start()
    copies[0].wait()
    copies[1].wait()
    prior = prior_out_ref[...]
    turned_ref[...] = dot_wide(transition_ref[...].T, prior)
    copies[2].wait()
    basis_out_ref[...] = basis_ref[...].T


def add_and_round(keep_ref, received_ref, sum_ref, send_ref):
    states = keep_ref.shape[2]
    for pair in range(keep_ref.shape[0]):
        total = sum_of(keep_ref, received_ref, pair, states)
        sum_ref[pair] = total
        store_rounded(send_ref, pair, total[:states], total[states:])


def store_rounded(out_ref, pair, square, tail):
    states = square.shape[1]
    out_ref[pair, :states, :] = square.astype(BF16)
    high = tail.astype(BF16).astype(F32)
    out_ref[pair, states:, :] = jnp.concatenate([high, tail - high], axis=0).astype(BF16)


def add_received(sum_ref, received_ref, out_ref):
    states = sum_ref.shape[2]
    for pair in range(sum_ref.shape[0]):
        out_ref[pair] = sum_of(sum_ref, received_ref, pair, states)


def sum_of(sum_ref, received_ref, pair, states):
    received = received_ref[pair].astype(F32)
    tail = received[states : states + TAIL] + received[states + TAIL :]
    return sum_ref[pair] + jnp.concatenate([received[:states], tail], axis=0)


def times_own(z, coarse):
    states = z.shape[1]
    high, low = split(z)
    d_high, d_low = high[:states], low[:states]
    mixed = dot(d_high, d_low)
    square = dot(d_high, d_high) + (mixed + mixed.T)
    left, right = [high[states:], high[states:]], [d_high, d_low]
    if not coarse:
        left, right = left + [low[states:]], right + [d_high]
    rest = dot(jnp.concatenate(left, axis=1), jnp.concatenate(right, axis=0))
    return jnp.concatenate([square, rest], axis=0)


def hour_maps(
    sum_ref,
    received_ref,
    prior_ref,
    turned_ref,
    last_ref,
    firsts_ref,
    rounded_last_ref,
    rounded_firsts_ref,
):
    states = prior_ref.shape[0]
    prior = prior_ref[...]
    turned = turned_ref[...]
    row_id = lax.broadcasted_iota(jnp.int32, (states, states), 0)
    column_id = lax.broadcasted_iota(jnp.int32, (states, states), 1)
    running = []
    for pair in range(sum_ref.shape[0]):
        total = sum_of(sum_ref, received_ref, pair, states)
        square = total[:states]
        flipped = square.T
        upper, lower = row_id <= column_id, row_id > column_id
        grams = (jnp.where(upper, square, flipped), jnp.where(lower, square, flipped))
        for place, gram in enumerate(grams):
            diagonal, drive = [total[states + i : states + i + 1] for i in (place, place + 2)]
            gram = jnp.where(row_id == column_id, diagonal, gram)
            precision = prior + gram
            bound = jnp.max(jnp.sum(jnp.abs(precision), axis=0, keepdims=True), axis=1, keepdims=True)
            scale = 1.0 / bound
            offset = jnp.concatenate([drive, jnp.zeros((15, states), F32)], axis=0)
            running.append((precision * scale, turned * scale, offset * scale))
    stacked = [jnp.concatenate(parts, axis=0) for parts in running]

    for step in range(NS_ITERS - 2):
        stacked = [2.0 * z - times_own(z, step < 2) for z in stacked]
    maps = []
    for z in stacked:
        power = (jnp.where(row_id == column_id, 1.0, 0.0) - z[:states]).astype(BF16)
        v = z[states:]
        product = dot(jnp.concatenate([power, v.astype(BF16)], axis=0), power)
        v = v + product[states:]
        maps.append(v + dot(v.astype(BF16), product[:states].astype(BF16)))
    for position in range(len(maps)):
        joined = maps[0] if position == 0 else append(joined, maps[position])
        if position < len(maps) - 1:
            firsts_ref[position] = joined
            rounded_firsts_ref[position] = rounded(joined)
    last_ref[...] = joined
    rounded_last_ref[...] = rounded(joined)


def rounded(affine):
    states = affine.shape[1]
    return jnp.concatenate([affine[:states].astype(BF16), thirds(affine[states : states + 1])], axis=0)


def append(earlier, latter):
    states = latter.shape[1]
    product = dot_wide(earlier, latter[:states])
    return jnp.concatenate([product[:states], product[states:] + latter[states:]], axis=0)


def in_order(own_ref, received_ref):
    first = lax.rem(lax.axis_index("site"), 2) == 0
    count = len(own_ref) if isinstance(own_ref, list) else own_ref.shape[0]
    early = [jnp.where(first, own_ref[i], received_ref[i]) for i in range(count)]
    late = [jnp.where(first, received_ref[i], own_ref[i]) for i in range(count)]
    return early, late


def widened(block):
    states = block.shape[1]
    pad = jnp.zeros((15, states), F32)
    return jnp.concatenate([block[:states].astype(F32), shift_of(block), pad], axis=0)


def block_map(own_ref, received_ref, out_ref):
    (early,), (late,) = in_order([own_ref[...]], [received_ref[...]])
    out_ref[...] = rounded(append(early, late))


def pair_block(own_ref, last_ref, other_last_ref, next_ref, pair_ref):
    (early,), (late,) = in_order([last_ref[...]], [other_last_ref[...]])
    own, following = own_ref[...], follow(early, late)
    next_ref[...] = following
    odd = lax.rem(lax.axis_index("tm"), 2) == 1
    first, second = jnp.where(odd, following, own), jnp.where(odd, own, following)
    states = own.shape[1]
    pair_ref[:states, :] = dot(first[:states], second[:states])
    pair_ref[states:, :] = jnp.broadcast_to(apply(second, shift_of(first)), (8, states))


def group_blocks(own_ref, next_ref, pair_ref, far_ref, other_far_ref, out_ref, shift_ref):
    (near,), (far,) = in_order([far_ref[...]], [other_far_ref[...]])
    out_ref[0] = own_ref[...]
    out_ref[1] = next_ref[...]
    out_ref[2] = near
    out_ref[3] = far
    states = near.shape[1]
    place = lax.rem(lax.axis_index("tm"), out_ref.shape[0])
    odd, upper = lax.rem(place, 2) == 1, place >= 2
    first, second = jnp.where(odd, far, near), jnp.where(odd, near, far)
    pair = pair_ref[:states, :]
    pair_shift = pair_ref[states : states + 1, :]
    high, low = split(pair)
    mean = jnp.where(upper, shift_of(first), pair_shift)
    mean = apply(jnp.where(upper, second, first), mean)
    high = jnp.where(upper, high, second[:states])
    low = jnp.where(upper, low, jnp.zeros_like(low))
    mean = row_times(mean, high, low) + jnp.where(upper, pair_shift, shift_of(second))
    shift_ref[...] = jnp.broadcast_to(mean, shift_ref.shape)


def shift_of(block):
    states = block.shape[1]
    return jnp.sum(block[states:].astype(F32), axis=0, keepdims=True)


def choose(values, slot):
    value = values[0]
    for i in range(1, len(values)):
        value = jnp.where(slot == i, values[i], value)
    return value


def apply(block, mean):
    return row_times(mean, block[: block.shape[1]]) + shift_of(block)


def follow(earlier, latter):
    states = latter.shape[1]
    product = dot(earlier[:states], latter[:states]).astype(BF16)
    return jnp.concatenate([product, thirds(apply(latter, shift_of(earlier)))], axis=0)


def group_map(gathered_ref, out_ref):
    place = lax.rem(lax.axis_index("tm"), gathered_ref.shape[0])
    joined = gathered_ref[place]
    for i in range(1, gathered_ref.shape[0]):
        joined = follow(joined, gathered_ref[place ^ i])
    out_ref[...] = joined


def pair_map(distance, own_ref, received_ref, out_ref):
    upper = is_upper(distance)
    first = jnp.where(upper, received_ref[...], own_ref[...])
    second = jnp.where(upper, own_ref[...], received_ref[...])
    out_ref[...] = follow(first, second)


def is_upper(distance):
    return lax.rem(lax.axis_index("tm") // distance, 2) == 1


def hold(maps_ref, received_ref, out_ref):
    out_ref[...] = maps_ref[...]


def pair_means(distances, *refs):
    out_ref = refs[-1]
    own_last_ref, own_other_ref, own_firsts_ref, other_firsts_ref, last_ref, other_last_ref = refs[:6]
    levels, gathered_ref = refs[6:-2], refs[-2]
    rows, states = own_last_ref.shape
    half = own_firsts_ref.shape[0] + 1
    mean = jnp.zeros((1, states), F32)
    for level in reversed(range(len(distances))):
        if level == len(distances) - 1:
            entered = levels[level][0:1, :]
        else:
            entered = apply(levels[level][...], mean)
        mean = jnp.where(is_upper(distances[level]), entered, mean)
    place = lax.rem(lax.axis_index("tm"), gathered_ref.shape[0])
    for i in range(2):
        mean = jnp.where(place >= 2, apply(gathered_ref[place ^ i], mean), mean)
    odd = lax.rem(place, 2) == 1
    between = apply(gathered_ref[place & 1], mean)
    own_start = jnp.where(odd, between, mean)
    own = []
    sides = [
        [own_firsts_ref[i] for i in range(half - 1)] + [own_last_ref[...]],
        [widened(other_firsts_ref[i]) for i in range(half - 1)] + [own_other_ref[...]],
    ]
    for maps in in_order(*sides):
        start = own_start if not own else own[-1]
        for each in maps:
            own.append(row_times(start, *split(each[:states])) + each[states : states + 1])
    state = jnp.where(odd, mean, own[-1])
    partner = []
    for maps in in_order([last_ref[...]], [other_last_ref[...]]):
        partner += [state] * (half - 1)
        state = apply(maps[0], state)
        partner.append(state)
    own, partner = jnp.concatenate(own, axis=0), jnp.concatenate(partner, axis=0)
    out_ref[: 2 * half, :] = jnp.where(odd, partner, own)
    out_ref[2 * half :, :] = jnp.where(odd, own, partner)


def rest_of_means(means_ref, firsts_ref, other_ref, out_ref):
    count = firsts_ref.shape[0]
    hours = 2 * (count + 1)
    odd = lax.rem(lax.axis_index("tm"), 2) == 1
    out_ref[...] = means_ref[...]
    partner = jnp.where(odd, means_ref[:hours, :], means_ref[hours:, :])
    for side, maps in enumerate(in_order(firsts_ref, other_ref)):
        for i in range(count):
            hour = side * (count + 1) + i
            mean = apply(maps[i], partner[hour : hour + 1])
            out_ref[pl.ds(jnp.where(odd, hour, hours + hour), 1), :] = mean


def own_means(means_ref, out_ref):
    hours = out_ref.shape[1]
    odd = lax.rem(lax.axis_index("tm"), 2) == 1
    means = jnp.where(odd, means_ref[hours:, :], means_ref[:hours, :]).astype(BF16)
    for copy in range(out_ref.shape[0]):
        out_ref[copy] = means


def predict(*refs):
    means_refs, basis_ref, out_hbm, held_ref, sems = refs[:-4], *refs[-4:]
    if len(means_refs) > 1:
        place = lax.axis_index("tm") // 2
        own, near, far, other_far = [ref[...] for ref in means_refs]
        (third,), (fourth,) = in_order([far], [other_far])
        by_distance = [own, near, third, fourth]
        means = jnp.concatenate([choose(by_distance, place ^ i) for i in range(4)], axis=0)
        means = means.astype(BF16)
    else:
        means = means_refs[0][...]
    width = held_ref.shape[2]
    copies = []
    for chunk in range(CHUNKS):
        columns = pl.ds(chunk * width, width)
        held_ref[chunk] = dot(means, basis_ref[:, columns]).astype(BF16)
        copy = pltpu.make_async_copy(held_ref.at[chunk], out_hbm.at[:, columns], sems.at[chunk])
        copy.start()
        copies.append(copy)
    for copy in copies:
        copy.wait()


def core_swaps(blocks, hours, first, second):
    distances = [first, second] * (hours // 2)
    return [
        (t * hours + d, (t ^ distances[d]) * hours + d) for t in range(blocks) for d in range(hours)
    ]


def swaps(size, distance):
    return [(i, i ^ distance) for i in range(size)]


def body(obs_rows, obs_values, obs_hours, prior_precision, transition, site_basis):
    hours = lax.axis_size("site")
    blocks = lax.axis_size("tm")
    count, states = obs_rows.shape
    half = hours // 2
    pairs = half // 2
    sds = jax.ShapeDtypeStruct
    square = sds((states, states), F32)
    prior, turned, basis = call(
        prepare,
        (square, square, sds(site_basis.shape[::-1], BF16)),
        (prior_precision, transition, site_basis),
        "prepare",
        [
            pltpu.VMEM(transition.shape, F32),
            pltpu.VMEM(site_basis.shape, BF16),
            pltpu.SemaphoreType.DMA((3,)),
        ],
        in_hbm=True,
    )
    packed = sds((pairs, states + TAIL, states), F32)
    rounded = sds((pairs, states + 2 * TAIL, states), BF16)
    keep, send = call(
        functools.partial(local_grams, hours),
        (packed, rounded),
        (obs_rows, obs_values, obs_hours),
        "local_grams",
        [
            pltpu.VMEM(obs_rows.shape, BF16),
            pltpu.VMEM(obs_values.shape, BF16),
            pltpu.VMEM(obs_hours.shape, jnp.int32),
            pltpu.SemaphoreType.DMA((3,)),
        ],
        in_hbm=True,
    )
    received = lax.ppermute(send, "site", swaps(hours, 1))
    distance = 2
    while distance < hours:
        total, send = call(add_and_round, (packed, rounded), (keep, received), "add_and_round")
        received = lax.ppermute(send, "site", swaps(hours, distance))
        distance *= 2
        if distance < hours:
            keep = call(add_received, packed, (total, received), "add_received")
            received = jnp.zeros_like(received)
    rows = states + 16
    block = sds((rows, states), BF16)
    firsts = sds((half - 1, rows, states), BF16)
    own_last, own_firsts, last, own_rounded = call(
        hour_maps,
        (sds((rows, states), F32), sds((half - 1, rows, states), F32), block, firsts),
        (total, received, prior, turned),
        "hour_maps",
    )
    other_last = lax.ppermute(own_last, "site", swaps(hours, 1))
    last = lax.ppermute(last, "tm", swaps(blocks, 1))
    first_maps = lax.ppermute(own_rounded, "tm", swaps(blocks, 1))
    own = call(block_map, block, (own_last, other_last), "block_map")
    far = lax.ppermute(own, ("tm", "site"), core_swaps(blocks, hours, 2, 3))
    others_last = lax.ppermute(last, "site", swaps(hours, 1))
    others_far = lax.ppermute(far, "site", swaps(hours, 1))
    radix = 4
    following, pair = call(
        pair_block,
        (block, sds((states + 8, states), F32)),
        (own, last, others_last),
        "pair_block",
    )
    gathered, shift = call(
        group_blocks,
        (sds((radix, rows, states), BF16), sds((8, states), F32)),
        (own, following, pair, far, others_far),
        "group_blocks",
    )
    distances, levels = [], []
    distance = radix
    if 2 * distance < blocks:
        joined = call(group_map, sds(own.shape, BF16), (gathered,), "group_map")
    while distance < blocks:
        if 2 * distance == blocks:
            if levels:
                shift = joined[states:].astype(F32).sum(axis=0, keepdims=True)
                shift = jnp.broadcast_to(shift, (8, states))
            received = lax.ppermute(shift, "tm", swaps(blocks, distance))
        else:
            received = lax.ppermute(joined, "tm", swaps(blocks, distance))
            joined = call(
                functools.partial(pair_map, distance),
                sds(own.shape, BF16),
                (joined, received),
                "pair_map",
            )
        distances.append(distance)
        levels.append(received)
        distance *= 2
    other_firsts = lax.ppermute(own_rounded, "site", swaps(hours, 1))
    means = call(
        functools.partial(pair_means, tuple(distances)),
        sds((2 * hours, states), F32),
        [own_last, other_last, own_firsts, other_firsts, last, others_last]
        + levels
        + [gathered],
        "pair_means",
    )
    first_maps = call(hold, firsts, (first_maps, levels[-1]), "hold")
    other_firsts = lax.ppermute(first_maps, "site", swaps(hours, 1))
    means = call(
        rest_of_means,
        sds(means.shape, F32),
        (means, first_maps, other_firsts),
        "rest_of_means",
    )
    if blocks == 2 * radix:
        far = lax.ppermute(means, ("tm", "site"), core_swaps(blocks, hours, 4, 6))
        near = lax.ppermute(means, "tm", swaps(blocks, 2))
        other_far = lax.ppermute(far, "site", swaps(hours, 1))
        means = [means, near, far, other_far]
    else:
        means = call(own_means, sds((blocks, hours, states), BF16), (means,), "own_means")
        means = [lax.all_to_all(means, "tm", 0, 0, tiled=True).reshape(blocks * hours, states)]
    sites = site_basis.shape[0]
    return pl.pallas_call(
        predict,
        out_shape=sds((blocks * hours, sites), BF16),
        in_specs=[whole()] * (len(means) + 1),
        out_specs=pl.BlockSpec(memory_space=pltpu.HBM),
        scratch_shapes=[
            pltpu.VMEM((CHUNKS, blocks * hours, sites // CHUNKS), BF16),
            pltpu.SemaphoreType.DMA((CHUNKS,)),
        ],
        compiler_params=pltpu.CompilerParams(vmem_limit_bytes=VMEM_LIMIT),
        name="predict",
    )(*means, basis)


def solution(mesh):
    in_specs = (
        P(("tm", "site"), None),
        P(("tm", "site")),
        P(("tm", "site")),
        P(),
        P(),
        P(("tm", "site"), None),
    )
    out_specs = P(None, ("tm", "site"))
    return jax.shard_map(body, mesh=mesh, in_specs=in_specs, out_specs=out_specs, check_vma=False)
```
